32 devices in a mesh: grp: 2 (over x), seq: 16 (over z, y, core).
Axes of the slice: x: 2, y: 2, z: 4, core: 2. Of those that a mesh axis runs over, the one named last changes fastest.
Arguments:
- signal: bfloat16 [32768, 768], P(('grp', 'seq')), parts along dimension 0, may hold values from -6 to 6
- dilated_tap_weight: bfloat16 [4, 3, 768, 384], replicated, may hold values from -0.125 to 0.125
- point_weight: bfloat16 [4, 384, 768], replicated, may hold values from -0.3125 to 0.3125
Outputs:
- activations: bfloat16 [4, 32768, 768], P(None, ('grp', 'seq')), parts along dimension 1
The draws below stay inside these ranges and needn't reach their ends.
There are 2 independent parts, one for each index of `grp`. The reference program is written for one: setup_inputs(seed, part) draws one part's arguments, and reference() takes and returns one part's arrays. A program takes and returns all parts, laid end to end along the dimension named above; an argument that names none is the same for every part. Nothing has to cross between parts.
All inputs are finite; a program needn't handle non-finite values.
Results may differ from the reference program's by a relative error of at most 0.0075.
Values may be sent and summed in bfloat16 or wider, within the bound.
No kernel may reach another device: no remote copies, remote signals or barrier semaphores. Data moves between devices by JAX's collectives and lax.ppermute only.
A program may use at most 64 MiB of HBM per device.

```python
import jax
import jax.numpy as jnp
from jax import lax

C = 768
H = 384
FIRST_DILATION = 256
BLOCKS = 4
BINS = 16384


def block_scale(stream_key, dims, pieces, smallest, top_value):
    gain = 1.0
    for axis_at, shards_of in pieces:
        heights = jax.random.uniform(jax.random.fold_in(jax.random.fold_in(stream_key, 6), axis_at), (shards_of,), jnp.float32, smallest / len(pieces), top_value / len(pieces))
        gain = gain * jnp.repeat(jnp.exp(heights), dims[axis_at] // shards_of).reshape((-1,) + (1,) * (len(dims) - 1 - axis_at))
    return gain


def noise(rng, shape, width, bound, shards=(), held_as=jnp.bfloat16):
    loudness = block_scale(rng, shape, shards, -0.22, 0.18) if shards else 1.0
    entries = jax.random.normal(rng, shape, jnp.float32) * width * loudness
    return jnp.minimum(jnp.maximum(entries, -bound), bound).astype(held_as)


def setup_inputs(seed: int = 0, part: int = 0) -> dict:
    seeds = jax.random.split(jax.random.key(seed), 4)
    part_keys = jax.random.split(jax.random.fold_in(seeds[3], part), 4)
    return {
        "signal": noise(part_keys[0], (BINS, C), 1.0, 6.0, ((0, 16),)),
        "dilated_tap_weight": noise(seeds[1], (BLOCKS, 3, C, H), (3 * C) ** -0.5, 0.125),
        "point_weight": noise(seeds[2], (BLOCKS, H, C), H ** -0.5, 0.3125),
    }


def tap_term(rows, weight):
    product = jnp.dot(rows, weight, preferred_element_type=jnp.float32).astype(jnp.bfloat16)
    return lax.optimization_barrier(product).astype(jnp.float32)


def reference(signal, dilated_tap_weight, point_weight):
    current = signal
    outputs = []
    for block_layer_index in range(BLOCKS):
        dilation_step = FIRST_DILATION * 2 ** block_layer_index
        lower_neighbour_rows = jnp.pad(current, ((dilation_step, 0), (0, 0)))[:BINS]
        above_side = jnp.pad(current, ((0, dilation_step), (0, 0)))[dilation_step:]
        convolved = jnp.dot(current, dilated_tap_weight[block_layer_index, 1], preferred_element_type=jnp.float32)
        convolved = convolved + tap_term(lower_neighbour_rows, dilated_tap_weight[block_layer_index, 0])
        convolved = convolved + tap_term(above_side, dilated_tap_weight[block_layer_index, 2])
        hidden = jax.nn.gelu(convolved, approximate=True).astype(jnp.bfloat16)
        residual_branch = jnp.dot(hidden, point_weight[block_layer_index], preferred_element_type=jnp.float32)
        current = (current.astype(jnp.float32) + residual_branch).astype(jnp.bfloat16)
        outputs.append(current)
    return jnp.stack(outputs)
```

```python
import functools

import jax
import jax.numpy as jnp
from jax import lax
from jax.experimental import pallas as pl
from jax.experimental.pallas import tpu as pltpu
from jax.sharding import PartitionSpec as P

FIRST_DILATION = 256
GROUP = 4
CHUNKS = 1
ROWS = 256
VMEM_LIMIT = 40 * 2**20

F32, BF16 = jnp.float32, jnp.bfloat16
ANY = pl.BlockSpec(memory_space=pl.ANY)
VMEM = pl.BlockSpec(memory_space=pltpu.VMEM)
SMEM = pl.BlockSpec(memory_space=pltpu.SMEM)


def dot(a, b):
    return jnp.dot(a, b, preferred_element_type=F32)


def gelu(v):
    return 0.5 * v * (1.0 + jnp.tanh(0.7978845608028654 * (v + 0.044715 * (v * v * v))))


def over_rows(rows, body):
    whole = rows // ROWS

    def step(i, _):
        body(pl.multiple_of(i * ROWS, ROWS), ROWS)
        return 0

    if whole:
        lax.fori_loop(0, whole, step, 0)
    if rows % ROWS:
        body(whole * ROWS, rows % ROWS)


def start_all(copies):
    for copy in copies:
        copy.start()
    return copies


def wait_all(copies):
    for copy in copies:
        copy.wait()


def params():
    return pltpu.CompilerParams(vmem_limit_bytes=VMEM_LIMIT)


def cost(flops, bytes_accessed):
    return pl.CostEstimate(flops=int(flops), bytes_accessed=int(bytes_accessed), transcendentals=0)


def tap_copies(taps_hbm, block, taps, w_ref, sems, first):
    width = taps_hbm.shape[3]
    return [
        pltpu.make_async_copy(
            taps_hbm.at[block, tap], w_ref.at[:, pl.ds(i * width, width)], sems.at[first + i]
        )
        for i, tap in enumerate(taps)
    ]


def all_taps(x_ref, w_ref, low_ref, mid_ref, high_ref, rows, low_at=0):
    width = mid_ref.shape[1]

    def body(start, size):
        terms = dot(x_ref[pl.ds(start, size)], w_ref[...])
        low_ref[pl.ds(start + low_at, size)] = terms[:, :width].astype(BF16)
        mid_ref[pl.ds(start, size)] = terms[:, width : 2 * width]
        high_ref[pl.ds(start, size)] = terms[:, 2 * width :].astype(BF16)

    over_rows(rows, body)


def edges_kernel(halo, s_ref, own, r1, r2, r3, even_ref, odd_ref, sem):
    q, parity = s_ref[0], s_ref[1]
    rows = own.shape[0]

    def move(source, target):
        copy = pltpu.make_async_copy(source, target, sem)
        copy.start()
        copy.wait()

    for k, piece in enumerate((own, r1, r2, r3)):
        j = q ^ k
        top = piece.at[pl.ds(rows - halo, halo)]
        bottom = piece.at[pl.ds(0, halo)]
        for at, going_up, going_down in ((0, even_ref, odd_ref), (1, odd_ref, even_ref)):
            pl.when((j == GROUP - 1) & (parity == at))(functools.partial(move, top, going_up))
            pl.when((j == 0) & (parity == at))(functools.partial(move, bottom, going_down))


def edges(scalars, pieces, halo):
    shape = jax.ShapeDtypeStruct((halo, pieces[0].shape[1]), BF16)
    return pl.pallas_call(
        functools.partial(edges_kernel, halo),
        out_shape=(shape, shape),
        in_specs=[SMEM] + [ANY] * GROUP,
        out_specs=(ANY, ANY),
        scratch_shapes=[pltpu.SemaphoreType.DMA],
        compiler_params=params(),
        cost_estimate=cost(0, 4 * shape.size * 2),
    )(scalars, *pieces)


def first_kernel(
    r, s_ref, own, r1, r2, r3, from_even, from_odd, taps_hbm, point_hbm,
    x2_ref, even_ref, odd_ref, g0, g1, g2, g3,
    x0, x1, w0, w1, w2, p0, p1, low, mid, high, h0, h1, sems, wsems,
):
    q, parity, has_lower, has_upper = (s_ref[i] for i in range(4))
    rows = own.shape[0]
    halo = from_even.shape[0]
    length = GROUP * rows
    copies = []
    for k, piece in enumerate((own, r1, r2, r3)):
        at = pl.multiple_of(halo + (q ^ k) * rows, r)
        copies.append(pltpu.make_async_copy(piece, x0.at[pl.ds(at, rows)], sems.at[k]))
    even_at = pl.multiple_of(jnp.where(parity == 0, halo + length, 0), r)
    odd_at = pl.multiple_of(jnp.where(parity == 0, 0, halo + length), r)
    copies.append(pltpu.make_async_copy(from_even, x0.at[pl.ds(even_at, halo)], sems.at[4]))
    copies.append(pltpu.make_async_copy(from_odd, x0.at[pl.ds(odd_at, halo)], sems.at[5]))
    start_all(copies)
    c0 = start_all(tap_copies(taps_hbm, 0, (0, 1, 2), w0, wsems, 0))
    cp0 = pltpu.make_async_copy(point_hbm.at[0], p0, wsems.at[3])
    cp0.start()
    c1 = start_all(tap_copies(taps_hbm, 1, (0, 1, 2), w1, wsems, 4))
    cp1 = pltpu.make_async_copy(point_hbm.at[1], p1, wsems.at[7])
    cp1.start()
    c2 = start_all(tap_copies(taps_hbm, 2, (0, 2), w2, wsems, 8))
    wait_all(copies)

    @pl.when(has_lower == 0)
    def _():
        x0[pl.ds(0, halo)] = jnp.zeros((halo, x0.shape[1]), BF16)

    @pl.when(has_upper == 0)
    def _():
        x0[pl.ds(halo + length, halo)] = jnp.zeros((halo, x0.shape[1]), BF16)

    wait_all(c0)
    all_taps(x0, w0, low, mid, high, length + 2 * halo)
    cp0.wait()
    reach = halo - r

    def block0(start, size):
        v = mid[pl.ds(start + r, size)] + low[pl.ds(start, size)].astype(F32)
        v = v + high[pl.ds(start + 2 * r, size)].astype(F32)
        hidden = gelu(v).astype(BF16)
        h0[pl.ds(start, size)] = hidden
        x1[pl.ds(start, size)] = (
            x0[pl.ds(start + r, size)].astype(F32) + dot(hidden, p0[...])
        ).astype(BF16)

    over_rows(length + 2 * reach, block0)

    @pl.when(has_lower == 0)
    def _():
        x1[pl.ds(0, reach)] = jnp.zeros((reach, x1.shape[1]), BF16)

    @pl.when(has_upper == 0)
    def _():
        x1[pl.ds(reach + length, reach)] = jnp.zeros((reach, x1.shape[1]), BF16)

    wait_all(c1)
    all_taps(x1, w1, low, mid, high, length + 2 * reach)
    cp1.wait()

    def block1(start, size):
        v = mid[pl.ds(start + reach, size)] + low[pl.ds(start, size)].astype(F32)
        v = v + high[pl.ds(start + 2 * reach, size)].astype(F32)
        hidden = gelu(v).astype(BF16)
        h1[pl.ds(start, size)] = hidden
        x2_ref[pl.ds(start, size)] = (
            x1[pl.ds(start + reach, size)].astype(F32) + dot(hidden, p1[...])
        ).astype(BF16)

    over_rows(length, block1)

    wait_all(c2)
    width = even_ref.shape[1]
    send = even_ref.shape[0]
    up = dot(x2_ref[pl.ds(length - send, send)], w2[:, :width])
    down = dot(x2_ref[pl.ds(0, send)], w2[:, width:])
    even_ref[...] = jnp.where(parity == 0, up, down).astype(BF16)
    odd_ref[...] = jnp.where(parity == 0, down, up).astype(BF16)
    for k, piece in enumerate((g0, g1, g2, g3)):
        at = pl.multiple_of((q ^ k) * rows, r)
        piece[0] = h0[pl.ds(reach + at, rows)]
        piece[1] = h1[pl.ds(at, rows)]


def first_blocks(scalars, pieces, from_even, from_odd, taps, point, r):
    rows, c = pieces[0].shape
    h = taps.shape[3]
    halo = from_even.shape[0]
    length = GROUP * rows
    wide = length + 2 * halo
    terms = jax.ShapeDtypeStruct((4 * r, h), BF16)
    piece = jax.ShapeDtypeStruct((2, rows, h), BF16)
    return pl.pallas_call(
        functools.partial(first_kernel, r),
        out_shape=(jax.ShapeDtypeStruct((length, c), BF16), terms, terms) + (piece,) * GROUP,
        in_specs=[SMEM] + [ANY] * (GROUP + 4),
        out_specs=(VMEM,) * (3 + GROUP),
        scratch_shapes=[
            pltpu.VMEM((wide, c), BF16),
            pltpu.VMEM((wide - 2 * r, c), BF16),
            pltpu.VMEM((c, 3 * h), BF16),
            pltpu.VMEM((c, 3 * h), BF16),
            pltpu.VMEM((c, 2 * h), BF16),
            pltpu.VMEM((h, c), BF16),
            pltpu.VMEM((h, c), BF16),
            pltpu.VMEM((wide, h), BF16),
            pltpu.VMEM((wide, h), F32),
            pltpu.VMEM((wide, h), BF16),
            pltpu.VMEM((wide - 2 * r, h), BF16),
            pltpu.VMEM((length, h), BF16),
            pltpu.SemaphoreType.DMA((6,)),
            pltpu.SemaphoreType.DMA((10,)),
        ],
        compiler_params=params(),
        cost_estimate=cost(2 * c * h * (3 * wide + 4 * wide + 2 * length), 10 * 2**20),
    )(scalars, *pieces, from_even, from_odd, taps, point)


def third_kernel(
    r, s_ref, x2, from_even, from_odd, taps_hbm, point_hbm,
    x3_ref, even_ref, odd_ref, g0, g1, g2, g3,
    w2, w3, p2, low, mid, high, h2, wsems,
):
    q, parity, has_lower, has_upper = (s_ref[i] for i in range(4))
    length, rows = x2.shape[0], x2.shape[0] // GROUP
    d = from_even.shape[0]
    width = from_even.shape[1]
    c2 = start_all(tap_copies(taps_hbm, 2, (0, 1, 2), w2, wsems, 0))
    cp2 = pltpu.make_async_copy(point_hbm.at[2], p2, wsems.at[3])
    cp2.start()
    c3 = start_all(tap_copies(taps_hbm, 3, (0, 2), w3, wsems, 4))
    even = from_even[...].astype(F32)
    odd = from_odd[...].astype(F32)
    below = jnp.where(parity == 0, odd, even)
    above = jnp.where(parity == 0, even, odd)
    low[pl.ds(0, d)] = jnp.where(has_lower == 0, 0.0, below).astype(BF16)
    high[pl.ds(length, d)] = jnp.where(has_upper == 0, 0.0, above).astype(BF16)
    wait_all(c2)
    all_taps(x2, w2, low, mid, high, length, low_at=d)
    cp2.wait()

    def block2(start, size):
        v = mid[pl.ds(start, size)] + low[pl.ds(start, size)].astype(F32)
        v = v + high[pl.ds(start + d, size)].astype(F32)
        hidden = gelu(v).astype(BF16)
        h2[pl.ds(start, size)] = hidden
        x3_ref[pl.ds(start, size)] = (
            x2[pl.ds(start, size)].astype(F32) + dot(hidden, p2[...])
        ).astype(BF16)

    over_rows(length, block2)
    wait_all(c3)
    send = even_ref.shape[0]

    def terms(start, size):
        up = dot(x3_ref[pl.ds(length - send + start, size)], w3[:, :width])
        down = dot(x3_ref[pl.ds(start, size)], w3[:, width:])
        even_ref[pl.ds(start, size)] = jnp.where(parity == 0, up, down).astype(BF16)
        odd_ref[pl.ds(start, size)] = jnp.where(parity == 0, down, up).astype(BF16)

    over_rows(send, terms)
    for k, piece in enumerate((g0, g1, g2, g3)):
        piece[...] = h2[pl.ds(pl.multiple_of((q ^ k) * rows, r), rows)]


def third_block(scalars, x2, from_even, from_odd, taps, point, r):
    length, c = x2.shape
    rows = length // GROUP
    h = taps.shape[3]
    d = from_even.shape[0]
    terms = jax.ShapeDtypeStruct((2 * d, h), BF16)
    piece = jax.ShapeDtypeStruct((rows, h), BF16)
    return pl.pallas_call(
        functools.partial(third_kernel, r),
        out_shape=(jax.ShapeDtypeStruct((length, c), BF16), terms, terms) + (piece,) * GROUP,
        in_specs=[SMEM] + [VMEM] * 3 + [ANY] * 2,
        out_specs=(VMEM,) * (3 + GROUP),
        scratch_shapes=[
            pltpu.VMEM((c, 3 * h), BF16),
            pltpu.VMEM((c, 2 * h), BF16),
            pltpu.VMEM((h, c), BF16),
            pltpu.VMEM((length + d, h), BF16),
            pltpu.VMEM((length, h), F32),
            pltpu.VMEM((length + d, h), BF16),
            pltpu.VMEM((length, h), BF16),
            pltpu.SemaphoreType.DMA((6,)),
        ],
        compiler_params=params(),
        cost_estimate=cost(2 * c * h * 5 * length, 8 * 2**20),
    )(scalars, x2, from_even, from_odd, taps, point)


def near_kernel(x3, taps_hbm, near_ref, w, other, wsems):
    length = x3.shape[0]
    half = length // 2
    width = near_ref.shape[1]
    copies = start_all(tap_copies(taps_hbm, 3, (0, 1, 2), w, wsems, 0))
    wait_all(copies)

    def lower_half(start, size):
        terms = dot(x3[pl.ds(start, size)], w[:, : 2 * width])
        other[pl.ds(start, size)] = terms[:, :width].astype(BF16)
        near_ref[pl.ds(start, size)] = terms[:, width:]

    def upper_half(start, size):
        terms = dot(x3[pl.ds(half + start, size)], w[:, width:])
        near_ref[pl.ds(half + start, size)] = (
            terms[:, :width] + other[pl.ds(start, size)].astype(F32)
        )
        near_ref[pl.ds(start, size)] = near_ref[pl.ds(start, size)] + terms[:, width:].astype(
            BF16
        ).astype(F32)

    over_rows(half, lower_half)
    over_rows(half, upper_half)


def near_terms(x3, taps):
    length, c = x3.shape
    h = taps.shape[3]
    return pl.pallas_call(
        near_kernel,
        out_shape=jax.ShapeDtypeStruct((length, h), F32),
        in_specs=[VMEM, ANY],
        out_specs=VMEM,
        scratch_shapes=[
            pltpu.VMEM((c, 3 * h), BF16),
            pltpu.VMEM((length // 2, h), BF16),
            pltpu.SemaphoreType.DMA((3,)),
        ],
        compiler_params=params(),
        cost_estimate=cost(2 * c * h * 2 * length, 5 * 2**20),
    )(x3, taps)


def last_kernel(r, s_ref, near, from_even, from_odd, g0, g1, g2, g3, h3):
    q, parity, has_lower, has_upper = (s_ref[i] for i in range(4))
    length, rows = near.shape[0], near.shape[0] // GROUP
    half = length // 2

    def body(start, size):
        even = from_even[pl.ds(start, size)].astype(F32)
        odd = from_odd[pl.ds(start, size)].astype(F32)
        below = jnp.where(has_lower == 0, 0.0, jnp.where(parity == 0, odd, even))
        above = jnp.where(has_upper == 0, 0.0, jnp.where(parity == 0, even, odd))
        h3[pl.ds(start, size)] = gelu(near[pl.ds(start, size)] + below).astype(BF16)
        h3[pl.ds(half + start, size)] = gelu(near[pl.ds(half + start, size)] + above).astype(BF16)

    over_rows(half, body)
    for k, piece in enumerate((g0, g1, g2, g3)):
        piece[...] = h3[pl.ds(pl.multiple_of((q ^ k) * rows, r), rows)]


def last_hidden(scalars, near, from_even, from_odd, r):
    length, h = near.shape
    piece = jax.ShapeDtypeStruct((length // GROUP, h), BF16)
    return pl.pallas_call(
        functools.partial(last_kernel, r),
        out_shape=(piece,) * GROUP,
        in_specs=[SMEM] + [VMEM] * 3,
        out_specs=(VMEM,) * GROUP,
        scratch_shapes=[pltpu.VMEM((length, h), BF16)],
        compiler_params=params(),
        cost_estimate=cost(20 * length * h, 5 * 2**20),
    )(scalars, near, from_even, from_odd)


def early_out_kernel(ch, s_ref, x_hbm, a0, a1, a2, a3, b0, b1, b2, b3, point, out, xs, ys, sems, osems):
    q = s_ref[0]
    places, r, c = xs.shape[1], xs.shape[2], xs.shape[3]
    reads = start_all(
        [
            pltpu.make_async_copy(x_hbm.at[:, q ^ k, ch], xs.at[k], sems.at[k])
            for k in range(GROUP)
        ]
    )
    writes = []
    for k, (first, second) in enumerate(((a0, b0), (a1, b1), (a2, b2), (a3, b3))):
        reads[k].wait()
        x = xs[k].reshape(places * r, c)
        for b, hidden in enumerate((first[0], first[1], second[...])):
            x = (x.astype(F32) + dot(hidden, point[b])).astype(BF16)
            ys[b, k] = x.reshape(places, r, c)
            writes.append(
                pltpu.make_async_copy(ys.at[b, k], out.at[b, :, q ^ k, ch], osems.at[b, k])
            )
            writes[-1].start()
    wait_all(writes)


def late_out_kernel(ch, s_ref, a0, a1, a2, a3, point, before, out, xs, ys, sems, osems):
    q = s_ref[0]
    places, r, c = xs.shape[1], xs.shape[2], xs.shape[3]
    last = out.shape[0] - 1
    reads = start_all(
        [
            pltpu.make_async_copy(out.at[last - 1, :, q ^ k, ch], xs.at[k], sems.at[k])
            for k in range(GROUP)
        ]
    )
    writes = []
    for k, hidden in enumerate((a0, a1, a2, a3)):
        reads[k].wait()
        x = xs[k].reshape(places * r, c)
        x = (x.astype(F32) + dot(hidden[...], point[0])).astype(BF16)
        ys[k] = x.reshape(places, r, c)
        writes.append(pltpu.make_async_copy(ys.at[k], out.at[last, :, q ^ k, ch], osems.at[k]))
        writes[-1].start()
    wait_all(writes)


def early_outputs(ch, scalars, x, firsts, thirds, point, before):
    places, group, chunks, r, c = x.shape
    blocks = point.shape[0]
    shape = jax.ShapeDtypeStruct((blocks, places, group, chunks, r, c), BF16)
    operands = [scalars, x, *firsts, *thirds, point[: blocks - 1]]
    specs = [SMEM, ANY] + [VMEM] * (2 * GROUP + 1)
    kernel = functools.partial(early_out_kernel, ch)
    aliases = {}
    if before is not None:
        aliases = {len(operands): 0}
        operands.append(before)
        specs.append(ANY)
        kernel = lambda *refs: early_out_kernel(ch, *refs[: len(operands) - 1], *refs[len(operands) :])
    return pl.pallas_call(
        kernel,
        out_shape=shape,
        in_specs=specs,
        out_specs=ANY,
        scratch_shapes=[
            pltpu.VMEM((GROUP, places, r, c), BF16),
            pltpu.VMEM((blocks - 1, GROUP, places, r, c), BF16),
            pltpu.SemaphoreType.DMA((GROUP,)),
            pltpu.SemaphoreType.DMA((blocks - 1, GROUP)),
        ],
        input_output_aliases=aliases,
        compiler_params=params(),
        cost_estimate=cost(2 * 3 * GROUP * places * r * c * point.shape[1], 10 * 2**20),
    )(*operands)


def late_outputs(ch, scalars, hiddens, point, before):
    blocks, places, group, chunks, r, c = before.shape
    operands = [scalars, *hiddens, point[blocks - 1 :], before]
    return pl.pallas_call(
        functools.partial(late_out_kernel, ch),
        out_shape=jax.ShapeDtypeStruct(before.shape, BF16),
        in_specs=[SMEM] + [VMEM] * (GROUP + 1) + [ANY],
        out_specs=ANY,
        scratch_shapes=[
            pltpu.VMEM((GROUP, places, r, c), BF16),
            pltpu.VMEM((GROUP, places, r, c), BF16),
            pltpu.SemaphoreType.DMA((GROUP,)),
            pltpu.SemaphoreType.DMA((GROUP,)),
        ],
        input_output_aliases={len(operands) - 1: 0},
        compiler_params=params(),
        cost_estimate=cost(2 * GROUP * places * r * c * point.shape[1], 4 * 2**20),
    )(*operands)


def neighbour_pairs(size, parity):
    groups = size // GROUP
    pairs = []
    for i in range(size):
        group = i // GROUP
        other = group + 1 if group % 2 == parity else group - 1
        pairs.append((i, i + (other - group) * GROUP if 0 <= other < groups else i ^ 1))
    return pairs


def by_residue(signal, taps, point):
    size = lax.axis_size("seq")
    me = lax.axis_index("seq")
    length, c = signal.shape
    places = length // FIRST_DILATION
    r = FIRST_DILATION // GROUP // CHUNKS
    q, group = me % GROUP, me // GROUP
    scalars = jnp.stack(
        [q, group % 2, (group > 0).astype(jnp.int32), (group < size // GROUP - 1).astype(jnp.int32)]
    ).astype(jnp.int32)
    even_pairs, odd_pairs = neighbour_pairs(size, 0), neighbour_pairs(size, 1)
    x = signal.reshape(places, GROUP, CHUNKS, r, c)

    def swap(value, k):
        return lax.ppermute(value, "seq", [(i, i ^ k) for i in range(size)])

    def back(pieces):
        return [pieces[0]] + [swap(pieces[k], k) for k in range(1, GROUP)]

    def across(even, odd):
        return lax.ppermute(even, "seq", even_pairs), lax.ppermute(odd, "seq", odd_pairs)

    out = None
    firsts, thirds, lasts = [], [], []
    for ch in range(CHUNKS):
        pieces = [
            lax.dynamic_index_in_dim(x[:, :, ch], q ^ k, 1, keepdims=False).reshape(places * r, c)
            for k in range(GROUP)
        ]
        pieces = back(pieces)
        halos = across(*edges(scalars, pieces, 3 * r))
        x2, even, odd, *hidden = first_blocks(scalars, pieces, *halos, taps, point, r)
        terms = across(even, odd)
        firsts.append(back(hidden))
        x3, even, odd, *hidden = third_block(scalars, x2, *terms, taps, point, r)
        terms = across(even, odd)
        near = near_terms(x3, taps)
        thirds.append(back(hidden))
        hidden = last_hidden(scalars, near, *terms, r)
        lasts.append(back(hidden))
    for ch in range(CHUNKS):
        out = early_outputs(ch, scalars, x, firsts[ch], thirds[ch], point, out)
    for ch in range(CHUNKS):
        out = late_outputs(ch, scalars, lasts[ch], point, out)
    return out.reshape(point.shape[0], length, c)


def passed_along(value, by):
    size = lax.axis_size("seq")
    pairs = [(i, i + by) for i in range(size) if 0 <= i + by < size]
    return lax.ppermute(value, "seq", pairs)


def by_neighbours(signal, taps, point):
    length = signal.shape[0]
    current = signal
    outputs = []
    for block in range(taps.shape[0]):
        step = FIRST_DILATION * 2**block
        low = dot(current, taps[block, 0]).astype(BF16)
        high = dot(current, taps[block, 2]).astype(BF16)
        if step < length:
            below = jnp.concatenate([passed_along(low[length - step :], 1), low[: length - step]])
            above = jnp.concatenate([high[step:], passed_along(high[:step], -1)])
        else:
            below = passed_along(low, step // length)
            above = passed_along(high, -(step // length))
        v = dot(current, taps[block, 1]) + below.astype(F32) + above.astype(F32)
        hidden = jax.nn.gelu(v, approximate=True).astype(BF16)
        current = (current.astype(F32) + dot(hidden, point[block])).astype(BF16)
        outputs.append(current)
    return jnp.stack(outputs)


def shards(signal, taps, point):
    fits = (
        taps.shape[0] == 4
        and signal.shape[0] == GROUP * FIRST_DILATION
        and lax.axis_size("seq") % GROUP == 0
    )
    return (by_residue if fits else by_neighbours)(signal, taps, point)


def solution(mesh):
    in_specs = (P(("grp", "seq"), None), P(), P())
    out_specs = P(None, ("grp", "seq"), None)
    return jax.shard_map(shards, mesh=mesh, in_specs=in_specs, out_specs=out_specs, check_vma=False)
```

```python
import functools

import jax
import jax.numpy as jnp
from jax import lax
from jax.experimental import pallas as pl
from jax.experimental.pallas import tpu as pltpu
from jax.sharding import PartitionSpec as P

FIRST_DILATION = 256
GROUP = 4
CHUNKS = 2
ROWS = 512
VMEM_LIMIT = 24 * 2**20

F32, BF16 = jnp.float32, jnp.bfloat16
ANY = pl.BlockSpec(memory_space=pl.ANY)
VMEM = pl.BlockSpec(memory_space=pltpu.VMEM)
SMEM = pl.BlockSpec(memory_space=pltpu.SMEM)
HBM = pl.BlockSpec(memory_space=pltpu.HBM)


def dot(a, b):
    return jnp.dot(a, b, preferred_element_type=F32)


def gelu(v):
    half = 0.5 * v
    inner = v * (0.7978845608028654 + 0.035677408136300125 * (v * v))
    return half + half * jnp.tanh(inner)


def over_rows(rows, body):
    for start in range(0, rows, ROWS):
        body(start, min(ROWS, rows - start))


def start_all(copies):
    for copy in copies:
        copy.start()
    return copies


def wait_all(copies):
    for copy in copies:
        copy.wait()


def call(kernel, outs, operands, specs, out_specs, scratch, flops, moved, aliases=None, after=()):
    count = len(operands)
    operands, specs = [*operands, *after], [*specs, *[ANY] * len(after)]
    body = kernel
    if after:
        kernel = lambda *refs: body(*refs[:count], *refs[count + len(after) :])
    return pl.pallas_call(
        kernel,
        out_shape=outs,
        in_specs=specs,
        out_specs=out_specs,
        scratch_shapes=scratch,
        input_output_aliases=aliases or {},
        compiler_params=pltpu.CompilerParams(vmem_limit_bytes=VMEM_LIMIT),
        cost_estimate=pl.CostEstimate(
            flops=int(flops), bytes_accessed=int(moved), transcendentals=0
        ),
    )(*operands)


def array(*shape, dtype=BF16):
    return jax.ShapeDtypeStruct(shape, dtype)


def split_kernel(s_ref, x, g0, g1, g2, g3, sems):
    q = s_ref[0]
    copies = [
        pltpu.make_async_copy(x.at[:, q ^ k, ch], piece.at[ch], sems.at[k, ch])
        for k, piece in enumerate((g0, g1, g2, g3))
        for ch in range(x.shape[2])
    ]
    wait_all(start_all(copies))


def split(scalars, x):
    places, group, chunks, r, c = x.shape
    pieces = (array(chunks, places, r, c),) * group
    sems = [pltpu.SemaphoreType.DMA((group, chunks))]
    pieces = call(split_kernel, pieces, (scalars, x), [SMEM, HBM], (VMEM,) * group, sems, 0, 4 * x.size)
    return [piece.reshape(chunks * places * r, c) for piece in pieces]


def side_by_side_kernel(taps, w, sems):
    h = taps.shape[3]
    wait_all(
        start_all(
            [
                pltpu.make_async_copy(
                    taps.at[b, t], w.at[b, :, pl.ds(t * h, h)], sems.at[b, t]
                )
                for b in range(taps.shape[0])
                for t in range(3)
            ]
        )
    )


def side_by_side(taps):
    blocks, count, c, h = taps.shape
    sems = [pltpu.SemaphoreType.DMA((blocks, count))]
    return call(side_by_side_kernel, array(blocks, c, count * h), (taps,), [HBM], VMEM, sems, 0, 4 * taps.size)


def place_terms(parity, up, down, even_ref, odd_ref, start, size):
    even_ref[pl.ds(start, size)] = jnp.where(parity == 0, up, down).astype(BF16)
    odd_ref[pl.ds(start, size)] = jnp.where(parity == 0, down, up).astype(BF16)


def arrived(s_ref, from_even, from_odd, start, size):
    even = from_even[pl.ds(start, size)].astype(F32)
    odd = from_odd[pl.ds(start, size)].astype(F32)
    parity, has_lower, has_upper = s_ref[1], s_ref[2], s_ref[3]
    below = jnp.where(has_lower == 0, 0.0, jnp.where(parity == 0, odd, even))
    above = jnp.where(has_upper == 0, 0.0, jnp.where(parity == 0, even, odd))
    return below, above


def open_kernel(r, s_ref, own, r1, r2, r3, w, even_ref, odd_ref, ends):
    q, parity = s_ref[0], s_ref[1]
    part = own.shape[0] // CHUNKS
    h = even_ref.shape[1]

    def fetch(piece, at, to):
        for ch in range(CHUNKS):
            ends[pl.ds(to + ch * r, r)] = piece[pl.ds(ch * part + at, r)]

    for k, piece in enumerate((own, r1, r2, r3)):
        pl.when(q ^ k == GROUP - 1)(functools.partial(fetch, piece, part - r, 0))
        pl.when(q ^ k == 0)(functools.partial(fetch, piece, 0, CHUNKS * r))
    size = CHUNKS * r
    up = dot(ends[pl.ds(0, size)], w[0, :, :h])
    down = dot(ends[pl.ds(size, size)], w[0, :, 2 * h :])
    place_terms(parity, up, down, even_ref, odd_ref, 0, size)


def open_terms(scalars, pieces, w, r):
    c, h = w.shape[1], w.shape[2] // 3
    terms = array(CHUNKS * r, h)
    return call(
        functools.partial(open_kernel, r), (terms, terms), (scalars, *pieces, w),
        [SMEM] + [VMEM] * (GROUP + 1), (VMEM, VMEM), [pltpu.VMEM((2 * CHUNKS * r, c), BF16)],
        4 * CHUNKS * r * c * h, 2**20,
    )


def all_taps(x, w, low, mid, high):
    h = mid.shape[1]

    def body(start, size):
        terms = dot(x[pl.ds(start, size)], w)
        low[pl.ds(start, size)] = terms[:, :h].astype(BF16)
        mid[pl.ds(start, size)] = terms[:, h : 2 * h]
        high[pl.ds(start, size)] = terms[:, 2 * h :].astype(BF16)

    over_rows(x.shape[0], body)


def block_body(reach, x, point, x_ref, h_ref, part_ref, low, mid, high):
    length = x.shape[0] // CHUNKS
    for ch in range(CHUNKS):
        base = ch * length
        edge = 2 * ch * reach
        top = base + length - reach

        def body(start, size, base=base + reach):
            at = base + start
            v = mid[pl.ds(at, size)] + low[pl.ds(at - reach, size)].astype(F32)
            hidden = gelu(v + high[pl.ds(at + reach, size)].astype(F32)).astype(BF16)
            h_ref[pl.ds(at, size)] = hidden
            x_ref[pl.ds(at, size)] = (x[pl.ds(at, size)].astype(F32) + dot(hidden, point)).astype(BF16)

        over_rows(length - 2 * reach, body)
        part_ref[pl.ds(edge, reach)] = mid[pl.ds(base, reach)] + high[
            pl.ds(base + reach, reach)
        ].astype(F32)
        part_ref[pl.ds(edge + reach, reach)] = mid[pl.ds(top, reach)] + low[
            pl.ds(top - reach, reach)
        ].astype(F32)
        for at in (base, top):
            x_ref[pl.ds(at, reach)] = x[pl.ds(at, reach)]
            h_ref[pl.ds(at, reach)] = jnp.zeros((reach, h_ref.shape[1]), BF16)


def first_kernel(reach, s_ref, own, r1, r2, r3, w, point, x_ref, h_ref, part_ref, x, low, mid, high):
    q = s_ref[0]
    part = own.shape[0] // CHUNKS
    h = mid.shape[1]
    for k, piece in enumerate((own, r1, r2, r3)):
        terms = dot(piece[...], w[0])
        for ch in range(CHUNKS):
            here = slice(ch * part, (ch + 1) * part)
            there = pl.ds(pl.multiple_of((ch * GROUP + (q ^ k)) * part, part), part)
            x[there] = piece[here]
            low[there] = terms[here, :h].astype(BF16)
            mid[there] = terms[here, h : 2 * h]
            high[there] = terms[here, 2 * h :].astype(BF16)
    block_body(reach, x, point[0], x_ref, h_ref, part_ref, low, mid, high)


def middle_kernel(block, reach, x, w, point, x_ref, h_ref, part_ref, low, mid, high):
    all_taps(x, w[block], low, mid, high)
    block_body(reach, x, point[block], x_ref, h_ref, part_ref, low, mid, high)


def local_block(block, scalars, x, w, point, reach):
    c, h = w.shape[1], w.shape[2] // 3
    length = GROUP * x[0].shape[0] if block == 0 else x.shape[0]
    outs = (array(length, c), array(length, h), array(2 * CHUNKS * reach, h, dtype=F32))
    scratch = [
        pltpu.VMEM((length, h), BF16),
        pltpu.VMEM((length, h), F32),
        pltpu.VMEM((length, h), BF16),
    ]
    if block == 0:
        kernel = functools.partial(first_kernel, reach)
        operands, specs = (scalars, *x, w, point), [SMEM] + [VMEM] * (GROUP + 2)
        scratch = [pltpu.VMEM((length, c), BF16)] + scratch
    else:
        kernel = functools.partial(middle_kernel, block, reach)
        operands, specs = (x, w, point), [VMEM] * 3
    return call(kernel, outs, operands, specs, (VMEM,) * 3, scratch, 8 * length * c * h, 4 * 2**20)


def give_back(q, reach, hidden, edges, near_refs, far_ref):
    length = hidden.shape[0] // CHUNKS
    rows = length // GROUP
    size = CHUNKS * rows
    for k in range(GROUP):
        ref, to = (near_refs[k], 0) if k < 2 else (far_ref, (k - 2) * size)
        j = q ^ k
        for ch in range(CHUNKS):
            at = pl.multiple_of(ch * length + j * rows, rows)
            ref[pl.ds(to + ch * rows, rows)] = hidden[pl.ds(at, rows)]

        @pl.when(j == 0)
        def _(ref=ref, to=to):
            for ch in range(CHUNKS):
                ref[pl.ds(to + ch * rows, reach)] = edges[2 * ch]

        @pl.when(j == GROUP - 1)
        def _(ref=ref, to=to):
            for ch in range(CHUNKS):
                ref[pl.ds(to + (ch + 1) * rows - reach, reach)] = edges[2 * ch + 1]


def edge_kernel(
    block, reach, ahead, s_ref, x, hidden, part, from_even, from_odd, w, point, x_ref, *refs
):
    q, parity = s_ref[0], s_ref[1]
    length = x.shape[0] // CHUNKS
    h = hidden.shape[1]
    edges = []
    for ch in range(CHUNKS):
        below, above = arrived(s_ref, from_even, from_odd, ch * reach, reach)
        edge = 2 * ch * reach
        edges.append(gelu(part[pl.ds(edge, reach)] + below).astype(BF16))
        edges.append(gelu(part[pl.ds(edge + reach, reach)] + above).astype(BF16))
    more = dot(jnp.concatenate(edges), point[block])
    for i in range(2 * CHUNKS):
        at = (i // 2) * length + (i % 2) * (length - reach)
        new = x[pl.ds(at, reach)].astype(F32) + more[i * reach : (i + 1) * reach]
        x_ref[pl.ds(at, reach)] = new.astype(BF16)
    last = block + 2 == w.shape[0]
    for ch in range(CHUNKS):
        even_ref, odd_ref = refs[2 * ch : 2 * ch + 2] if last else refs[:2]
        up = dot(x_ref[pl.ds((ch + 1) * length - ahead, ahead)], w[block + 1, :, :h])
        down = dot(x_ref[pl.ds(ch * length, ahead)], w[block + 1, :, 2 * h :])
        place_terms(parity, up, down, even_ref, odd_ref, 0 if last else ch * ahead, ahead)
    if last:
        for i in range(2 * CHUNKS):
            refs[-1][pl.ds(i * reach, reach)] = edges[i]
    else:
        give_back(q, reach, hidden, edges, refs[2:4], refs[4])


def finish_edges(block, scalars, x, hidden, part, terms, w, point, reach, ahead):
    c, h = w.shape[1], w.shape[2] // 3
    rows = x.shape[0] // GROUP
    outs = (array(*x.shape),)
    if block + 2 == w.shape[0]:
        outs += (array(ahead, h),) * (2 * CHUNKS) + (array(2 * CHUNKS * reach, h),)
    else:
        outs += (array(CHUNKS * ahead, h),) * 2
        outs += (array(rows, h), array(rows, h), array(2 * rows, h))
    return call(
        functools.partial(edge_kernel, block, reach, ahead), outs,
        (scalars, x, hidden, part, *terms, w, point),
        [SMEM] + [VMEM] * 7, (VMEM,) * len(outs), [],
        2 * c * h * CHUNKS * (2 * reach + 2 * ahead), 4 * 2**20, {1: 0},
    )


def near_kernel(reach, s_ref, x, hidden, ends, w, near_ref, own_ref, core_ref, far_ref, other):
    length = x.shape[0] // CHUNKS
    half = length // 2
    h = near_ref.shape[1]
    block = w.shape[0] - 1
    for ch in range(CHUNKS):
        lower, upper = pl.ds(ch * length, half), pl.ds(ch * length + half, half)
        terms = dot(x[lower], w[block, :, : 2 * h])
        near_ref[lower] = terms[:, h:]
        other[...] = terms[:, :h].astype(BF16)
        terms = dot(x[upper], w[block, :, h:])
        near_ref[upper] = terms[:, :h] + other[...].astype(F32)
        near_ref[lower] = near_ref[lower] + terms[:, h:].astype(BF16).astype(F32)
    edges = [ends[pl.ds(i * reach, reach)] for i in range(2 * CHUNKS)]
    give_back(s_ref[0], reach, hidden, edges, (own_ref, core_ref), far_ref)


def near_terms(scalars, x, hidden, ends, w, reach):
    c, h = w.shape[1], w.shape[2] // 3
    rows = x.shape[0] // GROUP
    scratch = [pltpu.VMEM((x.shape[0] // CHUNKS // 2, h), BF16)]
    outs = (array(x.shape[0], h, dtype=F32), array(rows, h), array(rows, h), array(2 * rows, h))
    return call(
        functools.partial(near_kernel, reach), outs, (scalars, x, hidden, ends, w),
        [SMEM] + [VMEM] * 4, (VMEM,) * 4, scratch, 4 * x.shape[0] * c * h, 4 * 2**20,
    )


def forward_kernel(*refs):
    count = (len(refs) - 1) // 2
    out = refs[-1]
    for i in range(count):
        own, arrived_ref = refs[2 * i : 2 * i + 2]
        rows = own.shape[0]
        out[2 * i] = own[...]
        out[2 * i + 1] = arrived_ref[pl.ds(rows, rows)]


def forward(own, passing, after):
    operands = [v for pair in zip(own, passing) for v in pair]
    out = array(len(operands), *own[0].shape)
    return call(forward_kernel, out, operands, [VMEM] * len(operands), VMEM, [], 0, 4 * out.size, after=after)


def last_kernel(ch, s_ref, near, from_even, from_odd, g0, g1, g2, g3, hidden):
    q = s_ref[0]
    length = near.shape[0] // CHUNKS
    half, rows = length // 2, length // GROUP
    below, above = arrived(s_ref, from_even, from_odd, 0, half)
    base = ch * length
    hidden[pl.ds(0, half)] = gelu(near[pl.ds(base, half)] + below).astype(BF16)
    hidden[pl.ds(half, half)] = gelu(near[pl.ds(base + half, half)] + above).astype(BF16)
    for k, piece in enumerate((g0, g1, g2, g3)):
        piece[...] = hidden[pl.ds(pl.multiple_of((q ^ k) * rows, rows), rows)]


def last_hidden(ch, scalars, near, terms, after):
    length, h = near.shape[0] // CHUNKS, near.shape[1]
    return call(
        functools.partial(last_kernel, ch), (array(length // GROUP, h),) * GROUP,
        (scalars, near, *terms), [SMEM] + [VMEM] * 3, (VMEM,) * GROUP,
        [pltpu.VMEM((length, h), BF16)], 20 * length * h, 2 * 2**20, after=after,
    )


def early_out_kernel(first, count, s_ref, x, *refs):
    own, far = refs[:count], refs[count : 2 * count]
    core, point = refs[2 * count : 2 * count + 2]
    out, last, xs, ys, sems, osems = refs[-6:]
    q = s_ref[0]
    places, r, c = xs.shape[2:]
    rows = CHUNKS * places * r
    if first == 0:
        reads = start_all(
            [
                pltpu.make_async_copy(x.at[:, q ^ k, ch], xs.at[k, ch], sems.at[k, ch])
                for k in range(GROUP)
                for ch in range(CHUNKS)
            ]
        )
    writes = []
    for k in range(GROUP):
        if first == 0:
            wait_all(reads[k * CHUNKS : (k + 1) * CHUNKS])
        now = (xs if first == 0 else x)[k].reshape(rows, c)
        for b in range(count):
            hidden = (own[b][...], core[2 * b], far[b][pl.ds(0, rows)], core[2 * b + 1])[k]
            now = (now.astype(F32) + dot(hidden, point[first + b])).astype(BF16)
            target = last if b + 1 == count else ys.at[b]
            target[k] = now.reshape(CHUNKS, places, r, c)
            for ch in range(CHUNKS):
                writes.append(
                    pltpu.make_async_copy(
                        target.at[k, ch], out.at[first + b, :, q ^ k, ch], osems.at[b, k, ch]
                    )
                )
                writes[-1].start()
    wait_all(writes)


def early_outputs(first, scalars, x, own, far, core, point, after, before=None):
    blocks, h = point.shape[:2]
    count = len(own)
    if first == 0:
        places, group, chunks, r, c = x.shape
    else:
        group, chunks, places, r, c = x.shape
    operands = [scalars, x, *own, *far, core, point]
    specs = [SMEM, HBM if first == 0 else VMEM] + [VMEM] * (2 * count + 2)
    aliases = {}
    if before is not None:
        aliases = {len(operands): 0}
        operands.append(before)
        specs.append(HBM)
    scratch = [
        pltpu.VMEM((group, chunks, places, r, c), BF16),
        pltpu.VMEM((count, group, chunks, places, r, c), BF16),
        pltpu.SemaphoreType.DMA((group, chunks)),
        pltpu.SemaphoreType.DMA((count, group, chunks)),
    ]
    return call(
        functools.partial(early_out_kernel, first, count),
        (array(blocks, places, group, chunks, r, c), array(group, chunks, places, r, c)),
        operands, specs, (HBM, VMEM), scratch, 2 * count * x.size * h, 2 * count * 2**20, aliases, after,
    )


def late_out_kernel(ch, s_ref, a0, a1, a2, a3, point, xs, before, out, ys, osems):
    q = s_ref[0]
    places, r, c = xs.shape[2:]
    last = out.shape[0] - 1
    writes = []
    for k, hidden in enumerate((a0, a1, a2, a3)):
        x = xs[k, ch].reshape(places * r, c).astype(F32) + dot(hidden[...], point[last])
        ys[k] = x.astype(BF16).reshape(places, r, c)
        writes.append(pltpu.make_async_copy(ys.at[k], out.at[last, :, q ^ k, ch], osems.at[k]))
        writes[-1].start()
    wait_all(writes)


def late_outputs(ch, scalars, hiddens, point, xs, before):
    blocks, places, group, chunks, r, c = before.shape
    operands = (scalars, *hiddens, point, xs, before)
    scratch = [pltpu.VMEM((group, places, r, c), BF16), pltpu.SemaphoreType.DMA((group,))]
    return call(
        functools.partial(late_out_kernel, ch), array(*before.shape), operands,
        [SMEM] + [VMEM] * (GROUP + 2) + [HBM], HBM, scratch,
        2 * group * places * r * c * point.shape[1], 2 * 2**20, {len(operands) - 1: 0},
    )


def neighbour_pairs(size, parity):
    groups = size // GROUP
    pairs = []
    for i in range(size):
        group = i // GROUP
        other = group + 1 if group % 2 == parity else group - 1
        pairs.append((i, i + (other - group) * GROUP if 0 <= other < groups else i ^ 1))
    return pairs


def by_residue(signal, taps, point):
    size = lax.axis_size("seq")
    me = lax.axis_index("seq")
    length, c = signal.shape
    places = length // FIRST_DILATION
    r = FIRST_DILATION // GROUP // CHUNKS
    q, group = me % GROUP, me // GROUP
    scalars = jnp.stack(
        [q, group % 2, (group > 0).astype(jnp.int32), (group < size // GROUP - 1).astype(jnp.int32)]
    ).astype(jnp.int32)
    even_pairs, odd_pairs = neighbour_pairs(size, 0), neighbour_pairs(size, 1)
    x = signal.reshape(places, GROUP, CHUNKS, r, c)

    def swap(value, k):
        return lax.ppermute(value, "seq", [(i, i ^ k) for i in range(size)])

    def back(pieces):
        return [pieces[0]] + [swap(pieces[k], k) for k in range(1, GROUP)]

    def across(even, odd):
        return lax.ppermute(even, "seq", even_pairs), lax.ppermute(odd, "seq", odd_pairs)

    pieces = back(split(scalars, x))
    w = side_by_side(taps)
    terms = across(*open_terms(scalars, pieces, w, r))
    current = pieces
    own, core, far = [], [], []
    for block in range(2):
        reach = r * 2**block
        current, hidden, part = local_block(block, scalars, current, w, point, reach)
        current, even, odd, mine, beside, over = finish_edges(
            block, scalars, current, hidden, part, terms, w, point, reach, 2 * reach
        )
        terms = across(even, odd)
        own.append(mine)
        core.append(beside)
        far.append(swap(over, 2))
    reach = 4 * r
    current, hidden, part = local_block(2, scalars, current, w, point, reach)
    current, *sent, ends = finish_edges(
        2, scalars, current, hidden, part, terms, w, point, reach, 2 * reach
    )
    terms = [across(*sent[2 * ch : 2 * ch + 2]) for ch in range(CHUNKS)]
    near, mine, beside, over = near_terms(scalars, current, hidden, ends, w, reach)
    own.append(mine)
    core.append(beside)
    far.append(swap(over, 2))
    lasts, after = [], ()
    for ch in range(CHUNKS):
        hidden = last_hidden(ch, scalars, near, terms[ch], after)
        lasts.append(back(hidden))
        after = hidden[:1]
        if ch == 0:
            early = swap(forward(core[:2], far[:2], after), 1)
    late = swap(forward(core[2:], far[2:], after), 1)
    out, xs = early_outputs(0, scalars, x, own[:2], far[:2], early, point, after)
    out, xs = early_outputs(2, scalars, xs, own[2:], far[2:], late, point, (), out)
    for ch in range(CHUNKS):
        out = late_outputs(ch, scalars, lasts[ch], point, xs, out)
    return out.reshape(point.shape[0], length, c)


def passed_along(value, by):
    size = lax.axis_size("seq")
    pairs = [(i, i + by) for i in range(size) if 0 <= i + by < size]
    return lax.ppermute(value, "seq", pairs)


def by_neighbours(signal, taps, point):
    length = signal.shape[0]
    current = signal
    outputs = []
    for block in range(taps.shape[0]):
        step = FIRST_DILATION * 2**block
        low = dot(current, taps[block, 0]).astype(BF16)
        high = dot(current, taps[block, 2]).astype(BF16)
        if step < length:
            below = jnp.concatenate([passed_along(low[length - step :], 1), low[: length - step]])
            above = jnp.concatenate([high[step:], passed_along(high[:step], -1)])
        else:
            below = passed_along(low, step // length)
            above = passed_along(high, -(step // length))
        v = dot(current, taps[block, 1]) + below.astype(F32) + above.astype(F32)
        hidden = jax.nn.gelu(v, approximate=True).astype(BF16)
        current = (current.astype(F32) + dot(hidden, point[block])).astype(BF16)
        outputs.append(current)
    return jnp.stack(outputs)


def shards(signal, taps, point):
    fits = (
        taps.shape[0] == 4
        and signal.shape[0] == GROUP * FIRST_DILATION
        and lax.axis_size("seq") % GROUP == 0
    )
    return (by_residue if fits else by_neighbours)(signal, taps, point)


def solution(mesh):
    in_specs = (P(("grp", "seq"), None), P(), P())
    out_specs = P(None, ("grp", "seq"), None)
    return jax.shard_map(shards, mesh=mesh, in_specs=in_specs, out_specs=out_specs, check_vma=False)
```

```python
import functools

import jax
import jax.numpy as jnp
from jax import lax
from jax.experimental import pallas as pl
from jax.experimental.pallas import tpu as pltpu
from jax.sharding import PartitionSpec as P

FIRST_DILATION = 256
GROUP = 4
ROWS = 512
VMEM_LIMIT = 24 * 2**20

F32, BF16 = jnp.float32, jnp.bfloat16
ANY = pl.BlockSpec(memory_space=pl.ANY)
VMEM = pl.BlockSpec(memory_space=pltpu.VMEM)
SMEM = pl.BlockSpec(memory_space=pltpu.SMEM)
HBM = pl.BlockSpec(memory_space=pltpu.HBM)


def dot(a, b):
    return jnp.dot(a, b, preferred_element_type=F32)


def gelu(v):
    half = 0.5 * v
    inner = v * (0.7978845608028654 + 0.035677408136300125 * (v * v))
    return half + half * jnp.tanh(inner)


def over_rows(rows, body):
    for start in range(0, rows, ROWS):
        body(start, min(ROWS, rows - start))


def start_all(copies):
    for copy in copies:
        copy.start()
    return copies


def wait_all(copies):
    for copy in copies:
        copy.wait()


def call(kernel, outs, operands, specs, out_specs, scratch, flops, moved, aliases=None, after=()):
    count = len(operands)
    operands, specs = [*operands, *after], [*specs, *[ANY] * len(after)]
    body = kernel
    if after:
        kernel = lambda *refs: body(*refs[:count], *refs[count + len(after) :])
    return pl.pallas_call(
        kernel,
        out_shape=outs,
        in_specs=specs,
        out_specs=out_specs,
        scratch_shapes=scratch,
        input_output_aliases=aliases or {},
        compiler_params=pltpu.CompilerParams(vmem_limit_bytes=VMEM_LIMIT),
        cost_estimate=pl.CostEstimate(
            flops=int(flops), bytes_accessed=int(moved), transcendentals=0
        ),
    )(*operands)


def array(*shape, dtype=BF16):
    return jax.ShapeDtypeStruct(shape, dtype)


def split_kernel(s_ref, x, g0, g1, g2, g3, sems):
    q = s_ref[0]
    copies = [
        pltpu.make_async_copy(x.at[:, q ^ k], piece, sems.at[k])
        for k, piece in enumerate((g0, g1, g2, g3))
    ]
    wait_all(start_all(copies))


def split(scalars, x):
    places, group, r, c = x.shape
    pieces = (array(places, r, c),) * group
    sems = [pltpu.SemaphoreType.DMA((group,))]
    pieces = call(split_kernel, pieces, (scalars, x), [SMEM, HBM], (VMEM,) * group, sems, 0, 4 * x.size)
    return [piece.reshape(places * r, c) for piece in pieces]


def side_by_side_kernel(taps, w, sems):
    h = taps.shape[3]
    wait_all(
        start_all(
            [
                pltpu.make_async_copy(
                    taps.at[b, t], w.at[b, :, pl.ds(t * h, h)], sems.at[b, t]
                )
                for b in range(taps.shape[0])
                for t in range(3)
            ]
        )
    )


def side_by_side(taps):
    blocks, count, c, h = taps.shape
    sems = [pltpu.SemaphoreType.DMA((blocks, count))]
    return call(side_by_side_kernel, array(blocks, c, count * h), (taps,), [HBM], VMEM, sems, 0, 4 * taps.size)


def place_terms(parity, up, down, even_ref, odd_ref, start, size):
    even_ref[pl.ds(start, size)] = jnp.where(parity == 0, up, down).astype(BF16)
    odd_ref[pl.ds(start, size)] = jnp.where(parity == 0, down, up).astype(BF16)


def arrived(s_ref, from_even, from_odd, start, size):
    even = from_even[pl.ds(start, size)].astype(F32)
    odd = from_odd[pl.ds(start, size)].astype(F32)
    parity, has_lower, has_upper = s_ref[1], s_ref[2], s_ref[3]
    below = jnp.where(has_lower == 0, 0.0, jnp.where(parity == 0, odd, even))
    above = jnp.where(has_upper == 0, 0.0, jnp.where(parity == 0, even, odd))
    return below, above


def open_kernel(r, s_ref, own, r1, r2, r3, w, even_ref, odd_ref, ends):
    q, parity = s_ref[0], s_ref[1]
    rows = own.shape[0]
    h = even_ref.shape[1]

    def fetch(piece, at, to):
        ends[pl.ds(to, r)] = piece[pl.ds(at, r)]

    for k, piece in enumerate((own, r1, r2, r3)):
        pl.when(q ^ k == GROUP - 1)(functools.partial(fetch, piece, rows - r, 0))
        pl.when(q ^ k == 0)(functools.partial(fetch, piece, 0, r))
    up = dot(ends[pl.ds(0, r)], w[0, :, :h])
    down = dot(ends[pl.ds(r, r)], w[0, :, 2 * h :])
    place_terms(parity, up, down, even_ref, odd_ref, 0, r)


def open_terms(scalars, pieces, w, r, after):
    c, h = w.shape[1], w.shape[2] // 3
    terms = array(r, h)
    return call(
        functools.partial(open_kernel, r), (terms, terms), (scalars, *pieces, w),
        [SMEM] + [VMEM] * (GROUP + 1), (VMEM, VMEM), [pltpu.VMEM((2 * r, c), BF16)],
        4 * r * c * h, 2**20, after=after,
    )


def keep_terms(at, terms, low, mid, high):
    h = mid.shape[1]
    low[at] = terms[:, :h].astype(BF16)
    mid[at] = terms[:, h : 2 * h]
    high[at] = terms[:, 2 * h :].astype(BF16)


def piece_taps(q, first, pieces, w, x, low, mid, high):
    for i, piece in enumerate(pieces):
        rows = piece.shape[0]
        at = pl.ds(pl.multiple_of((q ^ (first + i)) * rows, rows), rows)
        x[at] = piece[...]
        keep_terms(at, dot(piece[...], w[0]), low, mid, high)


def block_body(reach, x, point, x_ref, h_ref, part_ref, low, mid, high):
    length = x.shape[0]
    top = length - reach

    def body(start, size):
        at = reach + start
        v = mid[pl.ds(at, size)] + low[pl.ds(start, size)].astype(F32)
        hidden = gelu(v + high[pl.ds(at + reach, size)].astype(F32)).astype(BF16)
        h_ref[pl.ds(at, size)] = hidden
        x_ref[pl.ds(at, size)] = (x[pl.ds(at, size)].astype(F32) + dot(hidden, point)).astype(BF16)

    over_rows(length - 2 * reach, body)
    part_ref[pl.ds(0, reach)] = mid[pl.ds(0, reach)] + high[pl.ds(reach, reach)].astype(F32)
    part_ref[pl.ds(reach, reach)] = mid[pl.ds(top, reach)] + low[pl.ds(top - reach, reach)].astype(F32)
    for at in (0, top):
        x_ref[pl.ds(at, reach)] = x[pl.ds(at, reach)]
        h_ref[pl.ds(at, reach)] = jnp.zeros((reach, h_ref.shape[1]), BF16)


def early_taps_kernel(s_ref, own, r1, w, x, low, mid, high):
    piece_taps(s_ref[0], 0, (own, r1), w, x, low, mid, high)


def early_taps(scalars, pieces, w):
    c, h = w.shape[1], w.shape[2] // 3
    rows = pieces[0].shape[0]
    length = GROUP * rows
    outs = (array(length, c), array(length, h), array(length, h, dtype=F32), array(length, h))
    return call(
        early_taps_kernel, outs, (scalars, *pieces, w), [SMEM] + [VMEM] * 3, (VMEM,) * 4, [],
        12 * rows * c * h, 2**20,
    )


def first_kernel(reach, s_ref, r2, r3, x, low, mid, high, w, point, *refs):
    piece_taps(s_ref[0], 2, (r2, r3), w, x, low, mid, high)
    block_body(reach, x, point[0], *refs[:3], low, mid, high)


def first_block(scalars, early, pieces, w, point, reach):
    c, h = w.shape[1], w.shape[2] // 3
    length = early[0].shape[0]
    outs = (array(length, c), array(length, h), array(2 * reach, h, dtype=F32))
    outs += tuple(array(*e.shape, dtype=e.dtype) for e in early)
    results = call(
        functools.partial(first_kernel, reach), outs, (scalars, *pieces, *early, w, point),
        [SMEM] + [VMEM] * 8, (VMEM,) * 7, [], 8 * length * c * h, 4 * 2**20,
        {3: 3, 4: 4, 5: 5, 6: 6},
    )
    return results[:3]


def middle_kernel(block, reach, parity_ref, x, w, point, x_ref, h_ref, part_ref, *refs):
    sent, (low, mid, high) = refs[:-3], refs[-3:]
    h = mid.shape[1]

    def body(start, size):
        at = pl.ds(start, size)
        keep_terms(at, dot(x[at], w[block]), low, mid, high)

    over_rows(x.shape[0], body)
    block_body(reach, x, point[block], x_ref, h_ref, part_ref, low, mid, high)
    if sent:
        middle = x.shape[0] // 2
        up = dot(x_ref[pl.ds(middle, reach)], w[block + 1, :, :h])
        down = dot(x_ref[pl.ds(middle - reach, reach)], w[block + 1, :, 2 * h :])
        place_terms(parity_ref[1], up, down, *sent, 0, reach)


def middle_block(block, scalars, x, w, point, reach):
    c, h = w.shape[1], w.shape[2] // 3
    length = x.shape[0]
    outs = (array(length, c), array(length, h), array(2 * reach, h, dtype=F32))
    if block + 2 == w.shape[0]:
        outs += (array(reach, h),) * 2
    scratch = [
        pltpu.VMEM((length, h), BF16),
        pltpu.VMEM((length, h), F32),
        pltpu.VMEM((length, h), BF16),
    ]
    return call(
        functools.partial(middle_kernel, block, reach), outs, (scalars, x, w, point),
        [SMEM] + [VMEM] * 3, (VMEM,) * len(outs), scratch, 8 * length * c * h, 4 * 2**20,
    )


def give_back(q, hidden, reach, edges, refs, first):
    rows = hidden.shape[0] // GROUP
    for i, ref in enumerate(refs):
        j = q ^ (first + i)
        ref[...] = hidden[pl.ds(pl.multiple_of(j * rows, rows), rows)]

        @pl.when(j == 0)
        def _(ref=ref):
            ref[pl.ds(0, reach)] = edges[0]

        @pl.when(j == GROUP - 1)
        def _(ref=ref):
            ref[pl.ds(rows - reach, reach)] = edges[1]


def edge_kernel(
    block, reach, ahead, s_ref, x, hidden, part, from_even, from_odd, w, point,
    x_ref, even_ref, odd_ref, far_ref, *refs
):
    q, parity = s_ref[0], s_ref[1]
    length = x.shape[0]
    h = hidden.shape[1]
    rows = length // GROUP
    below, above = arrived(s_ref, from_even, from_odd, 0, reach)
    edges = (
        gelu(part[pl.ds(0, reach)] + below).astype(BF16),
        gelu(part[pl.ds(reach, reach)] + above).astype(BF16),
    )
    more = dot(jnp.concatenate(edges), point[block])
    for i, at in enumerate((0, length - reach)):
        new = x[pl.ds(at, reach)].astype(F32) + more[i * reach : (i + 1) * reach]
        x_ref[pl.ds(at, reach)] = new.astype(BF16)
    up = dot(x_ref[pl.ds(length - ahead, ahead)], w[block + 1, :, :h])
    down = dot(x_ref[pl.ds(0, ahead)], w[block + 1, :, 2 * h :])
    place_terms(parity, up, down, even_ref, odd_ref, 0, ahead)
    give_back(q, hidden, reach, edges, (far_ref.at[0], far_ref.at[1]), 2)
    if block + 2 < w.shape[0]:
        give_back(q, hidden, reach, edges, refs, 1)
    else:
        refs[0][0] = edges[0]
        refs[0][1] = edges[1]


def finish_edges(block, scalars, x, hidden, part, terms, w, point, reach, ahead, after=()):
    c, h = w.shape[1], w.shape[2] // 3
    rows = x.shape[0] // GROUP
    outs = (array(*x.shape),) + (array(ahead, h),) * 2 + (array(2, rows, h),)
    outs += (array(2, reach, h),) if block + 2 == w.shape[0] else (array(rows, h),)
    return call(
        functools.partial(edge_kernel, block, reach, ahead), outs,
        (scalars, x, hidden, part, *terms, w, point),
        [SMEM] + [VMEM] * 7, (VMEM,) * len(outs), [],
        2 * c * h * (2 * reach + 2 * ahead), 4 * 2**20, {1: 0}, after,
    )


def near_kernel(reach, s_ref, x, hidden, ends, from_even, from_odd, w, h_ref, near_ref, core_ref, other):
    length = x.shape[0]
    half = length // 2
    h = near_ref.shape[1]
    block = w.shape[0] - 1
    terms = dot(x[pl.ds(0, half)], w[block, :, : 2 * h])
    other[...] = terms[:, :h].astype(BF16)
    near_ref[...] = terms[:, h:]
    terms = dot(x[pl.ds(half, half)], w[block, :, h:])
    high = terms[:, h:].astype(BF16).astype(F32)
    lower = near_ref[...] + high
    upper = terms[:, :h] + other[...].astype(F32)
    below, above = arrived(s_ref, from_even, from_odd, 0, reach)
    h_ref[0] = gelu(lower[:reach] + below).astype(BF16)
    h_ref[1] = gelu(upper[reach:] + above).astype(BF16)
    near_ref[pl.ds(0, reach)] = lower[reach:]
    near_ref[pl.ds(reach, reach)] = upper[:reach]
    give_back(s_ref[0], hidden, reach, (ends[0], ends[1]), (core_ref,), 1)


def near_terms(scalars, x, hidden, ends, terms, w, reach):
    c, h = w.shape[1], w.shape[2] // 3
    rows = x.shape[0] // GROUP
    half = x.shape[0] // 2
    scratch = [pltpu.VMEM((half, h), BF16)]
    outs = (array(2, reach, h), array(half, h, dtype=F32), array(rows, h))
    return call(
        functools.partial(near_kernel, reach), outs, (scalars, x, hidden, ends, *terms, w),
        [SMEM] + [VMEM] * 6, (VMEM,) * 3, scratch, 4 * x.shape[0] * c * h, 4 * 2**20,
    )


def forward_kernel(*refs):
    out = refs[-1]
    for i in range((len(refs) - 1) // 2):
        out[2 * i] = refs[2 * i][...]
        out[2 * i + 1] = refs[2 * i + 1][1]


def forward(own, passing, after):
    operands = [v for pair in zip(own, passing) for v in pair]
    out = array(len(operands), *own[0].shape)
    return call(forward_kernel, out, operands, [VMEM] * len(operands), VMEM, [], 0, 4 * out.size, after=after)


def last_kernel(s_ref, outer, near, from_even, from_odd, g0, g1, g2, g3, hidden):
    q = s_ref[0]
    reach, h = outer.shape[1:]
    below, above = arrived(s_ref, from_even, from_odd, 0, reach)
    hidden[0] = outer[0]
    hidden[1] = gelu(near[pl.ds(0, reach)] + below).astype(BF16)
    hidden[2] = gelu(near[pl.ds(reach, reach)] + above).astype(BF16)
    hidden[3] = outer[1]
    for k, piece in enumerate((g0, g1, g2, g3)):
        piece[...] = hidden[q ^ k]


def last_hidden(scalars, outer, near, terms, after):
    half, h = near.shape
    return call(
        last_kernel, (array(half // 2, h),) * GROUP, (scalars, outer, near, *terms),
        [SMEM] + [VMEM] * 4, (VMEM,) * GROUP, [pltpu.VMEM((GROUP, half // 2, h), BF16)],
        20 * half * h, 2 * 2**20, after=after,
    )


def early_out_kernel(count, s_ref, x, *refs):
    own, far = refs[:count], refs[count : 2 * count]
    core, lasts, point = refs[2 * count], refs[2 * count + 1 : 2 * count + 3], refs[2 * count + 3]
    out, last, xs, ys, sems, osems = refs[-6:]
    q = s_ref[0]
    places, r, c = xs.shape[1:]
    rows = places * r
    here = pl.ds(pl.multiple_of(q * places, places), places)
    writes = []
    for b in range(count):
        writes.append(pltpu.make_async_copy(own[b].at[here], out.at[b, :, q], osems.at[b, 0]))
    start_all(writes)
    reads = start_all(
        [pltpu.make_async_copy(x.at[:, q ^ k], xs.at[k], sems.at[k]) for k in range(1, GROUP)]
    )

    def write(b, k, now):
        target = last if b + 1 == count else ys.at[min(b, count - 1)]
        target[k] = now.reshape(places, r, c)
        writes.append(pltpu.make_async_copy(target.at[k], out.at[b, :, q ^ k], osems.at[b, k]))
        writes[-1].start()

    for k in range(GROUP):
        if k == 0:
            now = own[count - 1][here].reshape(rows, c)
        else:
            reads[k - 1].wait()
            now = xs[k].reshape(rows, c)
            for b in range(count):
                hidden = (core[2 * b], far[b][0], core[2 * b + 1])[k - 1]
                now = (now.astype(F32) + dot(hidden, point[b])).astype(BF16)
                write(b, k, now)
        if k < 2:
            write(count, k, (now.astype(F32) + dot(lasts[k][...], point[count])).astype(BF16))
    wait_all(writes)


def early_outputs(scalars, x, own, far, core, lasts, point):
    blocks, h = point.shape[:2]
    places, group, r, c = x.shape
    count = blocks - 1
    own = [v.reshape(group * places, r, c) for v in own]
    operands = [scalars, x, *own, *far, core, *lasts, point]
    scratch = [
        pltpu.VMEM((group, places, r, c), BF16),
        pltpu.VMEM((count, group, places, r, c), BF16),
        pltpu.SemaphoreType.DMA((group,)),
        pltpu.SemaphoreType.DMA((blocks, group)),
    ]
    return call(
        functools.partial(early_out_kernel, count),
        (array(blocks, places, group, r, c), array(group, places, r, c)),
        operands, [SMEM, HBM] + [VMEM] * (len(operands) - 2), (HBM, VMEM), scratch,
        2 * blocks * x.size * h, 8 * 2**20,
    )


def late_out_kernel(s_ref, a2, a3, xs, point, _, out, ys, osems):
    q = s_ref[0]
    places, r, c = xs.shape[1:]
    last = out.shape[0] - 1
    writes = []
    for i, hidden in enumerate((a2, a3)):
        x = xs[2 + i].reshape(places * r, c).astype(F32) + dot(hidden[...], point[last])
        ys[i] = x.astype(BF16).reshape(places, r, c)
        writes.append(pltpu.make_async_copy(ys.at[i], out.at[last, :, q ^ (2 + i)], osems.at[i]))
        writes[-1].start()
    wait_all(writes)


def late_outputs(scalars, hiddens, xs, point, before):
    blocks, places, group, r, c = before.shape
    operands = (scalars, *hiddens, xs, point, before)
    scratch = [pltpu.VMEM((2, places, r, c), BF16), pltpu.SemaphoreType.DMA((2,))]
    return call(
        late_out_kernel, array(*before.shape), operands,
        [SMEM] + [VMEM] * 4 + [HBM], HBM, scratch,
        4 * places * r * c * point.shape[1], 2 * 2**20, {len(operands) - 1: 0},
    )


def neighbour_pairs(size, parity):
    groups = size // GROUP
    pairs = []
    for i in range(size):
        group = i // GROUP
        other = group + 1 if group % 2 == parity else group - 1
        pairs.append((i, i + (other - group) * GROUP if 0 <= other < groups else i ^ 1))
    return pairs


def by_residue(signal, taps, point):
    size = lax.axis_size("seq")
    me = lax.axis_index("seq")
    length, c = signal.shape
    places = length // FIRST_DILATION
    r = FIRST_DILATION // GROUP
    q, group = me % GROUP, me // GROUP
    scalars = jnp.stack(
        [q, group % 2, (group > 0).astype(jnp.int32), (group < size // GROUP - 1).astype(jnp.int32)]
    ).astype(jnp.int32)
    even_pairs, odd_pairs = neighbour_pairs(size, 0), neighbour_pairs(size, 1)
    x = signal.reshape(places, GROUP, r, c)

    def swap(value, k):
        return lax.ppermute(value, "seq", [(i, i ^ k) for i in range(size)])

    def back(pieces):
        return [pieces[0]] + [swap(pieces[k], k) for k in range(1, GROUP)]

    def across(even, odd):
        return lax.ppermute(even, "seq", even_pairs), lax.ppermute(odd, "seq", odd_pairs)

    pieces = back(split(scalars, x))
    w = side_by_side(taps)
    early = early_taps(scalars, pieces[:2], w)
    terms = across(*open_terms(scalars, pieces, w, r, early[:1]))
    own, core, far = [], [], []
    for block in range(2):
        reach = r * 2**block
        if block == 0:
            current, hidden, part = first_block(scalars, early, pieces[2:], w, point, reach)
        else:
            current, hidden, part = middle_block(block, scalars, current, w, point, reach)
        current, even, odd, over, beside = finish_edges(
            block, scalars, current, hidden, part, terms, w, point, reach, 2 * reach
        )
        terms = across(even, odd)
        own.append(current)
        core.append(beside)
        far.append(swap(over, 2))
    reach = 4 * r
    current, hidden, part, *inner = middle_block(2, scalars, current, w, point, reach)
    inner = across(*inner)
    current, even, odd, over, ends = finish_edges(
        2, scalars, current, hidden, part, terms, w, point, reach, reach, far[:1]
    )
    terms = across(even, odd)
    own.append(current)
    far.append(swap(over, 2))
    outer, near, beside = near_terms(scalars, current, hidden, ends, inner, w, reach)
    core.append(beside)
    hidden = last_hidden(scalars, outer, near, terms, far[1:2])
    after = (hidden[0],)
    lasts = back(hidden)
    beside = swap(forward(core, far, after), 1)
    out, xs = early_outputs(scalars, x, own, far, beside, lasts[:2], point)
    out = late_outputs(scalars, lasts[2:], xs, point, out)
    return out.reshape(point.shape[0], length, c)


def passed_along(value, by):
    size = lax.axis_size("seq")
    pairs = [(i, i + by) for i in range(size) if 0 <= i + by < size]
    return lax.ppermute(value, "seq", pairs)


def by_neighbours(signal, taps, point):
    length = signal.shape[0]
    current = signal
    outputs = []
    for block in range(taps.shape[0]):
        step = FIRST_DILATION * 2**block
        low = dot(current, taps[block, 0]).astype(BF16)
        high = dot(current, taps[block, 2]).astype(BF16)
        if step < length:
            below = jnp.concatenate([passed_along(low[length - step :], 1), low[: length - step]])
            above = jnp.concatenate([high[step:], passed_along(high[:step], -1)])
        else:
            below = passed_along(low, step // length)
            above = passed_along(high, -(step // length))
        v = dot(current, taps[block, 1]) + below.astype(F32) + above.astype(F32)
        hidden = jax.nn.gelu(v, approximate=True).astype(BF16)
        current = (current.astype(F32) + dot(hidden, point[block])).astype(BF16)
        outputs.append(current)
    return jnp.stack(outputs)


def shards(signal, taps, point):
    fits = (
        taps.shape[0] == 4
        and signal.shape[0] == GROUP * FIRST_DILATION
        and lax.axis_size("seq") % GROUP == 0
    )
    return (by_residue if fits else by_neighbours)(signal, taps, point)


def solution(mesh):
    in_specs = (P(("grp", "seq"), None), P(), P())
    out_specs = P(None, ("grp", "seq"), None)
    return jax.shard_map(shards, mesh=mesh, in_specs=in_specs, out_specs=out_specs, check_vma=False)
```

```python
import functools

import jax
import jax.numpy as jnp
from jax import lax
from jax.experimental import pallas as pl
from jax.experimental.pallas import tpu as pltpu
from jax.sharding import PartitionSpec as P

FIRST_DILATION = 256
GROUP = 4
ROWS = 512
VMEM_LIMIT = 24 * 2**20

F32, BF16 = jnp.float32, jnp.bfloat16
ANY = pl.BlockSpec(memory_space=pl.ANY)
VMEM = pl.BlockSpec(memory_space=pltpu.VMEM)
SMEM = pl.BlockSpec(memory_space=pltpu.SMEM)
HBM = pl.BlockSpec(memory_space=pltpu.HBM)


def dot(a, b):
    return jnp.dot(a, b, preferred_element_type=F32)


def gelu(v):
    half = 0.5 * v
    inner = v * (0.7978845608028654 + 0.035677408136300125 * (v * v))
    return half + half * jnp.tanh(inner)


def over_rows(rows, body):
    for start in range(0, rows, ROWS):
        body(start, min(ROWS, rows - start))


def start_all(copies):
    for copy in copies:
        copy.start()
    return copies


def wait_all(copies):
    for copy in copies:
        copy.wait()


def call(kernel, outs, operands, specs, out_specs, scratch, flops, moved, aliases=None, after=()):
    count = len(operands)
    operands, specs = [*operands, *after], [*specs, *[ANY] * len(after)]
    body = kernel
    if after:
        kernel = lambda *refs: body(*refs[:count], *refs[count + len(after) :])
    return pl.pallas_call(
        kernel,
        out_shape=outs,
        in_specs=specs,
        out_specs=out_specs,
        scratch_shapes=scratch,
        input_output_aliases=aliases or {},
        compiler_params=pltpu.CompilerParams(vmem_limit_bytes=VMEM_LIMIT),
        cost_estimate=pl.CostEstimate(
            flops=int(flops), bytes_accessed=int(moved), transcendentals=0
        ),
    )(*operands)


def array(*shape, dtype=BF16):
    return jax.ShapeDtypeStruct(shape, dtype)


def split_kernel(s_ref, x, own, beside, over, rest, sems):
    q = s_ref[0]
    places = x.shape[0]
    is_top = q == GROUP - 1
    edge = pl.ds(jnp.where(is_top, places - 1, 0), 1)
    others = pl.ds(jnp.where(is_top, 0, 1), places - 1)
    copies = [
        pltpu.make_async_copy(source, target, sems.at[i])
        for i, (source, target) in enumerate(
            (
                (x.at[:, q ^ 2], over.at[pl.ds(0, places)]),
                (x.at[edge, q ^ 3], over.at[pl.ds(places, 1)]),
                (x.at[others, q ^ 3], rest),
                (x.at[:, q ^ 1], beside),
                (x.at[:, q], own),
            )
        )
    ]
    wait_all(start_all(copies))


def split(scalars, x):
    places, group, r, c = x.shape
    x = pltpu.with_memory_space_constraint(x, pltpu.HBM)
    outs = [array(n, r, c) for n in (places, places, places + 1, places - 1)]
    sems = [pltpu.SemaphoreType.DMA((5,))]
    pieces = call(split_kernel, outs, (scalars, x), [SMEM, HBM], (VMEM,) * 4, sems, 0, 4 * x.size)
    return [piece.reshape(piece.shape[0] * r, c) for piece in pieces]


def edge_part_kernel(over, out):
    out[...] = over[pl.ds(over.shape[0] - out.shape[0], out.shape[0])]


def edge_part(over, r, after):
    out = array(r, over.shape[1])
    return call(edge_part_kernel, out, (over,), [VMEM], VMEM, [], 0, 2 * out.size, after=after)


def side_by_side_kernel(taps, w, sems):
    h = taps.shape[3]
    wait_all(
        start_all(
            [
                pltpu.make_async_copy(
                    taps.at[b, t], w.at[b, :, pl.ds(t * h, h)], sems.at[b, t]
                )
                for b in range(taps.shape[0])
                for t in range(3)
            ]
        )
    )


def side_by_side(taps):
    blocks, count, c, h = taps.shape
    sems = [pltpu.SemaphoreType.DMA((blocks, count))]
    taps = pltpu.with_memory_space_constraint(taps, pltpu.HBM)
    return call(side_by_side_kernel, array(blocks, c, count * h), (taps,), [HBM], VMEM, sems, 0, 4 * taps.size)


def place_terms(parity, up, down, even_ref, odd_ref, start, size):
    even_ref[pl.ds(start, size)] = jnp.where(parity == 0, up, down).astype(BF16)
    odd_ref[pl.ds(start, size)] = jnp.where(parity == 0, down, up).astype(BF16)


def arrived(s_ref, from_even, from_odd, start, size):
    even = from_even[pl.ds(start, size)].astype(F32)
    odd = from_odd[pl.ds(start, size)].astype(F32)
    parity, has_lower, has_upper = s_ref[1], s_ref[2], s_ref[3]
    below = jnp.where(has_lower == 0, 0.0, jnp.where(parity == 0, odd, even))
    above = jnp.where(has_upper == 0, 0.0, jnp.where(parity == 0, even, odd))
    return below, above


def open_kernel(r, s_ref, own, beside, over, edge, w, even_ref, odd_ref, ends):
    q, parity = s_ref[0], s_ref[1]
    h = even_ref.shape[1]
    last = own.shape[0] - r

    def fetch(piece, at, to):
        ends[pl.ds(to, r)] = piece[pl.ds(at, r)]

    for k, (piece, top) in enumerate(((own, last), (beside, last), (over, last), (edge, 0))):
        pl.when(q ^ k == GROUP - 1)(functools.partial(fetch, piece, top, 0))
        pl.when(q ^ k == 0)(functools.partial(fetch, piece, 0, r))
    up = dot(ends[pl.ds(0, r)], w[0, :, :h])
    down = dot(ends[pl.ds(r, r)], w[0, :, 2 * h :])
    place_terms(parity, up, down, even_ref, odd_ref, 0, r)


def open_terms(scalars, pieces, w, r):
    c, h = w.shape[1], w.shape[2] // 3
    terms = array(r, h)
    return call(
        functools.partial(open_kernel, r), (terms, terms), (scalars, *pieces, w),
        [SMEM] + [VMEM] * (GROUP + 1), (VMEM, VMEM), [pltpu.VMEM((2 * r, c), BF16)],
        4 * r * c * h, 2**20,
    )


def keep_terms(at, terms, low, mid, high):
    h = mid.shape[1]
    low[at] = terms[:, :h].astype(BF16)
    mid[at] = terms[:, h : 2 * h]
    high[at] = terms[:, 2 * h :].astype(BF16)


def piece_taps(at, piece, w, x, low, mid, high):
    x[at] = piece
    keep_terms(at, dot(piece, w[0]), low, mid, high)


def part_rows(j, rows, r, first):
    is_top = j == GROUP - 1
    if first:
        return pl.ds(pl.multiple_of(j * rows + jnp.where(is_top, rows - r, 0), r), r)
    return pl.ds(pl.multiple_of(j * rows + jnp.where(is_top, 0, r), r), rows - r)


def block_body(reach, x, point, x_ref, h_ref, part_ref, low, mid, high):
    length = x.shape[0]
    top = length - reach

    def body(start, size):
        at = reach + start
        v = mid[pl.ds(at, size)] + low[pl.ds(start, size)].astype(F32)
        hidden = gelu(v + high[pl.ds(at + reach, size)].astype(F32)).astype(BF16)
        h_ref[pl.ds(at, size)] = hidden
        x_ref[pl.ds(at, size)] = (x[pl.ds(at, size)].astype(F32) + dot(hidden, point)).astype(BF16)

    over_rows(length - 2 * reach, body)
    part_ref[pl.ds(0, reach)] = mid[pl.ds(0, reach)] + high[pl.ds(reach, reach)].astype(F32)
    part_ref[pl.ds(reach, reach)] = mid[pl.ds(top, reach)] + low[pl.ds(top - reach, reach)].astype(F32)
    for at in (0, top):
        x_ref[pl.ds(at, reach)] = x[pl.ds(at, reach)]
        h_ref[pl.ds(at, reach)] = jnp.zeros((reach, h_ref.shape[1]), BF16)


def early_taps_kernel(s_ref, own, beside, w, x, low, mid, high):
    rows = own.shape[0]
    for k, piece in enumerate((own, beside)):
        at = pl.ds(pl.multiple_of((s_ref[0] ^ k) * rows, rows), rows)
        piece_taps(at, piece[...], w, x, low, mid, high)


def early_taps(scalars, own, beside, w):
    c, h = w.shape[1], w.shape[2] // 3
    rows = own.shape[0]
    length = GROUP * rows
    outs = (array(length, c), array(length, h), array(length, h, dtype=F32), array(length, h))
    return call(
        early_taps_kernel, outs, (scalars, own, beside, w), [SMEM] + [VMEM] * 3, (VMEM,) * 4, [],
        12 * rows * c * h, 2**20,
    )


def more_taps_kernel(s_ref, over, edge, w, *refs):
    x, low, mid, high = refs[4:]
    q = s_ref[0]
    rows, r = x.shape[0] // GROUP, edge.shape[0]
    at = pl.ds(pl.multiple_of((q ^ 2) * rows, rows), rows)
    piece_taps(at, over[pl.ds(0, rows)], w, x, low, mid, high)
    piece_taps(part_rows(q ^ 3, rows, r, True), edge[...], w, x, low, mid, high)


def more_taps(scalars, over, edge, w, early):
    c, h = w.shape[1], w.shape[2] // 3
    return call(
        more_taps_kernel, tuple(array(*e.shape, dtype=e.dtype) for e in early),
        (scalars, over, edge, w, *early), [SMEM] + [VMEM] * 7, (VMEM,) * 4, [],
        6 * over.shape[0] * c * h, 2**20, {4: 0, 5: 1, 6: 2, 7: 3},
    )


def first_kernel(
    r, s_ref, rest, x, low, mid, high, from_even, from_odd, w, point,
    x_ref, even_ref, odd_ref, far_ref, core_ref, *refs
):
    hidden = refs[-1]
    q, parity = s_ref[0], s_ref[1]
    length = x.shape[0]
    rows = length // GROUP
    h = mid.shape[1]
    piece_taps(part_rows(q ^ 3, rows, r, False), rest[...], w, x, low, mid, high)
    below, above = arrived(s_ref, from_even, from_odd, 0, r)

    def finish(start, size, v):
        at = pl.ds(start, size)
        hidden[at] = gelu(v).astype(BF16)
        x_ref[at] = (x[at].astype(F32) + dot(hidden[at], point[0])).astype(BF16)

    def body(start, size):
        v = mid[pl.ds(start, size)]
        if start == 0:
            low_terms = jnp.concatenate([below, low[pl.ds(0, size - r)].astype(F32)])
        else:
            low_terms = low[pl.ds(start - r, size)].astype(F32)
        if start + size == length:
            high_terms = jnp.concatenate([high[pl.ds(start + r, size - r)].astype(F32), above])
        else:
            high_terms = high[pl.ds(start + r, size)].astype(F32)
        finish(start, size, v + low_terms + high_terms)

    over_rows(length, body)
    ahead = even_ref.shape[0]
    up = dot(x_ref[pl.ds(length - ahead, ahead)], w[1, :, :h])
    down = dot(x_ref[pl.ds(0, ahead)], w[1, :, 2 * h :])
    place_terms(parity, up, down, even_ref, odd_ref, 0, ahead)
    for k, ref in ((1, core_ref), (2, far_ref.at[0]), (3, far_ref.at[1])):
        ref[...] = hidden[pl.ds(pl.multiple_of((q ^ k) * rows, rows), rows)]


def first_block(scalars, rest, early, terms, w, point, r):
    c, h = w.shape[1], w.shape[2] // 3
    length = early[0].shape[0]
    rows = length // GROUP
    outs = (array(length, c), array(2 * r, h), array(2 * r, h), array(2, rows, h), array(rows, h))
    outs += tuple(array(*e.shape, dtype=e.dtype) for e in early)
    results = call(
        functools.partial(first_kernel, r), outs, (scalars, rest, *early, *terms, w, point),
        [SMEM] + [VMEM] * 9, (VMEM,) * 9, [pltpu.VMEM((length, h), BF16)],
        8 * length * c * h, 4 * 2**20, {2: 5, 3: 6, 4: 7, 5: 8},
    )
    return results[:5]


def middle_kernel(block, reach, parity_ref, x, w, point, x_ref, h_ref, part_ref, *refs):
    sent, (low, mid, high) = refs[:-3], refs[-3:]
    h = mid.shape[1]

    def body(start, size):
        at = pl.ds(start, size)
        keep_terms(at, dot(x[at], w[block]), low, mid, high)

    over_rows(x.shape[0], body)
    block_body(reach, x, point[block], x_ref, h_ref, part_ref, low, mid, high)
    if sent:
        middle = x.shape[0] // 2
        up = dot(x_ref[pl.ds(middle, reach)], w[block + 1, :, :h])
        down = dot(x_ref[pl.ds(middle - reach, reach)], w[block + 1, :, 2 * h :])
        place_terms(parity_ref[1], up, down, *sent, 0, reach)


def middle_block(block, scalars, x, w, point, reach, after=()):
    c, h = w.shape[1], w.shape[2] // 3
    length = x.shape[0]
    outs = (array(length, c), array(length, h), array(2 * reach, h, dtype=F32))
    if block + 2 == w.shape[0]:
        outs += (array(reach, h),) * 2
    scratch = [
        pltpu.VMEM((length, h), BF16),
        pltpu.VMEM((length, h), F32),
        pltpu.VMEM((length, h), BF16),
    ]
    return call(
        functools.partial(middle_kernel, block, reach), outs, (scalars, x, w, point),
        [SMEM] + [VMEM] * 3, (VMEM,) * len(outs), scratch, 8 * length * c * h, 4 * 2**20, after=after,
    )


def give_back(q, hidden, reach, edges, refs, first):
    rows = hidden.shape[0] // GROUP
    for i, ref in enumerate(refs):
        j = q ^ (first + i)
        ref[...] = hidden[pl.ds(pl.multiple_of(j * rows, rows), rows)]

        @pl.when(j == 0)
        def _(ref=ref):
            ref[pl.ds(0, reach)] = edges[0]

        @pl.when(j == GROUP - 1)
        def _(ref=ref):
            ref[pl.ds(rows - reach, reach)] = edges[1]


def edge_kernel(
    block, reach, ahead, s_ref, x, hidden, part, from_even, from_odd, w, point,
    x_ref, even_ref, odd_ref, far_ref, *refs
):
    q, parity = s_ref[0], s_ref[1]
    length = x.shape[0]
    h = hidden.shape[1]
    rows = length // GROUP
    below, above = arrived(s_ref, from_even, from_odd, 0, reach)
    edges = (
        gelu(part[pl.ds(0, reach)] + below).astype(BF16),
        gelu(part[pl.ds(reach, reach)] + above).astype(BF16),
    )
    more = dot(jnp.concatenate(edges), point[block])
    for i, at in enumerate((0, length - reach)):
        new = x[pl.ds(at, reach)].astype(F32) + more[i * reach : (i + 1) * reach]
        x_ref[pl.ds(at, reach)] = new.astype(BF16)
    up = dot(x_ref[pl.ds(length - ahead, ahead)], w[block + 1, :, :h])
    down = dot(x_ref[pl.ds(0, ahead)], w[block + 1, :, 2 * h :])
    place_terms(parity, up, down, even_ref, odd_ref, 0, ahead)
    give_back(q, hidden, reach, edges, (far_ref.at[0], far_ref.at[1]), 2)
    if block + 2 < w.shape[0]:
        give_back(q, hidden, reach, edges, refs, 1)
    else:
        refs[0][0] = edges[0]
        refs[0][1] = edges[1]


def finish_edges(block, scalars, x, hidden, part, terms, w, point, reach, ahead, after=()):
    c, h = w.shape[1], w.shape[2] // 3
    rows = x.shape[0] // GROUP
    outs = (array(*x.shape),) + (array(ahead, h),) * 2 + (array(2, rows, h),)
    outs += (array(2, reach, h),) if block + 2 == w.shape[0] else (array(rows, h),)
    return call(
        functools.partial(edge_kernel, block, reach, ahead), outs,
        (scalars, x, hidden, part, *terms, w, point),
        [SMEM] + [VMEM] * 7, (VMEM,) * len(outs), [],
        2 * c * h * (2 * reach + 2 * ahead), 4 * 2**20, {1: 0}, after,
    )


def near_kernel(reach, s_ref, x, hidden, ends, from_even, from_odd, w, h_ref, near_ref, core_ref, other):
    length = x.shape[0]
    half = length // 2
    h = near_ref.shape[1]
    block = w.shape[0] - 1
    terms = dot(x[pl.ds(0, half)], w[block, :, : 2 * h])
    other[...] = terms[:, :h].astype(BF16)
    near_ref[...] = terms[:, h:]
    terms = dot(x[pl.ds(half, half)], w[block, :, h:])
    high = terms[:, h:].astype(BF16).astype(F32)
    lower = near_ref[...] + high
    upper = terms[:, :h] + other[...].astype(F32)
    below, above = arrived(s_ref, from_even, from_odd, 0, reach)
    h_ref[0] = gelu(lower[:reach] + below).astype(BF16)
    h_ref[1] = gelu(upper[reach:] + above).astype(BF16)
    near_ref[pl.ds(0, reach)] = lower[reach:]
    near_ref[pl.ds(reach, reach)] = upper[:reach]
    give_back(s_ref[0], hidden, reach, (ends[0], ends[1]), (core_ref,), 1)


def near_terms(scalars, x, hidden, ends, terms, w, reach):
    c, h = w.shape[1], w.shape[2] // 3
    rows = x.shape[0] // GROUP
    half = x.shape[0] // 2
    scratch = [pltpu.VMEM((half, h), BF16)]
    outs = (array(2, reach, h), array(half, h, dtype=F32), array(rows, h))
    return call(
        functools.partial(near_kernel, reach), outs, (scalars, x, hidden, ends, *terms, w),
        [SMEM] + [VMEM] * 6, (VMEM,) * 3, scratch, 4 * x.shape[0] * c * h, 4 * 2**20,
    )


def forward_kernel(*refs):
    out = refs[-1]
    for i in range((len(refs) - 1) // 2):
        out[2 * i] = refs[2 * i][...]
        out[2 * i + 1] = refs[2 * i + 1][1]


def forward(own, passing, after):
    operands = [v for pair in zip(own, passing) for v in pair]
    out = array(len(operands), *own[0].shape)
    return call(forward_kernel, out, operands, [VMEM] * len(operands), VMEM, [], 0, 4 * out.size, after=after)


def last_kernel(s_ref, outer, near, from_even, from_odd, g0, g1, g2, g3, hidden):
    q = s_ref[0]
    reach, h = outer.shape[1:]
    below, above = arrived(s_ref, from_even, from_odd, 0, reach)
    hidden[0] = outer[0]
    hidden[1] = gelu(near[pl.ds(0, reach)] + below).astype(BF16)
    hidden[2] = gelu(near[pl.ds(reach, reach)] + above).astype(BF16)
    hidden[3] = outer[1]
    for k, piece in enumerate((g0, g1, g2, g3)):
        piece[...] = hidden[q ^ k]


def last_hidden(scalars, outer, near, terms, after):
    half, h = near.shape
    return call(
        last_kernel, (array(half // 2, h),) * GROUP, (scalars, outer, near, *terms),
        [SMEM] + [VMEM] * 4, (VMEM,) * GROUP, [pltpu.VMEM((GROUP, half // 2, h), BF16)],
        20 * half * h, 2 * 2**20, after=after,
    )


def early_out_kernel(count, s_ref, x, *refs):
    own, far = refs[:count], refs[count : 2 * count]
    core, lasts, point = refs[2 * count], refs[2 * count + 1 : 2 * count + 3], refs[2 * count + 3]
    out, last, xs, ys, sems, osems = refs[-6:]
    q = s_ref[0]
    places, r, c = xs.shape[1:]
    rows = places * r
    here = pl.ds(pl.multiple_of(q * places, places), places)
    writes = []
    for b in range(count):
        writes.append(pltpu.make_async_copy(own[b].at[here], out.at[b, :, q], osems.at[b, 0]))
    start_all(writes)
    reads = start_all(
        [pltpu.make_async_copy(x.at[:, q ^ k], xs.at[k], sems.at[k]) for k in range(1, GROUP)]
    )

    def write(b, k, now):
        target = last if b + 1 == count else ys.at[min(b, count - 1)]
        target[k] = now.reshape(places, r, c)
        writes.append(pltpu.make_async_copy(target.at[k], out.at[b, :, q ^ k], osems.at[b, k]))
        writes[-1].start()

    for k in range(GROUP):
        if k == 0:
            now = own[count - 1][here].reshape(rows, c)
        else:
            reads[k - 1].wait()
            now = xs[k].reshape(rows, c)
            for b in range(count):
                hidden = (core[2 * b], far[b][0], core[2 * b + 1])[k - 1]
                now = (now.astype(F32) + dot(hidden, point[b])).astype(BF16)
                write(b, k, now)
        if k < 2:
            write(count, k, (now.astype(F32) + dot(lasts[k][...], point[count])).astype(BF16))
    wait_all(writes)


def early_outputs(scalars, x, own, far, core, lasts, point):
    blocks, h = point.shape[:2]
    places, group, r, c = x.shape
    count = blocks - 1
    own = [v.reshape(group * places, r, c) for v in own]
    operands = [scalars, x, *own, *far, core, *lasts, point]
    scratch = [
        pltpu.VMEM((group, places, r, c), BF16),
        pltpu.VMEM((count, group, places, r, c), BF16),
        pltpu.SemaphoreType.DMA((group,)),
        pltpu.SemaphoreType.DMA((blocks, group)),
    ]
    return call(
        functools.partial(early_out_kernel, count),
        (array(blocks, places, group, r, c), array(group, places, r, c)),
        operands, [SMEM, HBM] + [VMEM] * (len(operands) - 2), (HBM, VMEM), scratch,
        2 * blocks * x.size * h, 8 * 2**20,
    )


def late_out_kernel(s_ref, a2, a3, xs, point, _, out, ys, osems):
    q = s_ref[0]
    places, r, c = xs.shape[1:]
    last = out.shape[0] - 1
    writes = []
    for i, hidden in enumerate((a2, a3)):
        x = xs[2 + i].reshape(places * r, c).astype(F32) + dot(hidden[...], point[last])
        ys[i] = x.astype(BF16).reshape(places, r, c)
        writes.append(pltpu.make_async_copy(ys.at[i], out.at[last, :, q ^ (2 + i)], osems.at[i]))
        writes[-1].start()
    wait_all(writes)


def late_outputs(scalars, hiddens, xs, point, before):
    blocks, places, group, r, c = before.shape
    operands = (scalars, *hiddens, xs, point, before)
    scratch = [pltpu.VMEM((2, places, r, c), BF16), pltpu.SemaphoreType.DMA((2,))]
    return call(
        late_out_kernel, array(*before.shape), operands,
        [SMEM] + [VMEM] * 4 + [HBM], HBM, scratch,
        4 * places * r * c * point.shape[1], 2 * 2**20, {len(operands) - 1: 0},
    )


def neighbour_pairs(size, parity):
    groups = size // GROUP
    pairs = []
    for i in range(size):
        group = i // GROUP
        other = group + 1 if group % 2 == parity else group - 1
        pairs.append((i, i + (other - group) * GROUP if 0 <= other < groups else i ^ 1))
    return pairs


def by_residue(signal, taps, point):
    size = lax.axis_size("seq")
    me = lax.axis_index("seq")
    length, c = signal.shape
    places = length // FIRST_DILATION
    r = FIRST_DILATION // GROUP
    q, group = me % GROUP, me // GROUP
    scalars = jnp.stack(
        [q, group % 2, (group > 0).astype(jnp.int32), (group < size // GROUP - 1).astype(jnp.int32)]
    ).astype(jnp.int32)
    even_pairs, odd_pairs = neighbour_pairs(size, 0), neighbour_pairs(size, 1)
    x = signal.reshape(places, GROUP, r, c)

    def swap(value, k):
        return lax.ppermute(value, "seq", [(i, i ^ k) for i in range(size)])

    def back(pieces):
        return [pieces[0]] + [swap(pieces[k], k) for k in range(1, GROUP)]

    def across(even, odd):
        return lax.ppermute(even, "seq", even_pairs), lax.ppermute(odd, "seq", odd_pairs)

    mine, beside, over, rest = split(scalars, x)
    over, rest, beside = swap(over, 2), swap(rest, 3), swap(beside, 1)
    w = side_by_side(taps)
    early = early_taps(scalars, mine, beside, w)
    edge = swap(edge_part(over, r, early[:1]), 1)
    pieces = (mine, beside, over, edge)
    terms = across(*open_terms(scalars, pieces, w, r))
    early = more_taps(scalars, over, edge, w, early)
    current, even, odd, over, beside = first_block(scalars, rest, early, terms, w, point, r)
    terms = across(even, odd)
    own, core, far = [current], [beside], [swap(over, 2)]
    reach = 2 * r
    current, hidden, part = middle_block(1, scalars, current, w, point, reach)
    current, even, odd, over, beside = finish_edges(
        1, scalars, current, hidden, part, terms, w, point, reach, 2 * reach
    )
    terms = across(even, odd)
    own.append(current)
    core.append(beside)
    far.append(swap(over, 2))
    reach = 4 * r
    current, hidden, part, *inner = middle_block(2, scalars, current, w, point, reach, far[:1])
    inner = across(*inner)
    current, even, odd, over, ends = finish_edges(
        2, scalars, current, hidden, part, terms, w, point, reach, reach
    )
    terms = across(even, odd)
    own.append(current)
    far.append(swap(over, 2))
    outer, near, beside = near_terms(scalars, current, hidden, ends, inner, w, reach)
    core.append(beside)
    hidden = last_hidden(scalars, outer, near, terms, far[1:2])
    after = (hidden[0],)
    lasts = back(hidden)
    beside = swap(forward(core, far, after), 1)
    out, xs = early_outputs(scalars, x, own, far, beside, lasts[:2], point)
    out = late_outputs(scalars, lasts[2:], xs, point, out)
    return out.reshape(point.shape[0], length, c)


def passed_along(value, by):
    size = lax.axis_size("seq")
    pairs = [(i, i + by) for i in range(size) if 0 <= i + by < size]
    return lax.ppermute(value, "seq", pairs)


def by_neighbours(signal, taps, point):
    length = signal.shape[0]
    current = signal
    outputs = []
    for block in range(taps.shape[0]):
        step = FIRST_DILATION * 2**block
        low = dot(current, taps[block, 0]).astype(BF16)
        high = dot(current, taps[block, 2]).astype(BF16)
        if step < length:
            below = jnp.concatenate([passed_along(low[length - step :], 1), low[: length - step]])
            above = jnp.concatenate([high[step:], passed_along(high[:step], -1)])
        else:
            below = passed_along(low, step // length)
            above = passed_along(high, -(step // length))
        v = dot(current, taps[block, 1]) + below.astype(F32) + above.astype(F32)
        hidden = jax.nn.gelu(v, approximate=True).astype(BF16)
        current = (current.astype(F32) + dot(hidden, point[block])).astype(BF16)
        outputs.append(current)
    return jnp.stack(outputs)


def shards(signal, taps, point):
    fits = (
        taps.shape[0] == 4
        and signal.shape[0] == GROUP * FIRST_DILATION
        and lax.axis_size("seq") % GROUP == 0
    )
    return (by_residue if fits else by_neighbours)(signal, taps, point)


def solution(mesh):
    in_specs = (P(("grp", "seq"), None), P(), P())
    out_specs = P(None, ("grp", "seq"), None)
    return jax.shard_map(shards, mesh=mesh, in_specs=in_specs, out_specs=out_specs, check_vma=False)
```

```python
import functools

import jax
import jax.numpy as jnp
from jax import lax
from jax.experimental import pallas as pl
from jax.experimental.pallas import tpu as pltpu
from jax.sharding import PartitionSpec as P

FIRST_DILATION = 256
GROUP = 4
ROWS = 512
VMEM_LIMIT = 24 * 2**20

F32, BF16 = jnp.float32, jnp.bfloat16
ANY = pl.BlockSpec(memory_space=pl.ANY)
VMEM = pl.BlockSpec(memory_space=pltpu.VMEM)
SMEM = pl.BlockSpec(memory_space=pltpu.SMEM)
HBM = pl.BlockSpec(memory_space=pltpu.HBM)


def dot(a, b):
    return jnp.dot(a, b, preferred_element_type=F32)


def gelu(v):
    half = 0.5 * v
    inner = v * (0.7978845608028654 + 0.035677408136300125 * (v * v))
    return half + half * jnp.tanh(inner)


def over_rows(rows, body):
    for start in range(0, rows, ROWS):
        body(start, min(ROWS, rows - start))


def start_all(copies):
    for copy in copies:
        copy.start()
    return copies


def wait_all(copies):
    for copy in copies:
        copy.wait()


def call(kernel, outs, operands, specs, out_specs, scratch, flops, moved, aliases=None, after=()):
    count = len(operands)
    operands, specs = [*operands, *after], [*specs, *[ANY] * len(after)]
    body = kernel
    if after:
        kernel = lambda *refs: body(*refs[:count], *refs[count + len(after) :])
    return pl.pallas_call(
        kernel,
        out_shape=outs,
        in_specs=specs,
        out_specs=out_specs,
        scratch_shapes=scratch,
        input_output_aliases=aliases or {},
        compiler_params=pltpu.CompilerParams(vmem_limit_bytes=VMEM_LIMIT),
        cost_estimate=pl.CostEstimate(
            flops=int(flops), bytes_accessed=int(moved), transcendentals=0
        ),
    )(*operands)


def array(*shape, dtype=BF16):
    return jax.ShapeDtypeStruct(shape, dtype)


def split_kernel(s_ref, x, own, beside, over, last, rest, sems):
    q = s_ref[0]
    count = x.shape[0] - 1
    is_top = q == GROUP - 1

    def some(bottom, top, size):
        return pl.ds(jnp.where(is_top, top, bottom), size)

    copies = [
        pltpu.make_async_copy(source, target, sems.at[i])
        for i, (source, target) in enumerate(
            (
                (x.at[some(0, 1, count), q ^ 2], over.at[pl.ds(0, count)]),
                (x.at[some(0, count, 1), q ^ 3], over.at[pl.ds(count, 1)]),
                (x.at[some(1, 0, count), q ^ 3], rest),
                (x.at[some(count, 0, 1), q ^ 2], last),
                (x.at[:, q ^ 1], beside),
                (x.at[:, q], own),
            )
        )
    ]
    wait_all(start_all(copies))


def split(scalars, x):
    places, group, r, c = x.shape
    x = pltpu.with_memory_space_constraint(x, pltpu.HBM)
    outs = [array(n, r, c) for n in (places, places, places, 1, places - 1)]
    sems = [pltpu.SemaphoreType.DMA((6,))]
    pieces = call(split_kernel, outs, (scalars, x), [SMEM, HBM], (VMEM,) * 5, sems, 0, 4 * x.size)
    return [piece.reshape(piece.shape[0] * r, c) for piece in pieces]


def edge_part_kernel(over, out):
    out[...] = over[pl.ds(over.shape[0] - out.shape[0], out.shape[0])]


def edge_part(over, r, after):
    out = array(r, over.shape[1])
    return call(edge_part_kernel, out, (over,), [VMEM], VMEM, [], 0, 2 * out.size, after=after)


def side_by_side_kernel(taps, w, sems):
    h = taps.shape[3]
    wait_all(
        start_all(
            [
                pltpu.make_async_copy(
                    taps.at[b, t], w.at[b, :, pl.ds(t * h, h)], sems.at[b, t]
                )
                for b in range(taps.shape[0])
                for t in range(3)
            ]
        )
    )


def side_by_side(taps):
    blocks, count, c, h = taps.shape
    sems = [pltpu.SemaphoreType.DMA((blocks, count))]
    taps = pltpu.with_memory_space_constraint(taps, pltpu.HBM)
    return call(side_by_side_kernel, array(blocks, c, count * h), (taps,), [HBM], VMEM, sems, 0, 4 * taps.size)


def place_terms(parity, up, down, even_ref, odd_ref, start, size):
    even_ref[pl.ds(start, size)] = jnp.where(parity == 0, up, down).astype(BF16)
    odd_ref[pl.ds(start, size)] = jnp.where(parity == 0, down, up).astype(BF16)


def arrived(s_ref, from_even, from_odd, start, size):
    even = from_even[pl.ds(start, size)].astype(F32)
    odd = from_odd[pl.ds(start, size)].astype(F32)
    parity, has_lower, has_upper = s_ref[1], s_ref[2], s_ref[3]
    below = jnp.where(has_lower == 0, 0.0, jnp.where(parity == 0, odd, even))
    above = jnp.where(has_upper == 0, 0.0, jnp.where(parity == 0, even, odd))
    return below, above


def open_kernel(r, s_ref, own, beside, over, edge, w, even_ref, odd_ref, ends):
    q, parity = s_ref[0], s_ref[1]
    h = even_ref.shape[1]
    last = own.shape[0] - r

    def fetch(piece, at, to):
        ends[pl.ds(to, r)] = piece[pl.ds(at, r)]

    for k, (piece, top) in enumerate(((own, last), (beside, last), (over, last - r), (edge, 0))):
        pl.when(q ^ k == GROUP - 1)(functools.partial(fetch, piece, top, 0))
        pl.when(q ^ k == 0)(functools.partial(fetch, piece, 0, r))
    up = dot(ends[pl.ds(0, r)], w[0, :, :h])
    down = dot(ends[pl.ds(r, r)], w[0, :, 2 * h :])
    place_terms(parity, up, down, even_ref, odd_ref, 0, r)


def open_terms(scalars, pieces, w, r):
    c, h = w.shape[1], w.shape[2] // 3
    terms = array(r, h)
    return call(
        functools.partial(open_kernel, r), (terms, terms), (scalars, *pieces, w),
        [SMEM] + [VMEM] * (GROUP + 1), (VMEM, VMEM), [pltpu.VMEM((2 * r, c), BF16)],
        4 * r * c * h, 2**20,
    )


def keep_terms(at, terms, low, mid, high):
    h = mid.shape[1]
    low[at] = terms[:, :h].astype(BF16)
    mid[at] = terms[:, h : 2 * h]
    high[at] = terms[:, 2 * h :].astype(BF16)


def piece_taps(at, piece, w, x, low, mid, high):
    x[at] = piece
    keep_terms(at, dot(piece, w[0]), low, mid, high)


def part_rows(j, rows, size, bottom, top):
    return pl.ds(pl.multiple_of(j * rows + jnp.where(j == GROUP - 1, top, bottom), rows // GROUP), size)


def block_body(reach, x, point, x_ref, h_ref, part_ref, low, mid, high):
    length = x.shape[0]
    top = length - reach

    def body(start, size):
        at = reach + start
        v = mid[pl.ds(at, size)] + low[pl.ds(start, size)].astype(F32)
        hidden = gelu(v + high[pl.ds(at + reach, size)].astype(F32)).astype(BF16)
        h_ref[pl.ds(at, size)] = hidden
        x_ref[pl.ds(at, size)] = (x[pl.ds(at, size)].astype(F32) + dot(hidden, point)).astype(BF16)

    over_rows(length - 2 * reach, body)
    part_ref[pl.ds(0, reach)] = mid[pl.ds(0, reach)] + high[pl.ds(reach, reach)].astype(F32)
    part_ref[pl.ds(reach, reach)] = mid[pl.ds(top, reach)] + low[pl.ds(top - reach, reach)].astype(F32)
    for at in (0, top):
        x_ref[pl.ds(at, reach)] = x[pl.ds(at, reach)]
        h_ref[pl.ds(at, reach)] = jnp.zeros((reach, h_ref.shape[1]), BF16)


def early_taps_kernel(s_ref, own, beside, w, x, low, mid, high):
    rows = own.shape[0]
    for k, piece in enumerate((own, beside)):
        at = pl.ds(pl.multiple_of((s_ref[0] ^ k) * rows, rows), rows)
        piece_taps(at, piece[...], w, x, low, mid, high)


def early_taps(scalars, own, beside, w):
    c, h = w.shape[1], w.shape[2] // 3
    rows = own.shape[0]
    length = GROUP * rows
    outs = (array(length, c), array(length, h), array(length, h, dtype=F32), array(length, h))
    return call(
        early_taps_kernel, outs, (scalars, own, beside, w), [SMEM] + [VMEM] * 3, (VMEM,) * 4, [],
        12 * rows * c * h, 2**20,
    )


def more_taps_kernel(s_ref, over, edge, w, *refs):
    x, low, mid, high = refs[4:]
    q = s_ref[0]
    rows, r = x.shape[0] // GROUP, edge.shape[0]
    size = rows - r
    piece_taps(part_rows(q ^ 2, rows, size, 0, r), over[pl.ds(0, size)], w, x, low, mid, high)
    piece_taps(part_rows(q ^ 3, rows, r, 0, size), edge[...], w, x, low, mid, high)


def more_taps(scalars, over, edge, w, early):
    c, h = w.shape[1], w.shape[2] // 3
    return call(
        more_taps_kernel, tuple(array(*e.shape, dtype=e.dtype) for e in early),
        (scalars, over, edge, w, *early), [SMEM] + [VMEM] * 7, (VMEM,) * 4, [],
        6 * over.shape[0] * c * h, 2**20, {4: 0, 5: 1, 6: 2, 7: 3},
    )


def first_kernel(
    r, s_ref, rest, last, x, low, mid, high, from_even, from_odd, w, point,
    x_ref, even_ref, odd_ref, far_ref, core_ref, *refs
):
    hidden = refs[-1]
    q, parity = s_ref[0], s_ref[1]
    length = x.shape[0]
    rows = length // GROUP
    h = mid.shape[1]
    size = rows - r
    piece_taps(part_rows(q ^ 3, rows, size, r, 0), rest[...], w, x, low, mid, high)
    piece_taps(part_rows(q ^ 2, rows, r, size, 0), last[...], w, x, low, mid, high)
    below, above = arrived(s_ref, from_even, from_odd, 0, r)

    def finish(start, size, v):
        at = pl.ds(start, size)
        hidden[at] = gelu(v).astype(BF16)
        x_ref[at] = (x[at].astype(F32) + dot(hidden[at], point[0])).astype(BF16)

    def body(start, size):
        v = mid[pl.ds(start, size)]
        if start == 0:
            low_terms = jnp.concatenate([below, low[pl.ds(0, size - r)].astype(F32)])
        else:
            low_terms = low[pl.ds(start - r, size)].astype(F32)
        if start + size == length:
            high_terms = jnp.concatenate([high[pl.ds(start + r, size - r)].astype(F32), above])
        else:
            high_terms = high[pl.ds(start + r, size)].astype(F32)
        finish(start, size, v + low_terms + high_terms)

    over_rows(length, body)
    ahead = even_ref.shape[0]
    up = dot(x_ref[pl.ds(length - ahead, ahead)], w[1, :, :h])
    down = dot(x_ref[pl.ds(0, ahead)], w[1, :, 2 * h :])
    place_terms(parity, up, down, even_ref, odd_ref, 0, ahead)
    for k, ref in ((1, core_ref), (2, far_ref.at[0]), (3, far_ref.at[1])):
        ref[...] = hidden[pl.ds(pl.multiple_of((q ^ k) * rows, rows), rows)]


def first_block(scalars, rests, early, terms, w, point, r):
    c, h = w.shape[1], w.shape[2] // 3
    length = early[0].shape[0]
    rows = length // GROUP
    outs = (array(length, c), array(2 * r, h), array(2 * r, h), array(2, rows, h), array(rows, h))
    outs += tuple(array(*e.shape, dtype=e.dtype) for e in early)
    results = call(
        functools.partial(first_kernel, r), outs, (scalars, *rests, *early, *terms, w, point),
        [SMEM] + [VMEM] * 10, (VMEM,) * 9, [pltpu.VMEM((length, h), BF16)],
        8 * length * c * h, 4 * 2**20, {3: 5, 4: 6, 5: 7, 6: 8},
    )
    return results[:5]


def middle_kernel(block, reach, parity_ref, x, w, point, x_ref, h_ref, part_ref, *refs):
    sent, (low, mid, high) = refs[:-3], refs[-3:]
    h = mid.shape[1]

    length = x.shape[0]
    bottom, top = pl.ds(0, reach), pl.ds(length - reach, reach)
    terms = dot(x[bottom], w[block, :, : 2 * h])
    low[bottom] = terms[:, :h].astype(BF16)
    mid[bottom] = terms[:, h:]

    def body(start, size):
        at = pl.ds(reach + start, size)
        keep_terms(at, dot(x[at], w[block]), low, mid, high)

    over_rows(length - 2 * reach, body)
    terms = dot(x[top], w[block, :, h:])
    mid[top] = terms[:, :h]
    high[top] = terms[:, h:].astype(BF16)
    block_body(reach, x, point[block], x_ref, h_ref, part_ref, low, mid, high)
    if sent:
        middle = x.shape[0] // 2
        up = dot(x_ref[pl.ds(middle, reach)], w[block + 1, :, :h])
        down = dot(x_ref[pl.ds(middle - reach, reach)], w[block + 1, :, 2 * h :])
        place_terms(parity_ref[1], up, down, *sent, 0, reach)


def middle_block(block, scalars, x, w, point, reach, after=()):
    c, h = w.shape[1], w.shape[2] // 3
    length = x.shape[0]
    outs = (array(length, c), array(length, h), array(2 * reach, h, dtype=F32))
    if block + 2 == w.shape[0]:
        outs += (array(reach, h),) * 2
    scratch = [
        pltpu.VMEM((length, h), BF16),
        pltpu.VMEM((length, h), F32),
        pltpu.VMEM((length, h), BF16),
    ]
    return call(
        functools.partial(middle_kernel, block, reach), outs, (scalars, x, w, point),
        [SMEM] + [VMEM] * 3, (VMEM,) * len(outs), scratch, 8 * length * c * h, 4 * 2**20, after=after,
    )


def give_back(q, hidden, reach, edges, refs, first):
    rows = hidden.shape[0] // GROUP
    for i, ref in enumerate(refs):
        j = q ^ (first + i)
        ref[...] = hidden[pl.ds(pl.multiple_of(j * rows, rows), rows)]

        @pl.when(j == 0)
        def _(ref=ref):
            ref[pl.ds(0, reach)] = edges[0]

        @pl.when(j == GROUP - 1)
        def _(ref=ref):
            ref[pl.ds(rows - reach, reach)] = edges[1]


def edge_kernel(
    block, reach, ahead, s_ref, x, hidden, part, from_even, from_odd, w, point,
    x_ref, even_ref, odd_ref, far_ref, *refs
):
    q, parity = s_ref[0], s_ref[1]
    length = x.shape[0]
    h = hidden.shape[1]
    rows = length // GROUP
    below, above = arrived(s_ref, from_even, from_odd, 0, reach)
    edges = (
        gelu(part[pl.ds(0, reach)] + below).astype(BF16),
        gelu(part[pl.ds(reach, reach)] + above).astype(BF16),
    )
    more = dot(jnp.concatenate(edges), point[block])
    for i, at in enumerate((0, length - reach)):
        new = x[pl.ds(at, reach)].astype(F32) + more[i * reach : (i + 1) * reach]
        x_ref[pl.ds(at, reach)] = new.astype(BF16)
    up = dot(x_ref[pl.ds(length - ahead, ahead)], w[block + 1, :, :h])
    down = dot(x_ref[pl.ds(0, ahead)], w[block + 1, :, 2 * h :])
    place_terms(parity, up, down, even_ref, odd_ref, 0, ahead)
    give_back(q, hidden, reach, edges, (far_ref.at[0], far_ref.at[1]), 2)
    if block + 2 < w.shape[0]:
        give_back(q, hidden, reach, edges, refs, 1)
    else:
        refs[0][0] = edges[0]
        refs[0][1] = edges[1]


def finish_edges(block, scalars, x, hidden, part, terms, w, point, reach, ahead, after=()):
    c, h = w.shape[1], w.shape[2] // 3
    rows = x.shape[0] // GROUP
    outs = (array(*x.shape),) + (array(ahead, h),) * 2 + (array(2, rows, h),)
    outs += (array(2, reach, h),) if block + 2 == w.shape[0] else (array(rows, h),)
    return call(
        functools.partial(edge_kernel, block, reach, ahead), outs,
        (scalars, x, hidden, part, *terms, w, point),
        [SMEM] + [VMEM] * 7, (VMEM,) * len(outs), [],
        2 * c * h * (2 * reach + 2 * ahead), 4 * 2**20, {1: 0}, after,
    )


def near_kernel(reach, s_ref, x, hidden, ends, from_even, from_odd, w, h_ref, near_ref, core_ref, other):
    length = x.shape[0]
    half = length // 2
    h = near_ref.shape[1]
    block = w.shape[0] - 1
    terms = dot(x[pl.ds(0, half)], w[block, :, : 2 * h])
    other[...] = terms[:, :h].astype(BF16)
    near_ref[...] = terms[:, h:]
    terms = dot(x[pl.ds(half, half)], w[block, :, h:])
    high = terms[:, h:].astype(BF16).astype(F32)
    lower = near_ref[...] + high
    upper = terms[:, :h] + other[...].astype(F32)
    below, above = arrived(s_ref, from_even, from_odd, 0, reach)
    h_ref[0] = gelu(lower[:reach] + below).astype(BF16)
    h_ref[1] = gelu(upper[reach:] + above).astype(BF16)
    near_ref[pl.ds(0, reach)] = lower[reach:]
    near_ref[pl.ds(reach, reach)] = upper[:reach]
    give_back(s_ref[0], hidden, reach, (ends[0], ends[1]), (core_ref,), 1)


def near_terms(scalars, x, hidden, ends, terms, w, reach):
    c, h = w.shape[1], w.shape[2] // 3
    rows = x.shape[0] // GROUP
    half = x.shape[0] // 2
    scratch = [pltpu.VMEM((half, h), BF16)]
    outs = (array(2, reach, h), array(half, h, dtype=F32), array(rows, h))
    return call(
        functools.partial(near_kernel, reach), outs, (scalars, x, hidden, ends, *terms, w),
        [SMEM] + [VMEM] * 6, (VMEM,) * 3, scratch, 2.4e9, 4 * 2**20,
    )


def forward_kernel(count, *refs):
    out = refs[-1]
    for i, ref in enumerate(refs[:-1]):
        out[i] = ref[...] if i < count else ref[1]


def forward(own, passing):
    out = array(len(own) + len(passing), *own[0].shape)
    operands = (*own, *passing)
    return call(
        functools.partial(forward_kernel, len(own)), out, operands, [VMEM] * len(operands), VMEM, [],
        0, 4 * out.size,
    )


def last_kernel(s_ref, outer, near, from_even, from_odd, g0, g1, g2, g3, hidden):
    q = s_ref[0]
    reach, h = outer.shape[1:]
    below, above = arrived(s_ref, from_even, from_odd, 0, reach)
    hidden[0] = outer[0]
    hidden[1] = gelu(near[pl.ds(0, reach)] + below).astype(BF16)
    hidden[2] = gelu(near[pl.ds(reach, reach)] + above).astype(BF16)
    hidden[3] = outer[1]
    for k, piece in enumerate((g0, g1, g2, g3)):
        piece[...] = hidden[q ^ k]


def last_hidden(scalars, outer, near, terms, after):
    half, h = near.shape
    return call(
        last_kernel, (array(half // 2, h),) * GROUP, (scalars, outer, near, *terms),
        [SMEM] + [VMEM] * 4, (VMEM,) * GROUP, [pltpu.VMEM((GROUP, half // 2, h), BF16)],
        20 * half * h, 2 * 2**20, after=after,
    )


def add_blocks(x, hiddens, point, keep):
    for b, hidden in enumerate(hiddens):
        x = (x.astype(F32) + dot(hidden, point[b])).astype(BF16)
        keep(b, x)
    return x


def chip_out_kernel(count, s_ref, x, *refs):
    own, far, refs = refs[:count], refs[count : 2 * count], refs[2 * count :]
    mine, point, out, kept, xs, ys, sem, osems = refs
    q = s_ref[0]
    places, r, c = xs.shape
    rows = places * r
    here = pl.ds(pl.multiple_of(q * places, places), places)
    read = pltpu.make_async_copy(x.at[:, q ^ 2], xs, sem)
    read.start()
    writes = start_all(
        [
            pltpu.make_async_copy(own[b].at[here], out.at[b, :, q], osems.at[0, b])
            for b in range(count)
        ]
    )

    def write(k, b, value):
        ys[b] = value.reshape(places, r, c)
        writes.append(pltpu.make_async_copy(ys.at[b], out.at[b, :, q ^ k], osems.at[k // 2, b]))
        writes[-1].start()

    now = own[count - 1][here].reshape(rows, c).astype(F32) + dot(mine[...], point[count])
    write(0, count, now.astype(BF16))
    read.wait()
    hiddens = [far[b][0] for b in range(count)]
    now = add_blocks(xs[...].reshape(rows, c), hiddens, point, functools.partial(write, 2))
    kept[...] = now
    wait_all(writes)


def chip_outputs(scalars, x, own, far, mine, point, flops):
    places, group, r, c = x.shape
    blocks = point.shape[0]
    own = [v.reshape(group * places, r, c) for v in own]
    operands = (scalars, x, *own, *far, mine, point)
    scratch = [
        pltpu.VMEM((places, r, c), BF16),
        pltpu.VMEM((blocks, places, r, c), BF16),
        pltpu.SemaphoreType.DMA,
        pltpu.SemaphoreType.DMA((2, blocks)),
    ]
    return call(
        functools.partial(chip_out_kernel, blocks - 1),
        (array(blocks, places, group, r, c), array(places * r, c)),
        operands, [SMEM, HBM] + [VMEM] * (len(operands) - 2), (HBM, VMEM), scratch, flops, 8 * 2**20,
    )


def core_out_kernel(count, s_ref, x, core, point, _, out, kept, xs, ys, sems, osems):
    q = s_ref[0]
    places, r, c = xs.shape[1:]
    rows = places * r
    reads = start_all(
        [pltpu.make_async_copy(x.at[:, q ^ k], xs.at[i], sems.at[i]) for i, k in enumerate((1, 3))]
    )
    writes = []

    def write(i, k, b, value):
        ys[i, b] = value.reshape(places, r, c)
        writes.append(pltpu.make_async_copy(ys.at[i, b], out.at[b, :, q ^ k], osems.at[i, b]))
        writes[-1].start()

    for i, k in enumerate((1, 3)):
        reads[i].wait()
        hiddens = [core[(count + 1) * i + b] for b in range(count + 1 - i)]
        now = add_blocks(xs[i].reshape(rows, c), hiddens, point, functools.partial(write, i, k))
    kept[...] = now
    wait_all(writes)


def core_outputs(scalars, x, core, point, before):
    places, group, r, c = x.shape
    blocks, h = point.shape[:2]
    operands = (scalars, x, core, point, before)
    scratch = [
        pltpu.VMEM((2, places, r, c), BF16),
        pltpu.VMEM((2, blocks, places, r, c), BF16),
        pltpu.SemaphoreType.DMA((2,)),
        pltpu.SemaphoreType.DMA((2, blocks)),
    ]
    return call(
        functools.partial(core_out_kernel, blocks - 1),
        (array(*before.shape), array(places * r, c)),
        operands, [SMEM, HBM, VMEM, VMEM, HBM], (HBM, VMEM), scratch,
        blocks * x.size * h, 4 * 2**20, {4: 0},
    )


def late_out_kernel(s_ref, a2, a3, x2, x3, point, _, out, ys, osems):
    q = s_ref[0]
    places, r, c = ys.shape[1:]
    last = out.shape[0] - 1
    writes = []
    for i, (hidden, x) in enumerate(((a2, x2), (a3, x3))):
        value = x[...].astype(F32) + dot(hidden[...], point[last])
        ys[i] = value.astype(BF16).reshape(places, r, c)
        writes.append(pltpu.make_async_copy(ys.at[i], out.at[last, :, q ^ (2 + i)], osems.at[i]))
        writes[-1].start()
    wait_all(writes)


def late_outputs(scalars, hiddens, xs, point, before):
    blocks, places, group, r, c = before.shape
    operands = (scalars, *hiddens, *xs, point, before)
    scratch = [pltpu.VMEM((2, places, r, c), BF16), pltpu.SemaphoreType.DMA((2,))]
    return call(
        late_out_kernel, array(*before.shape), operands,
        [SMEM] + [VMEM] * 5 + [HBM], HBM, scratch,
        4 * places * r * c * point.shape[1], 2 * 2**20, {len(operands) - 1: 0},
    )


def neighbour_pairs(size, parity):
    groups = size // GROUP
    pairs = []
    for i in range(size):
        group = i // GROUP
        other = group + 1 if group % 2 == parity else group - 1
        pairs.append((i, i + (other - group) * GROUP if 0 <= other < groups else i ^ 1))
    return pairs


def by_residue(signal, taps, point):
    size = lax.axis_size("seq")
    me = lax.axis_index("seq")
    length, c = signal.shape
    places = length // FIRST_DILATION
    r = FIRST_DILATION // GROUP
    q, group = me % GROUP, me // GROUP
    scalars = jnp.stack(
        [q, group % 2, (group > 0).astype(jnp.int32), (group < size // GROUP - 1).astype(jnp.int32)]
    ).astype(jnp.int32)
    even_pairs, odd_pairs = neighbour_pairs(size, 0), neighbour_pairs(size, 1)
    x = signal.reshape(places, GROUP, r, c)

    def swap(value, k):
        return lax.ppermute(value, "seq", [(i, i ^ k) for i in range(size)])

    def across(even, odd):
        return lax.ppermute(even, "seq", even_pairs), lax.ppermute(odd, "seq", odd_pairs)

    mine, beside, over, last, rest = split(scalars, x)
    over, rest, last, beside = swap(over, 2), swap(rest, 3), swap(last, 2), swap(beside, 1)
    w = side_by_side(taps)
    early = early_taps(scalars, mine, beside, w)
    edge = swap(edge_part(over, r, early[:1]), 1)
    pieces = (mine, beside, over, edge)
    terms = across(*open_terms(scalars, pieces, w, r))
    early = more_taps(scalars, over, edge, w, early)
    current, even, odd, over, beside = first_block(scalars, (rest, last), early, terms, w, point, r)
    terms = across(even, odd)
    own, core, far = [current], [beside], [swap(over, 2)]
    reach = 2 * r
    current, hidden, part = middle_block(1, scalars, current, w, point, reach)
    current, even, odd, over, beside = finish_edges(
        1, scalars, current, hidden, part, terms, w, point, reach, 2 * reach
    )
    terms = across(even, odd)
    own.append(current)
    core.append(beside)
    far.append(swap(over, 2))
    reach = 4 * r
    current, hidden, part, *inner = middle_block(2, scalars, current, w, point, reach, far[:1])
    inner = across(*inner)
    current, even, odd, over, ends = finish_edges(
        2, scalars, current, hidden, part, terms, w, point, reach, reach
    )
    terms = across(even, odd)
    own.append(current)
    far.append(swap(over, 2))
    outer, near, beside = near_terms(scalars, current, hidden, ends, inner, w, reach)
    core.append(beside)
    hidden = last_hidden(scalars, outer, near, terms, far[1:2])
    lasts = [swap(hidden[k], k) for k in (2, 3)]
    beside = swap(forward([*core, hidden[1]], far), 1)
    out, x2 = chip_outputs(scalars, x, own, far, hidden[0], point, 5e10)
    out, x3 = core_outputs(scalars, x, beside, point, out)
    out = late_outputs(scalars, lasts, (x2, x3), point, out)
    return out.reshape(point.shape[0], length, c)


def passed_along(value, by):
    size = lax.axis_size("seq")
    pairs = [(i, i + by) for i in range(size) if 0 <= i + by < size]
    return lax.ppermute(value, "seq", pairs)


def by_neighbours(signal, taps, point):
    length = signal.shape[0]
    current = signal
    outputs = []
    for block in range(taps.shape[0]):
        step = FIRST_DILATION * 2**block
        low = dot(current, taps[block, 0]).astype(BF16)
        high = dot(current, taps[block, 2]).astype(BF16)
        if step < length:
            below = jnp.concatenate([passed_along(low[length - step :], 1), low[: length - step]])
            above = jnp.concatenate([high[step:], passed_along(high[:step], -1)])
        else:
            below = passed_along(low, step // length)
            above = passed_along(high, -(step // length))
        v = dot(current, taps[block, 1]) + below.astype(F32) + above.astype(F32)
        hidden = jax.nn.gelu(v, approximate=True).astype(BF16)
        current = (current.astype(F32) + dot(hidden, point[block])).astype(BF16)
        outputs.append(current)
    return jnp.stack(outputs)


def shards(signal, taps, point):
    fits = (
        taps.shape[0] == 4
        and signal.shape[0] == GROUP * FIRST_DILATION
        and lax.axis_size("seq") % GROUP == 0
    )
    return (by_residue if fits else by_neighbours)(signal, taps, point)


def solution(mesh):
    in_specs = (P(("grp", "seq"), None), P(), P())
    out_specs = P(None, ("grp", "seq"), None)
    return jax.shard_map(shards, mesh=mesh, in_specs=in_specs, out_specs=out_specs, check_vma=False)
```

```python
import functools

import jax
import jax.numpy as jnp
from jax import lax
from jax.experimental import pallas as pl
from jax.experimental.pallas import tpu as pltpu
from jax.sharding import PartitionSpec as P

FIRST_DILATION = 256
GROUP = 4
ROWS = 512
VMEM_LIMIT = 24 * 2**20
NEAR_WORK, CHIP_WORK = 2.4e9, 5e10

F32, BF16 = jnp.float32, jnp.bfloat16
ANY = pl.BlockSpec(memory_space=pl.ANY)
VMEM = pl.BlockSpec(memory_space=pltpu.VMEM)
SMEM = pl.BlockSpec(memory_space=pltpu.SMEM)
HBM = pl.BlockSpec(memory_space=pltpu.HBM)


def dot(a, b):
    return jnp.dot(a, b, preferred_element_type=F32)


def gelu(v):
    half = 0.5 * v
    inner = v * (0.7978845608028654 + 0.035677408136300125 * (v * v))
    return half + half * jnp.tanh(inner)


def over_rows(rows, body):
    for start in range(0, rows, ROWS):
        body(start, min(ROWS, rows - start))


def start_all(copies):
    for copy in copies:
        copy.start()
    return copies


def wait_all(copies):
    for copy in copies:
        copy.wait()


def call(kernel, outs, operands, specs, out_specs, scratch, flops, moved, aliases=None, after=()):
    count = len(operands)
    operands, specs = [*operands, *after], [*specs, *[ANY] * len(after)]
    body = kernel
    if after:
        kernel = lambda *refs: body(*refs[:count], *refs[count + len(after) :])
    return pl.pallas_call(
        kernel,
        out_shape=outs,
        in_specs=specs,
        out_specs=out_specs,
        scratch_shapes=scratch,
        input_output_aliases=aliases or {},
        compiler_params=pltpu.CompilerParams(vmem_limit_bytes=VMEM_LIMIT),
        cost_estimate=pl.CostEstimate(
            flops=int(flops), bytes_accessed=int(moved), transcendentals=0
        ),
    )(*operands)


def array(*shape, dtype=BF16):
    return jax.ShapeDtypeStruct(shape, dtype)


def split_kernel(s_ref, x, own, beside, over, last, rest, sems):
    q = s_ref[0]
    count = x.shape[0] - 1
    is_top = q == GROUP - 1

    def some(bottom, top, size):
        return pl.ds(jnp.where(is_top, top, bottom), size)

    copies = [
        pltpu.make_async_copy(source, target, sems.at[i])
        for i, (source, target) in enumerate(
            (
                (x.at[some(0, 1, count), q ^ 2], over.at[pl.ds(0, count)]),
                (x.at[some(0, count, 1), q ^ 3], over.at[pl.ds(count, 1)]),
                (x.at[some(1, 0, count), q ^ 3], rest),
                (x.at[some(count, 0, 1), q ^ 2], last),
                (x.at[:, q ^ 1], beside),
                (x.at[:, q], own),
            )
        )
    ]
    wait_all(start_all(copies))


def split(scalars, x):
    places, group, r, c = x.shape
    x = pltpu.with_memory_space_constraint(x, pltpu.HBM)
    outs = [array(n, r, c) for n in (places, places, places, 1, places - 1)]
    sems = [pltpu.SemaphoreType.DMA((6,))]
    pieces = call(split_kernel, outs, (scalars, x), [SMEM, HBM], (VMEM,) * 5, sems, 0, 4 * x.size)
    return [piece.reshape(piece.shape[0] * r, c) for piece in pieces]


def edge_part_kernel(over, out):
    out[...] = over[pl.ds(over.shape[0] - out.shape[0], out.shape[0])]


def edge_part(over, r, after):
    out = array(r, over.shape[1])
    return call(edge_part_kernel, out, (over,), [VMEM], VMEM, [], 0, 2 * out.size, after=after)


def side_by_side_kernel(taps, w, sems):
    h = taps.shape[3]
    wait_all(
        start_all(
            [
                pltpu.make_async_copy(
                    taps.at[b, t], w.at[b, :, pl.ds(t * h, h)], sems.at[b, t]
                )
                for b in range(taps.shape[0])
                for t in range(3)
            ]
        )
    )


def side_by_side(taps):
    blocks, count, c, h = taps.shape
    sems = [pltpu.SemaphoreType.DMA((blocks, count))]
    taps = pltpu.with_memory_space_constraint(taps, pltpu.HBM)
    return call(side_by_side_kernel, array(blocks, c, count * h), (taps,), [HBM], VMEM, sems, 0, 4 * taps.size)


def place_terms(parity, up, down, even_ref, odd_ref, start, size):
    even_ref[pl.ds(start, size)] = jnp.where(parity == 0, up, down).astype(BF16)
    odd_ref[pl.ds(start, size)] = jnp.where(parity == 0, down, up).astype(BF16)


def arrived(s_ref, from_even, from_odd, start, size):
    even = from_even[pl.ds(start, size)].astype(F32)
    odd = from_odd[pl.ds(start, size)].astype(F32)
    parity, has_lower, has_upper = s_ref[1], s_ref[2], s_ref[3]
    below = jnp.where(has_lower == 0, 0.0, jnp.where(parity == 0, odd, even))
    above = jnp.where(has_upper == 0, 0.0, jnp.where(parity == 0, even, odd))
    return below, above


def open_kernel(r, s_ref, own, beside, over, edge, w, even_ref, odd_ref, ends):
    q, parity = s_ref[0], s_ref[1]
    h = even_ref.shape[1]
    last = own.shape[0] - r

    def fetch(piece, at, to):
        ends[pl.ds(to, r)] = piece[pl.ds(at, r)]

    for k, (piece, top) in enumerate(((own, last), (beside, last), (over, last - r), (edge, 0))):
        pl.when(q ^ k == GROUP - 1)(functools.partial(fetch, piece, top, 0))
        pl.when(q ^ k == 0)(functools.partial(fetch, piece, 0, r))
    up = dot(ends[pl.ds(0, r)], w[0, :, :h])
    down = dot(ends[pl.ds(r, r)], w[0, :, 2 * h :])
    place_terms(parity, up, down, even_ref, odd_ref, 0, r)


def open_terms(scalars, pieces, w, r):
    c, h = w.shape[1], w.shape[2] // 3
    terms = array(r, h)
    return call(
        functools.partial(open_kernel, r), (terms, terms), (scalars, *pieces, w),
        [SMEM] + [VMEM] * (GROUP + 1), (VMEM, VMEM), [pltpu.VMEM((2 * r, c), BF16)],
        4 * r * c * h, 2**20,
    )


def keep_terms(at, terms, low, mid, high, low_at=None):
    h = mid.shape[1]
    low[at if low_at is None else low_at] = terms[:, :h].astype(BF16)
    mid[at] = terms[:, h : 2 * h]
    high[at] = terms[:, 2 * h :].astype(BF16)


def piece_taps(starts, r, pieces, w, x, low, mid, high):
    terms = dot(jnp.concatenate(pieces), w[0])
    done = 0
    for start, piece in zip(starts, pieces):
        size = piece.shape[0]
        at, low_at = pl.ds(start, size), pl.ds(pl.multiple_of(start + r, r), size)
        x[at] = piece
        keep_terms(at, terms[done : done + size], low, mid, high, low_at)
        done += size


def first_finish(starts, sizes, r, point, x, low, mid, high, x_ref, hidden):
    values = []
    for start, size in zip(starts, sizes):
        at, after = pl.ds(start, size), pl.ds(pl.multiple_of(start + r, r), size)
        v = mid[at] + low[at].astype(F32) + high[after].astype(F32)
        values.append(gelu(v).astype(BF16))
        hidden[at] = values[-1]
    more = dot(jnp.concatenate(values), point[0])
    done = 0
    for start, size in zip(starts, sizes):
        at = pl.ds(start, size)
        x_ref[at] = (x[at].astype(F32) + more[done : done + size]).astype(BF16)
        done += size


def part_start(j, rows, bottom, top, r):
    return pl.multiple_of(j * rows + jnp.where(j == GROUP - 1, top, bottom), r)


def block_body(reach, x, point, x_ref, h_ref, part_ref, low, mid, high):
    length = x.shape[0]
    top = length - reach

    def body(start, size):
        at = reach + start
        v = mid[pl.ds(at, size)] + low[pl.ds(start, size)].astype(F32)
        hidden = gelu(v + high[pl.ds(at + reach, size)].astype(F32)).astype(BF16)
        h_ref[pl.ds(at, size)] = hidden
        x_ref[pl.ds(at, size)] = (x[pl.ds(at, size)].astype(F32) + dot(hidden, point)).astype(BF16)

    over_rows(length - 2 * reach, body)
    part_ref[pl.ds(0, reach)] = mid[pl.ds(0, reach)] + high[pl.ds(reach, reach)].astype(F32)
    part_ref[pl.ds(reach, reach)] = mid[pl.ds(top, reach)] + low[pl.ds(top - reach, reach)].astype(F32)
    for at in (0, top):
        x_ref[pl.ds(at, reach)] = x[pl.ds(at, reach)]
        h_ref[pl.ds(at, reach)] = jnp.zeros((reach, h_ref.shape[1]), BF16)


def early_taps_kernel(r, s_ref, own, beside, w, point, x, low, mid, high, x_ref, hidden):
    q = s_ref[0]
    rows = own.shape[0]
    starts = [pl.multiple_of((q ^ k) * rows, rows) for k in range(2)]
    piece_taps(starts, r, (own[...], beside[...]), w, x, low, mid, high)
    half = jnp.where(q < GROUP // 2, 0, GROUP // 2) * rows
    start = pl.multiple_of(half + r, r)
    first_finish((start,), (2 * rows - 2 * r,), r, point, x, low, mid, high, x_ref, hidden)


def early_taps(scalars, own, beside, w, point, r):
    c, h = w.shape[1], w.shape[2] // 3
    rows = own.shape[0]
    length = GROUP * rows
    outs = (array(length, c), array(length + r, h), array(length, h, dtype=F32))
    outs += (array(length + r, h), array(length, c), array(length, h))
    return call(
        functools.partial(early_taps_kernel, r), outs, (scalars, own, beside, w, point),
        [SMEM] + [VMEM] * 4, (VMEM,) * 6, [],
        12 * rows * c * h, 2**20,
    )


def more_taps_kernel(s_ref, over, edge, w, *refs):
    x, low, mid, high = refs[4:]
    q = s_ref[0]
    rows, r = x.shape[0] // GROUP, edge.shape[0]
    size = rows - r
    starts = (part_start(q ^ 2, rows, 0, r, r), part_start(q ^ 3, rows, 0, size, r))
    piece_taps(starts, r, (over[pl.ds(0, size)], edge[...]), w, x, low, mid, high)


def more_taps(scalars, over, edge, w, early):
    c, h = w.shape[1], w.shape[2] // 3
    return call(
        more_taps_kernel, tuple(array(*e.shape, dtype=e.dtype) for e in early),
        (scalars, over, edge, w, *early), [SMEM] + [VMEM] * 7, (VMEM,) * 4, [],
        6 * over.shape[0] * c * h, 2**20, {4: 0, 5: 1, 6: 2, 7: 3},
    )


def first_kernel(
    r, s_ref, rest, last, x, low, mid, high, x_in, hidden_in, from_even, from_odd, w, point,
    even_ref, odd_ref, far_ref, core_ref, *refs
):
    x_ref, hidden = refs[-2:]
    q, parity = s_ref[0], s_ref[1]
    length = x.shape[0]
    rows = length // GROUP
    h = mid.shape[1]
    size = rows - r
    starts = (part_start(q ^ 3, rows, r, 0, r), part_start(q ^ 2, rows, size, 0, r))
    piece_taps(starts, r, (rest[...], last[...]), w, x, low, mid, high)
    below, above = arrived(s_ref, from_even, from_odd, 0, r)
    low[pl.ds(0, r)] = below.astype(BF16)
    high[pl.ds(length, r)] = above.astype(BF16)
    is_low = q < GROUP // 2
    alone = pl.multiple_of(jnp.where(is_low, 0, length - r), r)
    others = pl.multiple_of(jnp.where(is_low, 2 * rows - r, 0), r)
    first_finish((alone, others), (r, 2 * rows + r), r, point, x, low, mid, high, x_ref, hidden)
    ahead = even_ref.shape[0]
    up = dot(x_ref[pl.ds(length - ahead, ahead)], w[1, :, :h])
    down = dot(x_ref[pl.ds(0, ahead)], w[1, :, 2 * h :])
    place_terms(parity, up, down, even_ref, odd_ref, 0, ahead)
    for k, ref in ((1, core_ref), (2, far_ref.at[0]), (3, far_ref.at[1])):
        ref[...] = hidden[pl.ds(pl.multiple_of((q ^ k) * rows, rows), rows)]


def first_block(scalars, rests, early, terms, w, point, r):
    c, h = w.shape[1], w.shape[2] // 3
    length = early[0].shape[0]
    rows = length // GROUP
    outs = (array(2 * r, h), array(2 * r, h), array(2, rows, h), array(rows, h))
    outs += tuple(array(*e.shape, dtype=e.dtype) for e in early)
    results = call(
        functools.partial(first_kernel, r), outs, (scalars, *rests, *early, *terms, w, point),
        [SMEM] + [VMEM] * 12, (VMEM,) * 10, [],
        8 * length * c * h, 4 * 2**20, {3 + i: 4 + i for i in range(6)},
    )
    return results[8], *results[:4]


def middle_kernel(block, reach, parity_ref, x, w, point, x_ref, h_ref, part_ref, *refs):
    sent, (low, mid, high) = refs[:-3], refs[-3:]
    h = mid.shape[1]

    length = x.shape[0]
    bottom, top = pl.ds(0, reach), pl.ds(length - reach, reach)
    terms = dot(x[bottom], w[block, :, : 2 * h])
    low[bottom] = terms[:, :h].astype(BF16)
    mid[bottom] = terms[:, h:]

    def body(start, size):
        at = pl.ds(reach + start, size)
        keep_terms(at, dot(x[at], w[block]), low, mid, high)

    over_rows(length - 2 * reach, body)
    terms = dot(x[top], w[block, :, h:])
    mid[top] = terms[:, :h]
    high[top] = terms[:, h:].astype(BF16)
    block_body(reach, x, point[block], x_ref, h_ref, part_ref, low, mid, high)
    if sent:
        middle = x.shape[0] // 2
        up = dot(x_ref[pl.ds(middle, reach)], w[block + 1, :, :h])
        down = dot(x_ref[pl.ds(middle - reach, reach)], w[block + 1, :, 2 * h :])
        place_terms(parity_ref[1], up, down, *sent, 0, reach)


def middle_block(block, scalars, x, w, point, reach, after=()):
    c, h = w.shape[1], w.shape[2] // 3
    length = x.shape[0]
    outs = (array(length, c), array(length, h), array(2 * reach, h, dtype=F32))
    if block + 2 == w.shape[0]:
        outs += (array(reach, h),) * 2
    scratch = [
        pltpu.VMEM((length, h), BF16),
        pltpu.VMEM((length, h), F32),
        pltpu.VMEM((length, h), BF16),
    ]
    return call(
        functools.partial(middle_kernel, block, reach), outs, (scalars, x, w, point),
        [SMEM] + [VMEM] * 3, (VMEM,) * len(outs), scratch, 8 * length * c * h, 4 * 2**20, after=after,
    )


def give_back(q, hidden, reach, edges, refs, first):
    rows = hidden.shape[0] // GROUP
    for i, ref in enumerate(refs):
        j = q ^ (first + i)
        ref[...] = hidden[pl.ds(pl.multiple_of(j * rows, rows), rows)]

        @pl.when(j == 0)
        def _(ref=ref):
            ref[pl.ds(0, reach)] = edges[0]

        @pl.when(j == GROUP - 1)
        def _(ref=ref):
            ref[pl.ds(rows - reach, reach)] = edges[1]


def edge_kernel(
    block, reach, ahead, s_ref, x, hidden, part, from_even, from_odd, w, point,
    x_ref, even_ref, odd_ref, far_ref, *refs
):
    q, parity = s_ref[0], s_ref[1]
    length = x.shape[0]
    h = hidden.shape[1]
    rows = length // GROUP
    below, above = arrived(s_ref, from_even, from_odd, 0, reach)
    edges = (
        gelu(part[pl.ds(0, reach)] + below).astype(BF16),
        gelu(part[pl.ds(reach, reach)] + above).astype(BF16),
    )
    more = dot(jnp.concatenate(edges), point[block])
    for i, at in enumerate((0, length - reach)):
        new = x[pl.ds(at, reach)].astype(F32) + more[i * reach : (i + 1) * reach]
        x_ref[pl.ds(at, reach)] = new.astype(BF16)
    up = dot(x_ref[pl.ds(length - ahead, ahead)], w[block + 1, :, :h])
    down = dot(x_ref[pl.ds(0, ahead)], w[block + 1, :, 2 * h :])
    place_terms(parity, up, down, even_ref, odd_ref, 0, ahead)
    give_back(q, hidden, reach, edges, (far_ref.at[0], far_ref.at[1]), 2)
    if block + 2 < w.shape[0]:
        give_back(q, hidden, reach, edges, refs, 1)
    else:
        refs[0][0] = edges[0]
        refs[0][1] = edges[1]


def finish_edges(block, scalars, x, hidden, part, terms, w, point, reach, ahead, after=()):
    c, h = w.shape[1], w.shape[2] // 3
    rows = x.shape[0] // GROUP
    outs = (array(*x.shape),) + (array(ahead, h),) * 2 + (array(2, rows, h),)
    outs += (array(2, reach, h),) if block + 2 == w.shape[0] else (array(rows, h),)
    return call(
        functools.partial(edge_kernel, block, reach, ahead), outs,
        (scalars, x, hidden, part, *terms, w, point),
        [SMEM] + [VMEM] * 7, (VMEM,) * len(outs), [],
        2 * c * h * (2 * reach + 2 * ahead), 4 * 2**20, {1: 0}, after,
    )


def near_kernel(
    reach, s_ref, x, hidden, ends, from_even, from_odd, w, signal, h_ref, near_ref, core_ref, xs_ref, other, sems
):
    length = x.shape[0]
    reads = start_all(
        [
            pltpu.make_async_copy(signal.at[:, s_ref[0] ^ k], xs_ref.at[k - 1], sems.at[k])
            for k in range(1, GROUP)
        ]
    )
    half = length // 2
    h = near_ref.shape[1]
    block = w.shape[0] - 1
    terms = dot(x[pl.ds(0, half)], w[block, :, : 2 * h])
    other[...] = terms[:, :h].astype(BF16)
    near_ref[...] = terms[:, h:]
    terms = dot(x[pl.ds(half, half)], w[block, :, h:])
    high = terms[:, h:].astype(BF16).astype(F32)
    lower = near_ref[...] + high
    upper = terms[:, :h] + other[...].astype(F32)
    below, above = arrived(s_ref, from_even, from_odd, 0, reach)
    h_ref[0] = gelu(lower[:reach] + below).astype(BF16)
    h_ref[1] = gelu(upper[reach:] + above).astype(BF16)
    near_ref[pl.ds(0, reach)] = lower[reach:]
    near_ref[pl.ds(reach, reach)] = upper[:reach]
    give_back(s_ref[0], hidden, reach, (ends[0], ends[1]), (core_ref,), 1)
    wait_all(reads)


def near_terms(scalars, x, hidden, ends, terms, w, signal, reach):
    c, h = w.shape[1], w.shape[2] // 3
    rows = x.shape[0] // GROUP
    half = x.shape[0] // 2
    scratch = [pltpu.VMEM((half, h), BF16), pltpu.SemaphoreType.DMA((GROUP,))]
    outs = (array(2, reach, h), array(half, h, dtype=F32), array(rows, h))
    places, _, r, _ = signal.shape
    outs += (array(GROUP - 1, places, r, c),)
    signal = pltpu.with_memory_space_constraint(signal, pltpu.HBM)
    return call(
        functools.partial(near_kernel, reach), outs, (scalars, x, hidden, ends, *terms, w, signal),
        [SMEM] + [VMEM] * 6 + [HBM], (VMEM,) * 4, scratch, NEAR_WORK, 4 * 2**20,
    )


def forward_kernel(count, *refs):
    out = refs[-1]
    for i, ref in enumerate(refs[:-1]):
        out[i] = ref[...] if i < count else ref[1]


def forward(own, passing):
    out = array(len(own) + len(passing), *own[0].shape)
    operands = (*own, *passing)
    return call(
        functools.partial(forward_kernel, len(own)), out, operands, [VMEM] * len(operands), VMEM, [],
        0, 4 * out.size,
    )


def last_kernel(s_ref, outer, near, from_even, from_odd, g0, g1, g2, g3, hidden):
    q = s_ref[0]
    reach, h = outer.shape[1:]
    below, above = arrived(s_ref, from_even, from_odd, 0, reach)
    hidden[0] = outer[0]
    hidden[1] = gelu(near[pl.ds(0, reach)] + below).astype(BF16)
    hidden[2] = gelu(near[pl.ds(reach, reach)] + above).astype(BF16)
    hidden[3] = outer[1]
    for k, piece in enumerate((g0, g1, g2, g3)):
        piece[...] = hidden[q ^ k]


def last_hidden(scalars, outer, near, terms, after):
    half, h = near.shape
    return call(
        last_kernel, (array(half // 2, h),) * GROUP, (scalars, outer, near, *terms),
        [SMEM] + [VMEM] * 4, (VMEM,) * GROUP, [pltpu.VMEM((GROUP, half // 2, h), BF16)],
        20 * half * h, 2 * 2**20, after=after,
    )


def add_blocks(x, hiddens, point, keep):
    for b, hidden in enumerate(hiddens):
        x = (x.astype(F32) + dot(hidden, point[b])).astype(BF16)
        keep(b, x)
    return x


def chip_out_kernel(count, s_ref, x, *refs):
    own, far, refs = refs[:count], refs[count : 2 * count], refs[2 * count :]
    mine, point, out, kept, ys, osems = refs
    q = s_ref[0]
    places, r, c = x.shape[1:]
    rows = places * r
    here = pl.ds(pl.multiple_of(q * places, places), places)
    writes = start_all(
        [
            pltpu.make_async_copy(own[b].at[here], out.at[b, :, q], osems.at[0, b])
            for b in range(count)
        ]
    )

    def write(k, b, value):
        ys[b] = value.reshape(places, r, c)
        writes.append(pltpu.make_async_copy(ys.at[b], out.at[b, :, q ^ k], osems.at[k // 2, b]))
        writes[-1].start()

    now = own[count - 1][here].reshape(rows, c).astype(F32) + dot(mine[...], point[count])
    write(0, count, now.astype(BF16))
    hiddens = [far[b][0] for b in range(count)]
    now = add_blocks(x[1].reshape(rows, c), hiddens, point, functools.partial(write, 2))
    kept[...] = now
    wait_all(writes)


def chip_outputs(scalars, x, own, far, mine, point):
    places, r, c = x.shape[1:]
    group, blocks = GROUP, point.shape[0]
    own = [v.reshape(group * places, r, c) for v in own]
    operands = (scalars, x, *own, *far, mine, point)
    scratch = [
        pltpu.VMEM((blocks, places, r, c), BF16),
        pltpu.SemaphoreType.DMA((2, blocks)),
    ]
    return call(
        functools.partial(chip_out_kernel, blocks - 1),
        (array(blocks, places, group, r, c), array(places * r, c)),
        operands, [SMEM] + [VMEM] * (len(operands) - 1), (HBM, VMEM), scratch, CHIP_WORK, 8 * 2**20,
    )


def core_out_kernel(count, s_ref, x, core, point, _, out, kept, ys, osems):
    q = s_ref[0]
    places, r, c = x.shape[1:]
    rows = places * r
    writes = []

    def write(i, k, b, value):
        ys[i, b] = value.reshape(places, r, c)
        writes.append(pltpu.make_async_copy(ys.at[i, b], out.at[b, :, q ^ k], osems.at[i, b]))
        writes[-1].start()

    for i, k in enumerate((1, 3)):
        hiddens = [core[(count + 1) * i + b] for b in range(count + 1 - i)]
        now = add_blocks(x[2 * i].reshape(rows, c), hiddens, point, functools.partial(write, i, k))
    kept[...] = now
    wait_all(writes)


def core_outputs(scalars, x, core, point, before):
    blocks, places, group, r, c = before.shape
    h = point.shape[1]
    operands = (scalars, x, core, point, before)
    scratch = [
        pltpu.VMEM((2, blocks, places, r, c), BF16),
        pltpu.SemaphoreType.DMA((2, blocks)),
    ]
    return call(
        functools.partial(core_out_kernel, blocks - 1),
        (array(*before.shape), array(places * r, c)),
        operands, [SMEM] + [VMEM] * 3 + [HBM], (HBM, VMEM), scratch,
        blocks * x.size * h, 4 * 2**20, {4: 0},
    )


def late_out_kernel(s_ref, x2, x3, point, _, a2, a3, out, ys, sems):
    places, r, c = ys.shape[1:]
    last = out.shape[0] - 1
    writes = []
    for i, (x, hidden) in enumerate(((x2, a2), (x3, a3))):
        value = x[...].astype(F32) + dot(hidden[...], point[last])
        ys[i] = value.astype(BF16).reshape(places, r, c)
        writes.append(pltpu.make_async_copy(ys.at[i], out.at[last, :, s_ref[0] ^ (2 + i)], sems.at[i]))
        writes[-1].start()
    wait_all(writes)


def late_outputs(scalars, hiddens, xs, point, before):
    blocks, places, group, r, c = before.shape
    operands = (scalars, *xs, point, before, *hiddens)
    scratch = [pltpu.VMEM((2, places, r, c), BF16), pltpu.SemaphoreType.DMA((2,))]
    return call(
        late_out_kernel, array(*before.shape), operands,
        [SMEM] + [VMEM] * 3 + [HBM] + [VMEM] * 2, HBM, scratch,
        4 * places * r * c * point.shape[1], 2 * 2**20, {4: 0},
    )


def neighbour_pairs(size, parity):
    groups = size // GROUP
    pairs = []
    for i in range(size):
        group = i // GROUP
        other = group + 1 if group % 2 == parity else group - 1
        pairs.append((i, i + (other - group) * GROUP if 0 <= other < groups else i ^ 1))
    return pairs


def by_residue(signal, taps, point):
    size = lax.axis_size("seq")
    me = lax.axis_index("seq")
    length, c = signal.shape
    places = length // FIRST_DILATION
    r = FIRST_DILATION // GROUP
    q, group = me % GROUP, me // GROUP
    scalars = jnp.stack(
        [q, group % 2, (group > 0).astype(jnp.int32), (group < size // GROUP - 1).astype(jnp.int32)]
    ).astype(jnp.int32)
    even_pairs, odd_pairs = neighbour_pairs(size, 0), neighbour_pairs(size, 1)
    x = signal.reshape(places, GROUP, r, c)

    def swap(value, k):
        return lax.ppermute(value, "seq", [(i, i ^ k) for i in range(size)])

    def across(even, odd):
        return lax.ppermute(even, "seq", even_pairs), lax.ppermute(odd, "seq", odd_pairs)

    mine, beside, over, last, rest = split(scalars, x)
    over, rest, last, beside = swap(over, 2), swap(rest, 3), swap(last, 2), swap(beside, 1)
    w = side_by_side(taps)
    early, ready = early_taps(scalars, mine, beside, w, point, r), ()
    early, ready = early[:4], early[4:]
    edge = swap(edge_part(over, r, early[:1]), 1)
    pieces = (mine, beside, over, edge)
    terms = across(*open_terms(scalars, pieces, w, r))
    early = more_taps(scalars, over, edge, w, early)
    current, even, odd, over, beside = first_block(scalars, (rest, last), (*early, *ready), terms, w, point, r)
    terms = across(even, odd)
    own, core, far = [current], [beside], [swap(over, 2)]
    reach = 2 * r
    current, hidden, part = middle_block(1, scalars, current, w, point, reach)
    current, even, odd, over, beside = finish_edges(
        1, scalars, current, hidden, part, terms, w, point, reach, 2 * reach
    )
    terms = across(even, odd)
    own.append(current)
    core.append(beside)
    far.append(swap(over, 2))
    reach = 4 * r
    current, hidden, part, *inner = middle_block(2, scalars, current, w, point, reach, far[:1])
    inner = across(*inner)
    current, even, odd, over, ends = finish_edges(
        2, scalars, current, hidden, part, terms, w, point, reach, reach
    )
    terms = across(even, odd)
    own.append(current)
    far.append(swap(over, 2))
    outer, near, beside, xs = near_terms(scalars, current, hidden, ends, inner, w, x, reach)
    core.append(beside)
    hidden = last_hidden(scalars, outer, near, terms, far[1:2])
    lasts = [swap(hidden[k], k) for k in (2, 3)]
    beside = swap(forward([*core, hidden[1]], far), 1)
    out, x2 = chip_outputs(scalars, xs, own, far, hidden[0], point)
    out, x3 = core_outputs(scalars, xs, beside, point, out)
    out = late_outputs(scalars, lasts, (x2, x3), point, out)
    return out.reshape(point.shape[0], length, c)


def passed_along(value, by):
    size = lax.axis_size("seq")
    pairs = [(i, i + by) for i in range(size) if 0 <= i + by < size]
    return lax.ppermute(value, "seq", pairs)


def by_neighbours(signal, taps, point):
    length = signal.shape[0]
    current = signal
    outputs = []
    for block in range(taps.shape[0]):
        step = FIRST_DILATION * 2**block
        low = dot(current, taps[block, 0]).astype(BF16)
        high = dot(current, taps[block, 2]).astype(BF16)
        if step < length:
            below = jnp.concatenate([passed_along(low[length - step :], 1), low[: length - step]])
            above = jnp.concatenate([high[step:], passed_along(high[:step], -1)])
        else:
            below = passed_along(low, step // length)
            above = passed_along(high, -(step // length))
        v = dot(current, taps[block, 1]) + below.astype(F32) + above.astype(F32)
        hidden = jax.nn.gelu(v, approximate=True).astype(BF16)
        current = (current.astype(F32) + dot(hidden, point[block])).astype(BF16)
        outputs.append(current)
    return jnp.stack(outputs)


def shards(signal, taps, point):
    fits = (
        taps.shape[0] == 4
        and signal.shape[0] == GROUP * FIRST_DILATION
        and lax.axis_size("seq") % GROUP == 0
    )
    return (by_residue if fits else by_neighbours)(signal, taps, point)


def solution(mesh):
    in_specs = (P(("grp", "seq"), None), P(), P())
    out_specs = P(None, ("grp", "seq"), None)
    return jax.shard_map(shards, mesh=mesh, in_specs=in_specs, out_specs=out_specs, check_vma=False)
```

```python
import functools

import jax
import jax.numpy as jnp
from jax import lax
from jax.experimental import pallas as pl
from jax.experimental.pallas import tpu as pltpu
from jax.sharding import PartitionSpec as P

FIRST_DILATION = 256
GROUP = 4
ROWS = 512
VMEM_LIMIT = 24 * 2**20
NEAR_WORK, CHIP_WORK = 2.4e9, 5e10

F32, BF16 = jnp.float32, jnp.bfloat16
ANY = pl.BlockSpec(memory_space=pl.ANY)
VMEM = pl.BlockSpec(memory_space=pltpu.VMEM)
SMEM = pl.BlockSpec(memory_space=pltpu.SMEM)
HBM = pl.BlockSpec(memory_space=pltpu.HBM)


def dot(a, b):
    return jnp.dot(a, b, preferred_element_type=F32)


def gelu(v):
    half = 0.5 * v
    inner = v * (0.7978845608028654 + 0.035677408136300125 * (v * v))
    return half + half * jnp.tanh(inner)


def over_rows(rows, body):
    for start in range(0, rows, ROWS):
        body(start, min(ROWS, rows - start))


def start_all(copies):
    for copy in copies:
        copy.start()
    return copies


def wait_all(copies):
    for copy in copies:
        copy.wait()


def call(kernel, outs, operands, specs, out_specs, scratch, flops, moved, aliases=None, after=()):
    count = len(operands)
    operands, specs = [*operands, *after], [*specs, *[ANY] * len(after)]
    body = kernel
    if after:
        kernel = lambda *refs: body(*refs[:count], *refs[count + len(after) :])
    return pl.pallas_call(
        kernel,
        out_shape=outs,
        in_specs=specs,
        out_specs=out_specs,
        scratch_shapes=scratch,
        input_output_aliases=aliases or {},
        compiler_params=pltpu.CompilerParams(vmem_limit_bytes=VMEM_LIMIT),
        cost_estimate=pl.CostEstimate(
            flops=int(flops), bytes_accessed=int(moved), transcendentals=0
        ),
    )(*operands)


def array(*shape, dtype=BF16):
    return jax.ShapeDtypeStruct(shape, dtype)


def split_kernel(s_ref, x, own, beside, over, last, rest, sems):
    q = s_ref[0]
    count = x.shape[0] - 1
    is_top = q == GROUP - 1

    def some(bottom, top, size):
        return pl.ds(jnp.where(is_top, top, bottom), size)

    copies = [
        pltpu.make_async_copy(source, target, sems.at[i])
        for i, (source, target) in enumerate(
            (
                (x.at[some(0, 1, count), q ^ 2], over.at[pl.ds(0, count)]),
                (x.at[some(0, count, 1), q ^ 3], over.at[pl.ds(count, 1)]),
                (x.at[some(1, 0, count), q ^ 3], rest),
                (x.at[some(count, 0, 1), q ^ 2], last),
                (x.at[:, q ^ 1], beside),
                (x.at[:, q], own),
            )
        )
    ]
    wait_all(start_all(copies))


def split(scalars, x):
    places, group, r, c = x.shape
    x = pltpu.with_memory_space_constraint(x, pltpu.HBM)
    outs = [array(n, r, c) for n in (places, places, places, 1, places - 1)]
    sems = [pltpu.SemaphoreType.DMA((6,))]
    pieces = call(split_kernel, outs, (scalars, x), [SMEM, HBM], (VMEM,) * 5, sems, 0, 4 * x.size)
    return [piece.reshape(piece.shape[0] * r, c) for piece in pieces]


def edge_part_kernel(over, out):
    out[...] = over[pl.ds(over.shape[0] - out.shape[0], out.shape[0])]


def edge_part(over, r, after):
    out = array(r, over.shape[1])
    return call(edge_part_kernel, out, (over,), [VMEM], VMEM, [], 0, 2 * out.size, after=after)


def side_by_side_kernel(taps, w, sems):
    h = taps.shape[3]
    wait_all(
        start_all(
            [
                pltpu.make_async_copy(
                    taps.at[b, t], w.at[b, :, pl.ds(t * h, h)], sems.at[b, t]
                )
                for b in range(taps.shape[0])
                for t in range(3)
            ]
        )
    )


def side_by_side(taps):
    blocks, count, c, h = taps.shape
    sems = [pltpu.SemaphoreType.DMA((blocks, count))]
    taps = pltpu.with_memory_space_constraint(taps, pltpu.HBM)
    return call(side_by_side_kernel, array(blocks, c, count * h), (taps,), [HBM], VMEM, sems, 0, 4 * taps.size)


def place_terms(parity, up, down, even_ref, odd_ref, start, size):
    even_ref[pl.ds(start, size)] = jnp.where(parity == 0, up, down).astype(BF16)
    odd_ref[pl.ds(start, size)] = jnp.where(parity == 0, down, up).astype(BF16)


def arrived(s_ref, from_even, from_odd, start, size):
    even = from_even[pl.ds(start, size)].astype(F32)
    odd = from_odd[pl.ds(start, size)].astype(F32)
    parity, has_lower, has_upper = s_ref[1], s_ref[2], s_ref[3]
    below = jnp.where(has_lower == 0, 0.0, jnp.where(parity == 0, odd, even))
    above = jnp.where(has_upper == 0, 0.0, jnp.where(parity == 0, even, odd))
    return below, above


def open_kernel(r, s_ref, own, beside, over, edge, w, even_ref, odd_ref, ends):
    q, parity = s_ref[0], s_ref[1]
    h = even_ref.shape[1]
    last = own.shape[0] - r

    def fetch(piece, at, to):
        ends[pl.ds(to, r)] = piece[pl.ds(at, r)]

    for k, (piece, top) in enumerate(((own, last), (beside, last), (over, last - r), (edge, 0))):
        pl.when(q ^ k == GROUP - 1)(functools.partial(fetch, piece, top, 0))
        pl.when(q ^ k == 0)(functools.partial(fetch, piece, 0, r))
    up = dot(ends[pl.ds(0, r)], w[0, :, :h])
    down = dot(ends[pl.ds(r, r)], w[0, :, 2 * h :])
    place_terms(parity, up, down, even_ref, odd_ref, 0, r)


def open_terms(scalars, pieces, w, r):
    c, h = w.shape[1], w.shape[2] // 3
    terms = array(r, h)
    return call(
        functools.partial(open_kernel, r), (terms, terms), (scalars, *pieces, w),
        [SMEM] + [VMEM] * (GROUP + 1), (VMEM, VMEM), [pltpu.VMEM((2 * r, c), BF16)],
        4 * r * c * h, 2**20,
    )


def keep_terms(at, terms, low, mid, high, low_at=None):
    h = mid.shape[1]
    low[at if low_at is None else low_at] = terms[:, :h].astype(BF16)
    mid[at] = terms[:, h : 2 * h]
    high[at] = terms[:, 2 * h :].astype(BF16)


def piece_taps(starts, r, pieces, w, x, low, mid, high):
    terms = dot(jnp.concatenate(pieces), w[0])
    done = 0
    for start, piece in zip(starts, pieces):
        size = piece.shape[0]
        at, low_at = pl.ds(start, size), pl.ds(pl.multiple_of(start + r, r), size)
        x[at] = piece
        keep_terms(at, terms[done : done + size], low, mid, high, low_at)
        done += size


def first_finish(starts, sizes, r, point, x, low, mid, high, x_ref, hidden):
    values = []
    for start, size in zip(starts, sizes):
        at, after = pl.ds(start, size), pl.ds(pl.multiple_of(start + r, r), size)
        v = mid[at] + low[at].astype(F32) + high[after].astype(F32)
        values.append(gelu(v).astype(BF16))
        hidden[at] = values[-1]
    more = dot(jnp.concatenate(values), point[0])
    done = 0
    for start, size in zip(starts, sizes):
        at = pl.ds(start, size)
        x_ref[at] = (x[at].astype(F32) + more[done : done + size]).astype(BF16)
        done += size


def part_start(j, rows, bottom, top, r):
    return pl.multiple_of(j * rows + jnp.where(j == GROUP - 1, top, bottom), r)


def block_body(reach, x, point, x_ref, h_ref, part_ref, low, mid, high):
    length = x.shape[0]
    top = length - reach

    def body(start, size):
        at = reach + start
        v = mid[pl.ds(at, size)] + low[pl.ds(start, size)].astype(F32)
        hidden = gelu(v + high[pl.ds(at + reach, size)].astype(F32)).astype(BF16)
        h_ref[pl.ds(at, size)] = hidden
        x_ref[pl.ds(at, size)] = (x[pl.ds(at, size)].astype(F32) + dot(hidden, point)).astype(BF16)

    over_rows(length - 2 * reach, body)
    part_ref[pl.ds(0, reach)] = mid[pl.ds(0, reach)] + high[pl.ds(reach, reach)].astype(F32)
    part_ref[pl.ds(reach, reach)] = mid[pl.ds(top, reach)] + low[pl.ds(top - reach, reach)].astype(F32)
    for at in (0, top):
        x_ref[pl.ds(at, reach)] = x[pl.ds(at, reach)]
        h_ref[pl.ds(at, reach)] = jnp.zeros((reach, h_ref.shape[1]), BF16)


def early_taps_kernel(
    r, s_ref, own, beside, w, point, signal, x, low, mid, high, x_ref, hidden, xs_ref, sems
):
    q = s_ref[0]
    reads = start_all(
        [
            pltpu.make_async_copy(signal.at[:, q ^ k], xs_ref.at[k - 1], sems.at[k])
            for k in range(1, GROUP)
        ]
    )
    rows = own.shape[0]
    starts = [pl.multiple_of((q ^ k) * rows, rows) for k in range(2)]
    piece_taps(starts, r, (own[...], beside[...]), w, x, low, mid, high)
    half = jnp.where(q < GROUP // 2, 0, GROUP // 2) * rows
    start = pl.multiple_of(half + r, r)
    first_finish((start,), (2 * rows - 2 * r,), r, point, x, low, mid, high, x_ref, hidden)
    wait_all(reads)


def early_taps(scalars, own, beside, w, point, signal):
    c, h = w.shape[1], w.shape[2] // 3
    rows = own.shape[0]
    length = GROUP * rows
    places, _, r, _ = signal.shape
    signal = pltpu.with_memory_space_constraint(signal, pltpu.HBM)
    outs = (array(length, c), array(length + r, h), array(length, h, dtype=F32))
    outs += (array(length + r, h), array(length, c), array(length, h))
    outs += (array(GROUP - 1, places, r, c),)
    return call(
        functools.partial(early_taps_kernel, r), outs, (scalars, own, beside, w, point, signal),
        [SMEM] + [VMEM] * 4 + [HBM], (VMEM,) * 7, [pltpu.SemaphoreType.DMA((GROUP,))],
        12 * rows * c * h, 2**20,
    )


def more_taps_kernel(s_ref, over, edge, w, *refs):
    x, low, mid, high = refs[4:]
    q = s_ref[0]
    rows, r = x.shape[0] // GROUP, edge.shape[0]
    size = rows - r
    starts = (part_start(q ^ 2, rows, 0, r, r), part_start(q ^ 3, rows, 0, size, r))
    piece_taps(starts, r, (over[pl.ds(0, size)], edge[...]), w, x, low, mid, high)


def more_taps(scalars, over, edge, w, early):
    c, h = w.shape[1], w.shape[2] // 3
    return call(
        more_taps_kernel, tuple(array(*e.shape, dtype=e.dtype) for e in early),
        (scalars, over, edge, w, *early), [SMEM] + [VMEM] * 7, (VMEM,) * 4, [],
        6 * over.shape[0] * c * h, 2**20, {4: 0, 5: 1, 6: 2, 7: 3},
    )


def first_kernel(
    r, s_ref, rest, last, x, low, mid, high, x_in, hidden_in, from_even, from_odd, w, point,
    even_ref, odd_ref, far_ref, core_ref, *refs
):
    x_ref, hidden = refs[-2:]
    q, parity = s_ref[0], s_ref[1]
    length = x.shape[0]
    rows = length // GROUP
    h = mid.shape[1]
    size = rows - r
    starts = (part_start(q ^ 3, rows, r, 0, r), part_start(q ^ 2, rows, size, 0, r))
    piece_taps(starts, r, (rest[...], last[...]), w, x, low, mid, high)
    below, above = arrived(s_ref, from_even, from_odd, 0, r)
    low[pl.ds(0, r)] = below.astype(BF16)
    high[pl.ds(length, r)] = above.astype(BF16)
    is_low = q < GROUP // 2
    alone = pl.multiple_of(jnp.where(is_low, 0, length - r), r)
    others = pl.multiple_of(jnp.where(is_low, 2 * rows - r, 0), r)
    first_finish((alone, others), (r, 2 * rows + r), r, point, x, low, mid, high, x_ref, hidden)
    ahead = even_ref.shape[0]
    up = dot(x_ref[pl.ds(length - ahead, ahead)], w[1, :, :h])
    down = dot(x_ref[pl.ds(0, ahead)], w[1, :, 2 * h :])
    place_terms(parity, up, down, even_ref, odd_ref, 0, ahead)
    for k, ref in ((1, core_ref), (2, far_ref.at[0]), (3, far_ref.at[1])):
        ref[...] = hidden[pl.ds(pl.multiple_of((q ^ k) * rows, rows), rows)]


def first_block(scalars, rests, early, terms, w, point, r):
    c, h = w.shape[1], w.shape[2] // 3
    length = early[0].shape[0]
    rows = length // GROUP
    outs = (array(2 * r, h), array(2 * r, h), array(2, rows, h), array(rows, h))
    outs += tuple(array(*e.shape, dtype=e.dtype) for e in early)
    results = call(
        functools.partial(first_kernel, r), outs, (scalars, *rests, *early, *terms, w, point),
        [SMEM] + [VMEM] * 12, (VMEM,) * 10, [],
        8 * length * c * h, 4 * 2**20, {3 + i: 4 + i for i in range(6)},
    )
    return results[8], *results[:4]


def middle_kernel(block, reach, parity_ref, x, w, point, x_ref, h_ref, part_ref, *refs):
    sent, (low, mid, high) = refs[:-3], refs[-3:]
    h = mid.shape[1]

    length = x.shape[0]
    bottom, top = pl.ds(0, reach), pl.ds(length - reach, reach)
    terms = dot(x[bottom], w[block, :, : 2 * h])
    low[bottom] = terms[:, :h].astype(BF16)
    mid[bottom] = terms[:, h:]

    def body(start, size):
        at = pl.ds(reach + start, size)
        keep_terms(at, dot(x[at], w[block]), low, mid, high)

    over_rows(length - 2 * reach, body)
    terms = dot(x[top], w[block, :, h:])
    mid[top] = terms[:, :h]
    high[top] = terms[:, h:].astype(BF16)
    block_body(reach, x, point[block], x_ref, h_ref, part_ref, low, mid, high)
    if sent:
        middle = x.shape[0] // 2
        up = dot(x_ref[pl.ds(middle, reach)], w[block + 1, :, :h])
        down = dot(x_ref[pl.ds(middle - reach, reach)], w[block + 1, :, 2 * h :])
        place_terms(parity_ref[1], up, down, *sent, 0, reach)


def middle_block(block, scalars, x, w, point, reach, after=()):
    c, h = w.shape[1], w.shape[2] // 3
    length = x.shape[0]
    outs = (array(length, c), array(length, h), array(2 * reach, h, dtype=F32))
    if block + 2 == w.shape[0]:
        outs += (array(reach, h),) * 2
    scratch = [
        pltpu.VMEM((length, h), BF16),
        pltpu.VMEM((length, h), F32),
        pltpu.VMEM((length, h), BF16),
    ]
    return call(
        functools.partial(middle_kernel, block, reach), outs, (scalars, x, w, point),
        [SMEM] + [VMEM] * 3, (VMEM,) * len(outs), scratch, 8 * length * c * h, 4 * 2**20, after=after,
    )


def give_back(q, hidden, reach, edges, refs, first):
    rows = hidden.shape[0] // GROUP
    for i, ref in enumerate(refs):
        j = q ^ (first + i)
        ref[...] = hidden[pl.ds(pl.multiple_of(j * rows, rows), rows)]

        @pl.when(j == 0)
        def _(ref=ref):
            ref[pl.ds(0, reach)] = edges[0]

        @pl.when(j == GROUP - 1)
        def _(ref=ref):
            ref[pl.ds(rows - reach, reach)] = edges[1]


def edge_kernel(
    block, reach, ahead, s_ref, x, hidden, part, from_even, from_odd, w, point,
    x_ref, even_ref, odd_ref, far_ref, *refs
):
    q, parity = s_ref[0], s_ref[1]
    length = x.shape[0]
    h = hidden.shape[1]
    rows = length // GROUP
    below, above = arrived(s_ref, from_even, from_odd, 0, reach)
    edges = (
        gelu(part[pl.ds(0, reach)] + below).astype(BF16),
        gelu(part[pl.ds(reach, reach)] + above).astype(BF16),
    )
    more = dot(jnp.concatenate(edges), point[block])
    for i, at in enumerate((0, length - reach)):
        new = x[pl.ds(at, reach)].astype(F32) + more[i * reach : (i + 1) * reach]
        x_ref[pl.ds(at, reach)] = new.astype(BF16)
    up = dot(x_ref[pl.ds(length - ahead, ahead)], w[block + 1, :, :h])
    down = dot(x_ref[pl.ds(0, ahead)], w[block + 1, :, 2 * h :])
    place_terms(parity, up, down, even_ref, odd_ref, 0, ahead)
    give_back(q, hidden, reach, edges, (far_ref.at[0], far_ref.at[1]), 2)
    if block + 2 < w.shape[0]:
        give_back(q, hidden, reach, edges, refs, 1)
    else:
        refs[0][0] = edges[0]
        refs[0][1] = edges[1]


def finish_edges(block, scalars, x, hidden, part, terms, w, point, reach, ahead, after=()):
    c, h = w.shape[1], w.shape[2] // 3
    rows = x.shape[0] // GROUP
    outs = (array(*x.shape),) + (array(ahead, h),) * 2 + (array(2, rows, h),)
    outs += (array(2, reach, h),) if block + 2 == w.shape[0] else (array(rows, h),)
    return call(
        functools.partial(edge_kernel, block, reach, ahead), outs,
        (scalars, x, hidden, part, *terms, w, point),
        [SMEM] + [VMEM] * 7, (VMEM,) * len(outs), [],
        2 * c * h * (2 * reach + 2 * ahead), 4 * 2**20, {1: 0}, after,
    )


def edge_hidden_kernel(reach, s_ref, hidden, part, from_even, from_odd, far_ref, ends_ref):
    below, above = arrived(s_ref, from_even, from_odd, 0, reach)
    edges = (
        gelu(part[pl.ds(0, reach)] + below).astype(BF16),
        gelu(part[pl.ds(reach, reach)] + above).astype(BF16),
    )
    ends_ref[0] = edges[0]
    ends_ref[1] = edges[1]
    give_back(s_ref[0], hidden, reach, edges, (far_ref.at[0], far_ref.at[1]), 2)


def edge_hidden(scalars, hidden, part, terms, reach):
    length, h = hidden.shape
    outs = (array(2, length // GROUP, h), array(2, reach, h))
    return call(
        functools.partial(edge_hidden_kernel, reach), outs, (scalars, hidden, part, *terms),
        [SMEM] + [VMEM] * 4, (VMEM,) * 2, [], 40 * reach * h, 2**20,
    )


def edge_terms_kernel(block, reach, s_ref, x, ends, w, point, x_ref, even_ref, odd_ref):
    length = x.shape[0]
    h = ends.shape[2]
    more = dot(ends[...].reshape(2 * reach, h), point[block])
    for i, at in enumerate((0, length - reach)):
        new = x[pl.ds(at, reach)].astype(F32) + more[i * reach : (i + 1) * reach]
        x_ref[pl.ds(at, reach)] = new.astype(BF16)
    up = dot(x_ref[pl.ds(length - reach, reach)], w[block + 1, :, :h])
    down = dot(x_ref[pl.ds(0, reach)], w[block + 1, :, 2 * h :])
    place_terms(s_ref[1], up, down, even_ref, odd_ref, 0, reach)


def edge_terms(block, scalars, x, ends, w, point, reach):
    c, h = w.shape[1], w.shape[2] // 3
    outs = (array(*x.shape), array(reach, h), array(reach, h))
    return call(
        functools.partial(edge_terms_kernel, block, reach), outs, (scalars, x, ends, w, point),
        [SMEM] + [VMEM] * 4, (VMEM,) * 3, [], 8 * c * h * reach, 2 * 2**20, {1: 0},
    )


def near_kernel(
    reach, s_ref, x, hidden, ends, from_even, from_odd, w, h_ref, near_ref, core_ref, other
):
    length = x.shape[0]
    half = length // 2
    h = near_ref.shape[1]
    block = w.shape[0] - 1
    terms = dot(x[pl.ds(0, half)], w[block, :, : 2 * h])
    other[...] = terms[:, :h].astype(BF16)
    near_ref[...] = terms[:, h:]
    terms = dot(x[pl.ds(half, half)], w[block, :, h:])
    high = terms[:, h:].astype(BF16).astype(F32)
    lower = near_ref[...] + high
    upper = terms[:, :h] + other[...].astype(F32)
    below, above = arrived(s_ref, from_even, from_odd, 0, reach)
    h_ref[0] = gelu(lower[:reach] + below).astype(BF16)
    h_ref[1] = gelu(upper[reach:] + above).astype(BF16)
    near_ref[pl.ds(0, reach)] = lower[reach:]
    near_ref[pl.ds(reach, reach)] = upper[:reach]
    give_back(s_ref[0], hidden, reach, (ends[0], ends[1]), (core_ref,), 1)


def near_terms(scalars, x, hidden, ends, terms, w, reach, after):
    c, h = w.shape[1], w.shape[2] // 3
    rows = x.shape[0] // GROUP
    half = x.shape[0] // 2
    scratch = [pltpu.VMEM((half, h), BF16)]
    outs = (array(2, reach, h), array(half, h, dtype=F32), array(rows, h))
    return call(
        functools.partial(near_kernel, reach), outs, (scalars, x, hidden, ends, *terms, w),
        [SMEM] + [VMEM] * 6, (VMEM,) * 3, scratch, NEAR_WORK, 4 * 2**20, after=after,
    )


def forward_kernel(count, *refs):
    out = refs[-1]
    for i, ref in enumerate(refs[:-1]):
        out[i] = ref[...] if i < count else ref[1]


def forward(own, passing):
    out = array(len(own) + len(passing), *own[0].shape)
    operands = (*own, *passing)
    return call(
        functools.partial(forward_kernel, len(own)), out, operands, [VMEM] * len(operands), VMEM, [],
        0, 4 * out.size,
    )


def last_kernel(s_ref, outer, near, from_even, from_odd, g0, g1, g2, g3, hidden):
    q = s_ref[0]
    reach, h = outer.shape[1:]
    below, above = arrived(s_ref, from_even, from_odd, 0, reach)
    hidden[0] = outer[0]
    hidden[1] = gelu(near[pl.ds(0, reach)] + below).astype(BF16)
    hidden[2] = gelu(near[pl.ds(reach, reach)] + above).astype(BF16)
    hidden[3] = outer[1]
    for k, piece in enumerate((g0, g1, g2, g3)):
        piece[...] = hidden[q ^ k]


def last_hidden(scalars, outer, near, terms, after):
    half, h = near.shape
    return call(
        last_kernel, (array(half // 2, h),) * GROUP, (scalars, outer, near, *terms),
        [SMEM] + [VMEM] * 4, (VMEM,) * GROUP, [pltpu.VMEM((GROUP, half // 2, h), BF16)],
        20 * half * h, 2 * 2**20, after=after,
    )


def add_blocks(x, hiddens, point, keep):
    for b, hidden in enumerate(hiddens):
        x = (x.astype(F32) + dot(hidden, point[b])).astype(BF16)
        keep(b, x)
    return x


def chip_out_kernel(count, s_ref, x, *refs):
    own, far, refs = refs[:count], refs[count : 2 * count], refs[2 * count :]
    mine, point, out, kept, ys, osems = refs
    q = s_ref[0]
    places, r, c = x.shape[1:]
    rows = places * r
    here = pl.ds(pl.multiple_of(q * places, places), places)
    writes = start_all(
        [
            pltpu.make_async_copy(own[b].at[here], out.at[b, :, q], osems.at[0, b])
            for b in range(count)
        ]
    )

    def write(k, b, value):
        ys[b] = value.reshape(places, r, c)
        writes.append(pltpu.make_async_copy(ys.at[b], out.at[b, :, q ^ k], osems.at[k // 2, b]))
        writes[-1].start()

    now = own[count - 1][here].reshape(rows, c).astype(F32) + dot(mine[...], point[count])
    write(0, count, now.astype(BF16))
    hiddens = [far[b][0] for b in range(count)]
    now = add_blocks(x[1].reshape(rows, c), hiddens, point, functools.partial(write, 2))
    kept[...] = now
    wait_all(writes)


def chip_outputs(scalars, x, own, far, mine, point):
    places, r, c = x.shape[1:]
    group, blocks = GROUP, point.shape[0]
    own = [v.reshape(group * places, r, c) for v in own]
    operands = (scalars, x, *own, *far, mine, point)
    scratch = [
        pltpu.VMEM((blocks, places, r, c), BF16),
        pltpu.SemaphoreType.DMA((2, blocks)),
    ]
    return call(
        functools.partial(chip_out_kernel, blocks - 1),
        (array(blocks, places, group, r, c), array(places * r, c)),
        operands, [SMEM] + [VMEM] * (len(operands) - 1), (HBM, VMEM), scratch, CHIP_WORK, 8 * 2**20,
    )


def core_out_kernel(count, s_ref, x, core, point, _, out, kept, ys, osems):
    q = s_ref[0]
    places, r, c = x.shape[1:]
    rows = places * r
    writes = []

    def write(i, k, b, value):
        ys[i, b] = value.reshape(places, r, c)
        writes.append(pltpu.make_async_copy(ys.at[i, b], out.at[b, :, q ^ k], osems.at[i, b]))
        writes[-1].start()

    for i, k in enumerate((1, 3)):
        hiddens = [core[(count + 1) * i + b] for b in range(count + 1 - i)]
        now = add_blocks(x[2 * i].reshape(rows, c), hiddens, point, functools.partial(write, i, k))
    kept[...] = now
    wait_all(writes)


def core_outputs(scalars, x, core, point, before):
    blocks, places, group, r, c = before.shape
    h = point.shape[1]
    operands = (scalars, x, core, point, before)
    scratch = [
        pltpu.VMEM((2, blocks, places, r, c), BF16),
        pltpu.SemaphoreType.DMA((2, blocks)),
    ]
    return call(
        functools.partial(core_out_kernel, blocks - 1),
        (array(*before.shape), array(places * r, c)),
        operands, [SMEM] + [VMEM] * 3 + [HBM], (HBM, VMEM), scratch,
        blocks * x.size * h, 4 * 2**20, {4: 0},
    )


def late_out_kernel(s_ref, x2, x3, point, _, a2, a3, out, ys, sems):
    places, r, c = ys.shape[1:]
    last = out.shape[0] - 1
    writes = []
    for i, (x, hidden) in enumerate(((x2, a2), (x3, a3))):
        value = x[...].astype(F32) + dot(hidden[...], point[last])
        ys[i] = value.astype(BF16).reshape(places, r, c)
        writes.append(pltpu.make_async_copy(ys.at[i], out.at[last, :, s_ref[0] ^ (2 + i)], sems.at[i]))
        writes[-1].start()
    wait_all(writes)


def late_outputs(scalars, hiddens, xs, point, before):
    blocks, places, group, r, c = before.shape
    operands = (scalars, *xs, point, before, *hiddens)
    scratch = [pltpu.VMEM((2, places, r, c), BF16), pltpu.SemaphoreType.DMA((2,))]
    return call(
        late_out_kernel, array(*before.shape), operands,
        [SMEM] + [VMEM] * 3 + [HBM] + [VMEM] * 2, HBM, scratch,
        4 * places * r * c * point.shape[1], 2 * 2**20, {4: 0},
    )


def neighbour_pairs(size, parity):
    groups = size // GROUP
    pairs = []
    for i in range(size):
        group = i // GROUP
        other = group + 1 if group % 2 == parity else group - 1
        pairs.append((i, i + (other - group) * GROUP if 0 <= other < groups else i ^ 1))
    return pairs


def by_residue(signal, taps, point):
    size = lax.axis_size("seq")
    me = lax.axis_index("seq")
    length, c = signal.shape
    places = length // FIRST_DILATION
    r = FIRST_DILATION // GROUP
    q, group = me % GROUP, me // GROUP
    scalars = jnp.stack(
        [q, group % 2, (group > 0).astype(jnp.int32), (group < size // GROUP - 1).astype(jnp.int32)]
    ).astype(jnp.int32)
    even_pairs, odd_pairs = neighbour_pairs(size, 0), neighbour_pairs(size, 1)
    x = signal.reshape(places, GROUP, r, c)

    def swap(value, k):
        return lax.ppermute(value, "seq", [(i, i ^ k) for i in range(size)])

    def across(even, odd):
        return lax.ppermute(even, "seq", even_pairs), lax.ppermute(odd, "seq", odd_pairs)

    mine, beside, over, last, rest = split(scalars, x)
    over, rest, last, beside = swap(over, 2), swap(rest, 3), swap(last, 2), swap(beside, 1)
    w = side_by_side(taps)
    *early, xs = early_taps(scalars, mine, beside, w, point, x)
    early, ready = early[:4], early[4:]
    edge = swap(edge_part(over, r, early[:1]), 1)
    pieces = (mine, beside, over, edge)
    terms = across(*open_terms(scalars, pieces, w, r))
    early = more_taps(scalars, over, edge, w, early)
    current, even, odd, over, beside = first_block(scalars, (rest, last), (*early, *ready), terms, w, point, r)
    terms = across(even, odd)
    own, core, far = [current], [beside], [swap(over, 2)]
    reach = 2 * r
    current, hidden, part = middle_block(1, scalars, current, w, point, reach)
    current, even, odd, over, beside = finish_edges(
        1, scalars, current, hidden, part, terms, w, point, reach, 2 * reach
    )
    terms = across(even, odd)
    own.append(current)
    core.append(beside)
    far.append(swap(over, 2))
    reach = 4 * r
    current, hidden, part, *inner = middle_block(2, scalars, current, w, point, reach, far[:1])
    inner = across(*inner)
    over, ends = edge_hidden(scalars, hidden, part, terms, reach)
    current, even, odd = edge_terms(2, scalars, current, ends, w, point, reach)
    terms = across(even, odd)
    own.append(current)
    far.append(swap(over, 2))
    outer, near, beside = near_terms(
        scalars, current, hidden, ends, inner, w, reach, far[1:2]
    )
    core.append(beside)
    hidden = last_hidden(scalars, outer, near, terms, ())
    lasts = [swap(hidden[k], k) for k in (2, 3)]
    beside = swap(forward([*core, hidden[1]], far), 1)
    out, x2 = chip_outputs(scalars, xs, own, far, hidden[0], point)
    out, x3 = core_outputs(scalars, xs, beside, point, out)
    out = late_outputs(scalars, lasts, (x2, x3), point, out)
    return out.reshape(point.shape[0], length, c)


def passed_along(value, by):
    size = lax.axis_size("seq")
    pairs = [(i, i + by) for i in range(size) if 0 <= i + by < size]
    return lax.ppermute(value, "seq", pairs)


def by_neighbours(signal, taps, point):
    length = signal.shape[0]
    current = signal
    outputs = []
    for block in range(taps.shape[0]):
        step = FIRST_DILATION * 2**block
        low = dot(current, taps[block, 0]).astype(BF16)
        high = dot(current, taps[block, 2]).astype(BF16)
        if step < length:
            below = jnp.concatenate([passed_along(low[length - step :], 1), low[: length - step]])
            above = jnp.concatenate([high[step:], passed_along(high[:step], -1)])
        else:
            below = passed_along(low, step // length)
            above = passed_along(high, -(step // length))
        v = dot(current, taps[block, 1]) + below.astype(F32) + above.astype(F32)
        hidden = jax.nn.gelu(v, approximate=True).astype(BF16)
        current = (current.astype(F32) + dot(hidden, point[block])).astype(BF16)
        outputs.append(current)
    return jnp.stack(outputs)


def shards(signal, taps, point):
    fits = (
        taps.shape[0] == 4
        and signal.shape[0] == GROUP * FIRST_DILATION
        and lax.axis_size("seq") % GROUP == 0
    )
    return (by_residue if fits else by_neighbours)(signal, taps, point)


def solution(mesh):
    in_specs = (P(("grp", "seq"), None), P(), P())
    out_specs = P(None, ("grp", "seq"), None)
    return jax.shard_map(shards, mesh=mesh, in_specs=in_specs, out_specs=out_specs, check_vma=False)
```

```python
import functools

import jax
import jax.numpy as jnp
from jax import lax
from jax.experimental import pallas as pl
from jax.experimental.pallas import tpu as pltpu
from jax.sharding import PartitionSpec as P

FIRST_DILATION = 256
GROUP = 4
ROWS = 512
VMEM_LIMIT = 24 * 2**20
NEAR_WORK, CHIP_WORK = 2.4e9, 5e10

F32, BF16 = jnp.float32, jnp.bfloat16
ANY = pl.BlockSpec(memory_space=pl.ANY)
VMEM = pl.BlockSpec(memory_space=pltpu.VMEM)
SMEM = pl.BlockSpec(memory_space=pltpu.SMEM)
HBM = pl.BlockSpec(memory_space=pltpu.HBM)


def dot(a, b):
    return jnp.dot(a, b, preferred_element_type=F32)


def gelu(v):
    half = 0.5 * v
    inner = v * (0.7978845608028654 + 0.035677408136300125 * (v * v))
    return half + half * jnp.tanh(inner)


def over_rows(rows, body):
    for start in range(0, rows, ROWS):
        body(start, min(ROWS, rows - start))


def start_all(copies):
    for copy in copies:
        copy.start()
    return copies


def wait_all(copies):
    for copy in copies:
        copy.wait()


def call(kernel, outs, operands, specs, out_specs, scratch, flops, moved, aliases=None, after=()):
    count = len(operands)
    operands, specs = [*operands, *after], [*specs, *[ANY] * len(after)]
    body = kernel
    if after:
        kernel = lambda *refs: body(*refs[:count], *refs[count + len(after) :])
    return pl.pallas_call(
        kernel,
        out_shape=outs,
        in_specs=specs,
        out_specs=out_specs,
        scratch_shapes=scratch,
        input_output_aliases=aliases or {},
        compiler_params=pltpu.CompilerParams(vmem_limit_bytes=VMEM_LIMIT),
        cost_estimate=pl.CostEstimate(
            flops=int(flops), bytes_accessed=int(moved), transcendentals=0
        ),
    )(*operands)


def array(*shape, dtype=BF16):
    return jax.ShapeDtypeStruct(shape, dtype)


def split_kernel(s_ref, x, own, beside, over, last, rest, sems):
    q = s_ref[0]
    count = x.shape[0] - 1
    is_top = q == GROUP - 1

    def some(bottom, top, size):
        return pl.ds(jnp.where(is_top, top, bottom), size)

    copies = [
        pltpu.make_async_copy(source, target, sems.at[i])
        for i, (source, target) in enumerate(
            (
                (x.at[some(0, 1, count), q ^ 2], over.at[pl.ds(0, count)]),
                (x.at[some(0, count, 1), q ^ 3], over.at[pl.ds(count, 1)]),
                (x.at[some(1, 0, count), q ^ 3], rest),
                (x.at[some(count, 0, 1), q ^ 2], last),
                (x.at[:, q ^ 1], beside),
                (x.at[:, q], own),
            )
        )
    ]
    wait_all(start_all(copies))


def split(scalars, x):
    places, group, r, c = x.shape
    x = pltpu.with_memory_space_constraint(x, pltpu.HBM)
    outs = [array(n, r, c) for n in (places, places, places, 1, places - 1)]
    sems = [pltpu.SemaphoreType.DMA((6,))]
    pieces = call(split_kernel, outs, (scalars, x), [SMEM, HBM], (VMEM,) * 5, sems, 0, 4 * x.size)
    return [piece.reshape(piece.shape[0] * r, c) for piece in pieces]


def edge_part_kernel(over, out):
    out[...] = over[pl.ds(over.shape[0] - out.shape[0], out.shape[0])]


def edge_part(over, r, after):
    out = array(r, over.shape[1])
    return call(edge_part_kernel, out, (over,), [VMEM], VMEM, [], 0, 2 * out.size, after=after)


def side_by_side_kernel(taps, w, sems):
    h = taps.shape[3]
    wait_all(
        start_all(
            [
                pltpu.make_async_copy(
                    taps.at[b, t], w.at[b, :, pl.ds(t * h, h)], sems.at[b, t]
                )
                for b in range(taps.shape[0])
                for t in range(3)
            ]
        )
    )


def side_by_side(taps):
    blocks, count, c, h = taps.shape
    sems = [pltpu.SemaphoreType.DMA((blocks, count))]
    taps = pltpu.with_memory_space_constraint(taps, pltpu.HBM)
    return call(side_by_side_kernel, array(blocks, c, count * h), (taps,), [HBM], VMEM, sems, 0, 4 * taps.size)


def place_terms(parity, up, down, even_ref, odd_ref, start, size):
    even_ref[pl.ds(start, size)] = jnp.where(parity == 0, up, down).astype(BF16)
    odd_ref[pl.ds(start, size)] = jnp.where(parity == 0, down, up).astype(BF16)


def arrived(s_ref, from_even, from_odd, start, size):
    even = from_even[pl.ds(start, size)].astype(F32)
    odd = from_odd[pl.ds(start, size)].astype(F32)
    parity, has_lower, has_upper = s_ref[1], s_ref[2], s_ref[3]
    below = jnp.where(has_lower == 0, 0.0, jnp.where(parity == 0, odd, even))
    above = jnp.where(has_upper == 0, 0.0, jnp.where(parity == 0, even, odd))
    return below, above


def open_kernel(r, s_ref, own, beside, over, edge, w, even_ref, odd_ref, ends):
    q, parity = s_ref[0], s_ref[1]
    h = even_ref.shape[1]
    last = own.shape[0] - r

    def fetch(piece, at, to):
        ends[pl.ds(to, r)] = piece[pl.ds(at, r)]

    for k, (piece, top) in enumerate(((own, last), (beside, last), (over, last - r), (edge, 0))):
        pl.when(q ^ k == GROUP - 1)(functools.partial(fetch, piece, top, 0))
        pl.when(q ^ k == 0)(functools.partial(fetch, piece, 0, r))
    up = dot(ends[pl.ds(0, r)], w[0, :, :h])
    down = dot(ends[pl.ds(r, r)], w[0, :, 2 * h :])
    place_terms(parity, up, down, even_ref, odd_ref, 0, r)


def open_terms(scalars, pieces, w, r):
    c, h = w.shape[1], w.shape[2] // 3
    terms = array(r, h)
    return call(
        functools.partial(open_kernel, r), (terms, terms), (scalars, *pieces, w),
        [SMEM] + [VMEM] * (GROUP + 1), (VMEM, VMEM), [pltpu.VMEM((2 * r, c), BF16)],
        4 * r * c * h, 2**20,
    )


def keep_terms(at, terms, low, mid, high, low_at=None):
    h = mid.shape[1]
    low[at if low_at is None else low_at] = terms[:, :h].astype(BF16)
    mid[at] = terms[:, h : 2 * h]
    high[at] = terms[:, 2 * h :].astype(BF16)


def piece_taps(starts, r, pieces, w, x, low, mid, high):
    terms = dot(jnp.concatenate(pieces), w[0])
    done = 0
    for start, piece in zip(starts, pieces):
        size = piece.shape[0]
        at, low_at = pl.ds(start, size), pl.ds(pl.multiple_of(start + r, r), size)
        x[at] = piece
        keep_terms(at, terms[done : done + size], low, mid, high, low_at)
        done += size


def first_finish(starts, sizes, r, point, x, low, mid, high, x_ref, hidden):
    values = []
    for start, size in zip(starts, sizes):
        at, after = pl.ds(start, size), pl.ds(pl.multiple_of(start + r, r), size)
        v = mid[at] + low[at].astype(F32) + high[after].astype(F32)
        values.append(gelu(v).astype(BF16))
        hidden[at] = values[-1]
    more = dot(jnp.concatenate(values), point[0])
    done = 0
    for start, size in zip(starts, sizes):
        at = pl.ds(start, size)
        x_ref[at] = (x[at].astype(F32) + more[done : done + size]).astype(BF16)
        done += size


def part_start(j, rows, bottom, top, r):
    return pl.multiple_of(j * rows + jnp.where(j == GROUP - 1, top, bottom), r)


def block_body(reach, x, point, x_ref, h_ref, part_ref, low, mid, high):
    length = x.shape[0]
    top = length - reach

    def body(start, size):
        at = reach + start
        v = mid[pl.ds(at, size)] + low[pl.ds(start, size)].astype(F32)
        hidden = gelu(v + high[pl.ds(at + reach, size)].astype(F32)).astype(BF16)
        h_ref[pl.ds(at, size)] = hidden
        x_ref[pl.ds(at, size)] = (x[pl.ds(at, size)].astype(F32) + dot(hidden, point)).astype(BF16)

    over_rows(length - 2 * reach, body)
    part_ref[pl.ds(0, reach)] = mid[pl.ds(0, reach)] + high[pl.ds(reach, reach)].astype(F32)
    part_ref[pl.ds(reach, reach)] = mid[pl.ds(top, reach)] + low[pl.ds(top - reach, reach)].astype(F32)
    for at in (0, top):
        x_ref[pl.ds(at, reach)] = x[pl.ds(at, reach)]
        h_ref[pl.ds(at, reach)] = jnp.zeros((reach, h_ref.shape[1]), BF16)


def early_taps_kernel(
    r, s_ref, own, beside, w, point, signal, x, low, mid, high, x_ref, hidden, xs_ref, sems
):
    q = s_ref[0]
    reads = start_all(
        [
            pltpu.make_async_copy(signal.at[:, q ^ k], xs_ref.at[k - 1], sems.at[k])
            for k in range(1, GROUP)
        ]
    )
    rows = own.shape[0]
    starts = [pl.multiple_of((q ^ k) * rows, rows) for k in range(2)]
    piece_taps(starts, r, (own[...], beside[...]), w, x, low, mid, high)
    half = jnp.where(q < GROUP // 2, 0, GROUP // 2) * rows
    start = pl.multiple_of(half + r, r)
    first_finish((start,), (2 * rows - 2 * r,), r, point, x, low, mid, high, x_ref, hidden)
    wait_all(reads)


def early_taps(scalars, own, beside, w, point, signal):
    c, h = w.shape[1], w.shape[2] // 3
    rows = own.shape[0]
    length = GROUP * rows
    places, _, r, _ = signal.shape
    signal = pltpu.with_memory_space_constraint(signal, pltpu.HBM)
    outs = (array(length, c), array(length + r, h), array(length, h, dtype=F32))
    outs += (array(length + r, h), array(length, c), array(length, h))
    outs += (array(GROUP - 1, places, r, c),)
    return call(
        functools.partial(early_taps_kernel, r), outs, (scalars, own, beside, w, point, signal),
        [SMEM] + [VMEM] * 4 + [HBM], (VMEM,) * 7, [pltpu.SemaphoreType.DMA((GROUP,))],
        12 * rows * c * h, 2**20,
    )


def more_taps_kernel(s_ref, over, edge, w, *refs):
    x, low, mid, high = refs[4:]
    q = s_ref[0]
    rows, r = x.shape[0] // GROUP, edge.shape[0]
    size = rows - r
    starts = (part_start(q ^ 2, rows, 0, r, r), part_start(q ^ 3, rows, 0, size, r))
    piece_taps(starts, r, (over[pl.ds(0, size)], edge[...]), w, x, low, mid, high)


def more_taps(scalars, over, edge, w, early):
    c, h = w.shape[1], w.shape[2] // 3
    return call(
        more_taps_kernel, tuple(array(*e.shape, dtype=e.dtype) for e in early),
        (scalars, over, edge, w, *early), [SMEM] + [VMEM] * 7, (VMEM,) * 4, [],
        6 * over.shape[0] * c * h, 2**20, {4: 0, 5: 1, 6: 2, 7: 3},
    )


def first_kernel(
    r, s_ref, rest, last, x, low, mid, high, x_in, hidden_in, from_even, from_odd, w, point,
    even_ref, odd_ref, far_ref, core_ref, *refs
):
    x_ref, hidden = refs[-2:]
    q, parity = s_ref[0], s_ref[1]
    length = x.shape[0]
    rows = length // GROUP
    h = mid.shape[1]
    size = rows - r
    starts = (part_start(q ^ 3, rows, r, 0, r), part_start(q ^ 2, rows, size, 0, r))
    piece_taps(starts, r, (rest[...], last[...]), w, x, low, mid, high)
    below, above = arrived(s_ref, from_even, from_odd, 0, r)
    low[pl.ds(0, r)] = below.astype(BF16)
    high[pl.ds(length, r)] = above.astype(BF16)
    is_low = q < GROUP // 2
    alone = pl.multiple_of(jnp.where(is_low, 0, length - r), r)
    others = pl.multiple_of(jnp.where(is_low, 2 * rows - r, 0), r)
    first_finish((alone, others), (r, 2 * rows + r), r, point, x, low, mid, high, x_ref, hidden)
    ahead = even_ref.shape[0]
    up = dot(x_ref[pl.ds(length - ahead, ahead)], w[1, :, :h])
    down = dot(x_ref[pl.ds(0, ahead)], w[1, :, 2 * h :])
    place_terms(parity, up, down, even_ref, odd_ref, 0, ahead)
    for k, ref in ((1, core_ref), (2, far_ref.at[0]), (3, far_ref.at[1])):
        ref[...] = hidden[pl.ds(pl.multiple_of((q ^ k) * rows, rows), rows)]


def first_block(scalars, rests, early, terms, w, point, r):
    c, h = w.shape[1], w.shape[2] // 3
    length = early[0].shape[0]
    rows = length // GROUP
    outs = (array(2 * r, h), array(2 * r, h), array(2, rows, h), array(rows, h))
    outs += tuple(array(*e.shape, dtype=e.dtype) for e in early)
    results = call(
        functools.partial(first_kernel, r), outs, (scalars, *rests, *early, *terms, w, point),
        [SMEM] + [VMEM] * 12, (VMEM,) * 10, [],
        8 * length * c * h, 4 * 2**20, {3 + i: 4 + i for i in range(6)},
    )
    return results[8], *results[:4]


def middle_kernel(block, reach, parity_ref, x, w, point, x_ref, h_ref, part_ref, *refs):
    sent, (low, mid, high) = refs[:-3], refs[-3:]
    h = mid.shape[1]

    length = x.shape[0]
    bottom, top = pl.ds(0, reach), pl.ds(length - reach, reach)
    terms = dot(x[bottom], w[block, :, : 2 * h])
    low[bottom] = terms[:, :h].astype(BF16)
    mid[bottom] = terms[:, h:]

    def body(start, size):
        at = pl.ds(reach + start, size)
        keep_terms(at, dot(x[at], w[block]), low, mid, high)

    over_rows(length - 2 * reach, body)
    terms = dot(x[top], w[block, :, h:])
    mid[top] = terms[:, :h]
    high[top] = terms[:, h:].astype(BF16)
    block_body(reach, x, point[block], x_ref, h_ref, part_ref, low, mid, high)
    if sent:
        middle = x.shape[0] // 2
        up = dot(x_ref[pl.ds(middle, reach)], w[block + 1, :, :h])
        down = dot(x_ref[pl.ds(middle - reach, reach)], w[block + 1, :, 2 * h :])
        place_terms(parity_ref[1], up, down, *sent, 0, reach)


def middle_block(block, scalars, x, w, point, reach, after=()):
    c, h = w.shape[1], w.shape[2] // 3
    length = x.shape[0]
    outs = (array(length, c), array(length, h), array(2 * reach, h, dtype=F32))
    if block + 2 == w.shape[0]:
        outs += (array(reach, h),) * 2
    scratch = [
        pltpu.VMEM((length, h), BF16),
        pltpu.VMEM((length, h), F32),
        pltpu.VMEM((length, h), BF16),
    ]
    return call(
        functools.partial(middle_kernel, block, reach), outs, (scalars, x, w, point),
        [SMEM] + [VMEM] * 3, (VMEM,) * len(outs), scratch, 8 * length * c * h, 4 * 2**20, after=after,
    )


def give_back(q, hidden, reach, edges, refs, first):
    rows = hidden.shape[0] // GROUP
    for i, ref in enumerate(refs):
        j = q ^ (first + i)
        ref[...] = hidden[pl.ds(pl.multiple_of(j * rows, rows), rows)]

        @pl.when(j == 0)
        def _(ref=ref):
            ref[pl.ds(0, reach)] = edges[0]

        @pl.when(j == GROUP - 1)
        def _(ref=ref):
            ref[pl.ds(rows - reach, reach)] = edges[1]


def edge_kernel(
    block, reach, ahead, s_ref, x, hidden, part, from_even, from_odd, w, point,
    x_ref, even_ref, odd_ref, far_ref, *refs
):
    q, parity = s_ref[0], s_ref[1]
    length = x.shape[0]
    h = hidden.shape[1]
    rows = length // GROUP
    below, above = arrived(s_ref, from_even, from_odd, 0, reach)
    edges = (
        gelu(part[pl.ds(0, reach)] + below).astype(BF16),
        gelu(part[pl.ds(reach, reach)] + above).astype(BF16),
    )
    more = dot(jnp.concatenate(edges), point[block])
    for i, at in enumerate((0, length - reach)):
        new = x[pl.ds(at, reach)].astype(F32) + more[i * reach : (i + 1) * reach]
        x_ref[pl.ds(at, reach)] = new.astype(BF16)
    up = dot(x_ref[pl.ds(length - ahead, ahead)], w[block + 1, :, :h])
    down = dot(x_ref[pl.ds(0, ahead)], w[block + 1, :, 2 * h :])
    place_terms(parity, up, down, even_ref, odd_ref, 0, ahead)
    give_back(q, hidden, reach, edges, (far_ref.at[0], far_ref.at[1]), 2)
    if block + 2 < w.shape[0]:
        give_back(q, hidden, reach, edges, refs, 1)
    else:
        refs[0][0] = edges[0]
        refs[0][1] = edges[1]


def finish_edges(block, scalars, x, hidden, part, terms, w, point, reach, ahead, after=()):
    c, h = w.shape[1], w.shape[2] // 3
    rows = x.shape[0] // GROUP
    outs = (array(*x.shape),) + (array(ahead, h),) * 2 + (array(2, rows, h),)
    outs += (array(2, reach, h),) if block + 2 == w.shape[0] else (array(rows, h),)
    return call(
        functools.partial(edge_kernel, block, reach, ahead), outs,
        (scalars, x, hidden, part, *terms, w, point),
        [SMEM] + [VMEM] * 7, (VMEM,) * len(outs), [],
        2 * c * h * (2 * reach + 2 * ahead), 4 * 2**20, {1: 0}, after,
    )


def edge_hidden_kernel(reach, s_ref, hidden, part, from_even, from_odd, far_ref, ends_ref):
    below, above = arrived(s_ref, from_even, from_odd, 0, reach)
    edges = (
        gelu(part[pl.ds(0, reach)] + below).astype(BF16),
        gelu(part[pl.ds(reach, reach)] + above).astype(BF16),
    )
    ends_ref[0] = edges[0]
    ends_ref[1] = edges[1]
    give_back(s_ref[0], hidden, reach, edges, (far_ref.at[0], far_ref.at[1]), 2)


def edge_hidden(scalars, hidden, part, terms, reach):
    length, h = hidden.shape
    outs = (array(2, length // GROUP, h), array(2, reach, h))
    return call(
        functools.partial(edge_hidden_kernel, reach), outs, (scalars, hidden, part, *terms),
        [SMEM] + [VMEM] * 4, (VMEM,) * 2, [], 40 * reach * h, 2**20,
    )


def edge_terms_kernel(block, reach, s_ref, x, ends, w, point, x_ref, even_ref, odd_ref):
    length = x.shape[0]
    h = ends.shape[2]
    more = dot(ends[...].reshape(2 * reach, h), point[block])
    for i, at in enumerate((0, length - reach)):
        new = x[pl.ds(at, reach)].astype(F32) + more[i * reach : (i + 1) * reach]
        x_ref[pl.ds(at, reach)] = new.astype(BF16)
    up = dot(x_ref[pl.ds(length - reach, reach)], w[block + 1, :, :h])
    down = dot(x_ref[pl.ds(0, reach)], w[block + 1, :, 2 * h :])
    place_terms(s_ref[1], up, down, even_ref, odd_ref, 0, reach)


def edge_terms(block, scalars, x, ends, w, point, reach):
    c, h = w.shape[1], w.shape[2] // 3
    outs = (array(*x.shape), array(reach, h), array(reach, h))
    return call(
        functools.partial(edge_terms_kernel, block, reach), outs, (scalars, x, ends, w, point),
        [SMEM] + [VMEM] * 4, (VMEM,) * 3, [], 8 * c * h * reach, 2 * 2**20, {1: 0},
    )


def near_kernel(
    reach, s_ref, x, hidden, ends, from_even, from_odd, w, h_ref, near_ref, core_ref, other
):
    length = x.shape[0]
    half = length // 2
    h = near_ref.shape[1]
    block = w.shape[0] - 1
    terms = dot(x[pl.ds(0, half)], w[block, :, : 2 * h])
    other[...] = terms[:, :h].astype(BF16)
    near_ref[...] = terms[:, h:]
    terms = dot(x[pl.ds(half, half)], w[block, :, h:])
    high = terms[:, h:].astype(BF16).astype(F32)
    lower = near_ref[...] + high
    upper = terms[:, :h] + other[...].astype(F32)
    below, above = arrived(s_ref, from_even, from_odd, 0, reach)
    h_ref[0] = gelu(lower[:reach] + below).astype(BF16)
    h_ref[1] = gelu(upper[reach:] + above).astype(BF16)
    near_ref[pl.ds(0, reach)] = lower[reach:]
    near_ref[pl.ds(reach, reach)] = upper[:reach]
    give_back(s_ref[0], hidden, reach, (ends[0], ends[1]), (core_ref,), 1)


def near_terms(scalars, x, hidden, ends, terms, w, reach, after):
    c, h = w.shape[1], w.shape[2] // 3
    rows = x.shape[0] // GROUP
    half = x.shape[0] // 2
    scratch = [pltpu.VMEM((half, h), BF16)]
    outs = (array(2, reach, h), array(half, h, dtype=F32), array(rows, h))
    return call(
        functools.partial(near_kernel, reach), outs, (scalars, x, hidden, ends, *terms, w),
        [SMEM] + [VMEM] * 6, (VMEM,) * 3, scratch, NEAR_WORK, 4 * 2**20, after=after,
    )


def forward_kernel(count, *refs):
    out = refs[-1]
    for i, ref in enumerate(refs[:-1]):
        out[i] = ref[...] if i < count else ref[1]


def forward(own, passing):
    out = array(len(own) + len(passing), *own[0].shape)
    operands = (*own, *passing)
    return call(
        functools.partial(forward_kernel, len(own)), out, operands, [VMEM] * len(operands), VMEM, [],
        0, 4 * out.size,
    )


def last_kernel(s_ref, outer, near, from_even, from_odd, g0, g1, g2, g3, hidden):
    q = s_ref[0]
    reach, h = outer.shape[1:]
    below, above = arrived(s_ref, from_even, from_odd, 0, reach)
    hidden[0] = outer[0]
    hidden[1] = gelu(near[pl.ds(0, reach)] + below).astype(BF16)
    hidden[2] = gelu(near[pl.ds(reach, reach)] + above).astype(BF16)
    hidden[3] = outer[1]
    for k, piece in enumerate((g0, g1, g2, g3)):
        piece[...] = hidden[q ^ k]


def last_hidden(scalars, outer, near, terms, after):
    half, h = near.shape
    return call(
        last_kernel, (array(half // 2, h),) * GROUP, (scalars, outer, near, *terms),
        [SMEM] + [VMEM] * 4, (VMEM,) * GROUP, [pltpu.VMEM((GROUP, half // 2, h), BF16)],
        20 * half * h, 2 * 2**20, after=after,
    )


def add_blocks(x, hiddens, point, keep):
    for b, hidden in enumerate(hiddens):
        x = (x.astype(F32) + dot(hidden, point[b])).astype(BF16)
        keep(b, x)
    return x


def chip_out_kernel(count, s_ref, x, *refs):
    own, far, refs = refs[:count], refs[count : 2 * count], refs[2 * count :]
    mine, point, out, kept, ys, osems = refs
    q = s_ref[0]
    places, r, c = x.shape[1:]
    rows = places * r
    here = pl.ds(pl.multiple_of(q * places, places), places)
    writes = start_all(
        [
            pltpu.make_async_copy(own[b].at[here], out.at[b, :, q], osems.at[0, b])
            for b in range(count)
        ]
    )

    def write(k, b, value):
        ys[b] = value.reshape(places, r, c)
        writes.append(pltpu.make_async_copy(ys.at[b], out.at[b, :, q ^ k], osems.at[k // 2, b]))
        writes[-1].start()

    now = own[count - 1][here].reshape(rows, c).astype(F32) + dot(mine[...], point[count])
    write(0, count, now.astype(BF16))
    hiddens = [far[b][0] for b in range(count)]
    now = add_blocks(x[1].reshape(rows, c), hiddens, point, functools.partial(write, 2))
    kept[...] = now
    wait_all(writes)


def chip_outputs(scalars, x, own, far, mine, point):
    places, r, c = x.shape[1:]
    group, blocks = GROUP, point.shape[0]
    own = [v.reshape(group * places, r, c) for v in own]
    operands = (scalars, x, *own, *far, mine, point)
    scratch = [
        pltpu.VMEM((blocks, places, r, c), BF16),
        pltpu.SemaphoreType.DMA((2, blocks)),
    ]
    return call(
        functools.partial(chip_out_kernel, blocks - 1),
        (array(blocks, places, group, r, c), array(places * r, c)),
        operands, [SMEM] + [VMEM] * (len(operands) - 1), (HBM, VMEM), scratch, CHIP_WORK, 8 * 2**20,
    )


def core_out_kernel(count, s_ref, x, core, point, _, out, kept, ys, osems):
    q = s_ref[0]
    places, r, c = x.shape[1:]
    rows = places * r
    writes = []

    def write(i, k, b, value):
        ys[i, b] = value.reshape(places, r, c)
        writes.append(pltpu.make_async_copy(ys.at[i, b], out.at[b, :, q ^ k], osems.at[i, b]))
        writes[-1].start()

    for i, k in enumerate((1, 3)):
        hiddens = [core[(count + 1) * i + b] for b in range(count + 1 - i)]
        now = add_blocks(x[2 * i].reshape(rows, c), hiddens, point, functools.partial(write, i, k))
    kept[...] = now
    wait_all(writes)


def core_outputs(scalars, x, core, point, before):
    blocks, places, group, r, c = before.shape
    h = point.shape[1]
    operands = (scalars, x, core, point, before)
    scratch = [
        pltpu.VMEM((2, blocks, places, r, c), BF16),
        pltpu.SemaphoreType.DMA((2, blocks)),
    ]
    return call(
        functools.partial(core_out_kernel, blocks - 1),
        (array(*before.shape), array(places * r, c)),
        operands, [SMEM] + [VMEM] * 3 + [HBM], (HBM, VMEM), scratch,
        blocks * x.size * h, 4 * 2**20, {4: 0},
    )


def late_out_kernel(s_ref, x2, x3, point, _, a2, a3, out, ys, sems):
    places, r, c = ys.shape[1:]
    last = out.shape[0] - 1
    writes = []
    more = dot(jnp.concatenate([a2[...], a3[...]]), point[last])
    for i, x in enumerate((x2, x3)):
        for p in range(places):
            rows = pl.ds(p * r, r)
            at = (i * places + p) * r
            ys[i, p] = (x[rows].astype(F32) + more[at : at + r]).astype(BF16)
            to = out.at[last, p, s_ref[0] ^ (2 + i)]
            writes.append(pltpu.make_async_copy(ys.at[i, p], to, sems.at[i, p]))
            writes[-1].start()
    wait_all(writes)


def late_outputs(scalars, hiddens, xs, point, before):
    blocks, places, group, r, c = before.shape
    operands = (scalars, *xs, point, before, *hiddens)
    scratch = [pltpu.VMEM((2, places, r, c), BF16), pltpu.SemaphoreType.DMA((2, places))]
    return call(
        late_out_kernel, array(*before.shape), operands,
        [SMEM] + [VMEM] * 3 + [HBM] + [VMEM] * 2, HBM, scratch,
        4 * places * r * c * point.shape[1], 2 * 2**20, {4: 0},
    )


def neighbour_pairs(size, parity):
    groups = size // GROUP
    pairs = []
    for i in range(size):
        group = i // GROUP
        other = group + 1 if group % 2 == parity else group - 1
        pairs.append((i, i + (other - group) * GROUP if 0 <= other < groups else i ^ 1))
    return pairs


def by_residue(signal, taps, point):
    size = lax.axis_size("seq")
    me = lax.axis_index("seq")
    length, c = signal.shape
    places = length // FIRST_DILATION
    r = FIRST_DILATION // GROUP
    q, group = me % GROUP, me // GROUP
    scalars = jnp.stack(
        [q, group % 2, (group > 0).astype(jnp.int32), (group < size // GROUP - 1).astype(jnp.int32)]
    ).astype(jnp.int32)
    even_pairs, odd_pairs = neighbour_pairs(size, 0), neighbour_pairs(size, 1)
    x = signal.reshape(places, GROUP, r, c)

    def swap(value, k):
        return lax.ppermute(value, "seq", [(i, i ^ k) for i in range(size)])

    def across(even, odd):
        return lax.ppermute(even, "seq", even_pairs), lax.ppermute(odd, "seq", odd_pairs)

    mine, beside, over, last, rest = split(scalars, x)
    over, rest, last, beside = swap(over, 2), swap(rest, 3), swap(last, 2), swap(beside, 1)
    w = side_by_side(taps)
    *early, xs = early_taps(scalars, mine, beside, w, point, x)
    early, ready = early[:4], early[4:]
    edge = swap(edge_part(over, r, early[:1]), 1)
    pieces = (mine, beside, over, edge)
    terms = across(*open_terms(scalars, pieces, w, r))
    early = more_taps(scalars, over, edge, w, early)
    current, even, odd, over, beside = first_block(scalars, (rest, last), (*early, *ready), terms, w, point, r)
    terms = across(even, odd)
    own, core, far = [current], [beside], [swap(over, 2)]
    reach = 2 * r
    current, hidden, part = middle_block(1, scalars, current, w, point, reach)
    current, even, odd, over, beside = finish_edges(
        1, scalars, current, hidden, part, terms, w, point, reach, 2 * reach
    )
    terms = across(even, odd)
    own.append(current)
    core.append(beside)
    far.append(swap(over, 2))
    reach = 4 * r
    current, hidden, part, *inner = middle_block(2, scalars, current, w, point, reach, far[:1])
    inner = across(*inner)
    over, ends = edge_hidden(scalars, hidden, part, terms, reach)
    current, even, odd = edge_terms(2, scalars, current, ends, w, point, reach)
    terms = across(even, odd)
    own.append(current)
    far.append(swap(over, 2))
    outer, near, beside = near_terms(
        scalars, current, hidden, ends, inner, w, reach, far[1:2]
    )
    core.append(beside)
    hidden = last_hidden(scalars, outer, near, terms, ())
    lasts = [swap(hidden[k], k) for k in (2, 3)]
    beside = swap(forward([*core, hidden[1]], far), 1)
    out, x2 = chip_outputs(scalars, xs, own, far, hidden[0], point)
    out, x3 = core_outputs(scalars, xs, beside, point, out)
    out = late_outputs(scalars, lasts, (x2, x3), point, out)
    return out.reshape(point.shape[0], length, c)


def passed_along(value, by):
    size = lax.axis_size("seq")
    pairs = [(i, i + by) for i in range(size) if 0 <= i + by < size]
    return lax.ppermute(value, "seq", pairs)


def by_neighbours(signal, taps, point):
    length = signal.shape[0]
    current = signal
    outputs = []
    for block in range(taps.shape[0]):
        step = FIRST_DILATION * 2**block
        low = dot(current, taps[block, 0]).astype(BF16)
        high = dot(current, taps[block, 2]).astype(BF16)
        if step < length:
            below = jnp.concatenate([passed_along(low[length - step :], 1), low[: length - step]])
            above = jnp.concatenate([high[step:], passed_along(high[:step], -1)])
        else:
            below = passed_along(low, step // length)
            above = passed_along(high, -(step // length))
        v = dot(current, taps[block, 1]) + below.astype(F32) + above.astype(F32)
        hidden = jax.nn.gelu(v, approximate=True).astype(BF16)
        current = (current.astype(F32) + dot(hidden, point[block])).astype(BF16)
        outputs.append(current)
    return jnp.stack(outputs)


def shards(signal, taps, point):
    fits = (
        taps.shape[0] == 4
        and signal.shape[0] == GROUP * FIRST_DILATION
        and lax.axis_size("seq") % GROUP == 0
    )
    return (by_residue if fits else by_neighbours)(signal, taps, point)


def solution(mesh):
    in_specs = (P(("grp", "seq"), None), P(), P())
    out_specs = P(None, ("grp", "seq"), None)
    return jax.shard_map(shards, mesh=mesh, in_specs=in_specs, out_specs=out_specs, check_vma=False)
```
